32 devices in a mesh: fsdp: 4 (over y, x), seq: 8 (over z, core).
Axes of the slice: x: 2, y: 2, z: 4, core: 2. Of those that a mesh axis runs over, the one named last changes fastest.
Arguments:
- conv_input: bfloat16 [4, 1024, 3712], P('fsdp', 'seq'), may hold values from -6 to 6
- gate_input: bfloat16 [4, 1024, 3584], P('fsdp', 'seq'), may hold values from -6 to 6
- dt_raw: float32 [4, 1024, 56], P('fsdp', 'seq'), may hold values from -4 to 10
- grad_output: bfloat16 [4, 1024, 3584], P('fsdp', 'seq'), may hold values from -6 to 6
- conv_weight: float32 [4, 3712], P(None, 'fsdp'), may hold values from -3 to 3
- conv_bias: float32 [3712], P('fsdp'), may hold values from -0.5 to 0.5
- dt_bias: float32 [56], P('fsdp'), may hold values from -1 to 0.5
- a_log: float32 [56], P('fsdp'), may hold values from -14 to -2
- skip: float32 [56], P('fsdp'), may hold values from 0.5 to 2
- norm_gain: float32 [3584], P('fsdp'), may hold values from 0.5 to 1.5
Outputs:
- grad_conv_input: bfloat16 [4, 1024, 3712], P('fsdp', 'seq')
- grad_gate_input: bfloat16 [4, 1024, 3584], P('fsdp', 'seq')
- grad_dt_raw: float32 [4, 1024, 56], P('fsdp', 'seq')
- grad_conv_weight: float32 [4, 3712], P(None, 'fsdp')
- grad_conv_bias: float32 [3712], P('fsdp')
- grad_dt_bias: float32 [56], P('fsdp')
- grad_a_log: float32 [56], P('fsdp')
- grad_skip: float32 [56], P('fsdp')
- grad_norm_gain: float32 [3584], P('fsdp')
The draws below stay inside these ranges and needn't reach their ends.
All inputs are finite; a program needn't handle non-finite values.
Results may differ from the reference program's by a relative error of at most 0.012.
Values may be sent and summed in bfloat16 or wider, within the bound.
No kernel may reach another device: no remote copies, remote signals or barrier semaphores. Data moves between devices by JAX's collectives and lax.ppermute only.
A program may use at most 512 MiB of HBM per device.

```python
import jax
import jax.numpy as jnp
from jax import lax

H = 56
P_SIZE = 64
N = 64
KW = 4
TOK_DEV = 128
BATCH_ROWS = 4
TOKENS_PER_ROW = 1024
F = 3584
CH = 3712


def draw_dt_raw(key, part):
    key = jax.random.fold_in(key, 11)
    first_key, second_key, tertiary_seed = jax.random.split(key, 3)
    slab_count = TOKENS_PER_ROW // TOK_DEV
    lowest_position = 0.5 * jax.random.normal(first_key, (BATCH_ROWS, TOKENS_PER_ROW, H), jnp.float32)
    leading_shift = jax.random.uniform(second_key, (BATCH_ROWS, slab_count, 1, 1), jnp.float32, -0.8, 0.8)
    leading_shift = jnp.broadcast_to(leading_shift, (BATCH_ROWS, slab_count, TOK_DEV, H)).reshape(BATCH_ROWS, TOKENS_PER_ROW, H)
    slab_bundles = jax.random.bernoulli(tertiary_seed, 6.0 / TOKENS_PER_ROW, (BATCH_ROWS, TOKENS_PER_ROW, 1)).astype(jnp.float32) * 6.0
    return jnp.clip(lowest_position + leading_shift + slab_bundles, -4.0, 10.0)


def draw_a_log(key, part):
    key = jax.random.fold_in(key, 23)
    first_key, second_key, tertiary_seed = jax.random.split(key, 3)
    share = 0.5
    slow_pick = jax.random.uniform(first_key, (H,), jnp.float32) < share
    slow_rate = jnp.log(0.3 / TOKENS_PER_ROW) + jax.random.uniform(second_key, (H,), jnp.float32) * jnp.log(10.0)
    fast_rate = jnp.log(0.02) + jax.random.uniform(tertiary_seed, (H,), jnp.float32) * jnp.log(4.0)
    return jnp.where(slow_pick, slow_rate, fast_rate)


def block_scale(stream_key, extent, cuts, least, largest):
    factor_of, own = 1.0, jax.random.fold_in(stream_key, 6)
    for position, blocks in cuts:
        draws = jnp.exp(jax.random.uniform(jax.random.fold_in(own, position), (blocks,), jnp.float32, least / len(cuts), largest / len(cuts)))
        factor_of = factor_of * jnp.repeat(draws, extent[position] // blocks).reshape([-1 if axis == position else 1 for axis in range(len(extent))])
    return factor_of


def normal_values(rng, dims, deviation, bound, cuts=(), held_as=jnp.bfloat16):
    array = jax.random.normal(rng, dims, jnp.float32) * deviation
    if len(cuts) > 0:
        array = block_scale(rng, dims, cuts, -0.22, 0.18) * array
    return jnp.clip(array, min=-bound, max=bound).astype(held_as)


def setup_inputs(seed: int = 0) -> dict:
    arg_keys = jax.random.split(jax.random.key(seed), 11)
    return {
        "conv_input": normal_values(arg_keys[0], (BATCH_ROWS, TOKENS_PER_ROW, CH), 1.0, 6.0, ((0, 4), (1, 8))),
        "gate_input": normal_values(arg_keys[1], (BATCH_ROWS, TOKENS_PER_ROW, F), 1.0, 6.0, ((0, 4), (1, 8))),
        "dt_raw": draw_dt_raw(jax.random.fold_in(arg_keys[10], 71), 0),
        "grad_output": normal_values(arg_keys[3], (BATCH_ROWS, TOKENS_PER_ROW, F), 1.0, 6.0, ((0, 4), (1, 8))),
        "conv_weight": normal_values(arg_keys[4], (KW, CH), KW ** -0.5, 3.0, ((1, 4),), jnp.float32),
        "conv_bias": jnp.clip(jax.random.uniform(arg_keys[5], (CH,), jnp.float32, -0.5, 0.5) * block_scale(arg_keys[5], (CH,), ((0, 4),), -0.4, 0.0), -0.5, 0.5),
        "dt_bias": jnp.clip(-1.0 + 1.5 * jax.random.uniform(arg_keys[6], (H,), jnp.float32) ** block_scale(arg_keys[6], (H,), ((0, 4),), -0.2, 0.2), -1.0, 0.5),
        "a_log": draw_a_log(jax.random.fold_in(arg_keys[10], 71), 0),
        "skip": jnp.clip(0.5 + 1.5 * jax.random.uniform(arg_keys[8], (H,), jnp.float32) ** block_scale(arg_keys[8], (H,), ((0, 4),), -0.2, 0.2), 0.5, 2.0),
        "norm_gain": jnp.clip(1.0 + 0.1 * jax.random.normal(arg_keys[9], (F,), jnp.float32), 0.5, 1.5),
    }


EPS = 1e-05
HIGH = lax.Precision.HIGHEST

def convolve(padded, conv_weight, conv_bias):
    length = padded.shape[0] - conv_weight.shape[0] + 1
    summed = jnp.zeros((length, padded.shape[1]), jnp.float32) + conv_bias[None, :]
    for kernel_tap in range(conv_weight.shape[0]):
        summed = summed + conv_weight[kernel_tap][None, :] * padded[kernel_tap:kernel_tap + length]
    rounded = jax.nn.silu(summed).astype(jnp.bfloat16)
    return lax.optimization_barrier(rounded).astype(jnp.float32)

def slab_pieces(conv_out, raw_step, dt_bias, a_log):
    length = conv_out.shape[0]
    head_count = a_log.shape[0]
    inner_width = head_count * P_SIZE
    step_size = jax.nn.softplus(raw_step + dt_bias[None, :])
    running = jnp.cumsum(-jnp.exp(a_log)[None, :] * step_size, axis=0)
    values = conv_out[:, :inner_width].reshape(length, head_count, P_SIZE)
    input_projector = conv_out[:, inner_width:inner_width + N]
    read_vec = conv_out[:, inner_width + N:]
    scores = jnp.dot(read_vec, input_projector.T, precision=HIGH)
    by_head = running.T
    log_gap = by_head[:, :, None] - by_head[:, None, :]
    causal = lax.broadcasted_iota(jnp.int32, (length, length), 0) >= lax.broadcasted_iota(jnp.int32, (length, length), 1)
    decay = jnp.exp(jnp.where(causal[None], log_gap, -jnp.inf))
    weights = decay * scores[None] * step_size.T[:, None, :]
    intra_out = jnp.einsum('hts,shp->thp', weights, values, precision=HIGH)
    tail_weight = jnp.exp(running[-1][None, :] - running) * step_size
    local_state = jnp.einsum('sh,shp,sn->hpn', tail_weight, values, input_projector, precision=HIGH)
    return (running, intra_out, local_state)

def outer_part(conv_out, running, intra_out, gate_rows, skip, norm_gain, state_in):
    length, head_count = running.shape
    inner_width = head_count * P_SIZE
    values = conv_out[:, :inner_width].reshape(length, head_count, P_SIZE)
    read_vec = conv_out[:, inner_width + N:]
    carried = jnp.einsum('tn,hpn->thp', read_vec, state_in, precision=HIGH)
    mixed = intra_out + jnp.exp(running)[:, :, None] * carried + skip[None, :, None] * values
    gated = mixed.reshape(length, inner_width) * jax.nn.silu(gate_rows.astype(jnp.float32))
    scale = lax.rsqrt(lax.optimization_barrier(jnp.mean(gated * gated, axis=-1, keepdims=True)) + EPS)
    return gated * scale * norm_gain[None, :]

def forward(input_seq, gate_seq, raw_seq, conv_weight, conv_bias, dt_bias, a_log, skip, norm_gain):
    channels = input_seq.shape[1]
    padded = jnp.concatenate([jnp.zeros((KW - 1, channels), jnp.float32), input_seq.astype(jnp.float32)], axis=0)
    conv_out = convolve(padded, conv_weight, conv_bias)
    slab_count = TOKENS_PER_ROW // TOK_DEV
    conv_blocks = conv_out.reshape(slab_count, TOK_DEV, channels)
    raw_blocks = raw_seq.reshape(slab_count, TOK_DEV, H)
    gate_blocks = gate_seq.reshape(slab_count, TOK_DEV, H * P_SIZE)

    def advance(state_in, blocks):
        conv_block, raw_block, gate_block = blocks
        running, intra_out, local_state = slab_pieces(conv_block, raw_block, dt_bias, a_log)
        normed = outer_part(conv_block, running, intra_out, gate_block, skip, norm_gain, state_in)
        state_end = jnp.exp(running[-1])[:, None, None] * state_in + local_state
        return (state_end, normed)
    start = jnp.zeros((H, P_SIZE, N), jnp.float32)
    closing_state, normed = lax.scan(jax.checkpoint(advance), start, (conv_blocks, raw_blocks, gate_blocks))
    return normed.reshape(TOKENS_PER_ROW, H * P_SIZE)

def reference(conv_input, gate_input, dt_raw, grad_output, conv_weight, conv_bias, dt_bias, a_log, skip, norm_gain):
    grads_input = []
    grads_gate = []
    grads_step = []
    param_sums = [jnp.zeros_like(conv_weight), jnp.zeros_like(conv_bias), jnp.zeros_like(dt_bias), jnp.zeros_like(a_log), jnp.zeros_like(skip), jnp.zeros_like(norm_gain)]
    for sequence in range(BATCH_ROWS):
        primal, backward = jax.vjp(forward, conv_input[sequence], gate_input[sequence], dt_raw[sequence], conv_weight, conv_bias, dt_bias, a_log, skip, norm_gain)
        results = backward(grad_output[sequence].astype(jnp.float32))
        grads_input.append(results[0])
        grads_gate.append(results[1])
        grads_step.append(results[2])
        param_sums = [param_sums[number] + results[3 + number] for number in range(6)]
    return (jnp.stack(grads_input), jnp.stack(grads_gate), jnp.stack(grads_step), param_sums[0], param_sums[1], param_sums[2], param_sums[3], param_sums[4], param_sums[5])
```

```python
import functools

import jax
import jax.numpy as jnp
from jax import lax
from jax.experimental import pallas as pl
from jax.experimental.pallas import tpu as pltpu
from jax.sharding import PartitionSpec as P

P_SIZE = 64
N = 64
EPS = 1e-05
LANES = 2 * P_SIZE
HALO = 8
SMALL = 8
DEC_ROWS = 32
F32, BF16 = jnp.float32, jnp.bfloat16
HIGH = lax.Precision.HIGHEST


def dot(a, b, over=(1, 0), precision=None):
    return lax.dot_general(
        a, b, (((over[0],), (over[1],)), ((), ())), precision=precision, preferred_element_type=F32
    )


def iota(shape, axis):
    return lax.broadcasted_iota(jnp.int32, shape, axis)


def sigmoid(x):
    return 0.5 * jnp.tanh(0.5 * x) + 0.5


def split(x):
    high = x.astype(BF16)
    return high, (x - high.astype(F32)).astype(BF16)


def block(position):
    return slice(position * LANES, (position + 1) * LANES)


def by_head(columns, pair, shape):
    first = jnp.broadcast_to(columns[:, 2 * pair : 2 * pair + 1], shape)
    second = jnp.broadcast_to(columns[:, 2 * pair + 1 : 2 * pair + 2], shape)
    return jnp.where(iota(shape, 1) < P_SIZE, first, second)


def apart(pair_block):
    first = iota(pair_block.shape, 1) < P_SIZE
    zero = jnp.zeros_like(pair_block)
    return jnp.concatenate(
        [jnp.where(first, pair_block, zero), jnp.where(first, zero, pair_block)], axis=0
    )


def head_sums(product, pair):
    shape = (LANES, LANES)
    pick = (iota(shape, 1) == 2 * pair + (iota(shape, 0) >= P_SIZE).astype(jnp.int32)).astype(BF16)
    high, low = split(product)
    return dot(jnp.concatenate([high, low], axis=1), jnp.concatenate([pick, pick], axis=0))


def fill_rows(rows, x_ref, halo_ref):
    rows[0:HALO, :] = halo_ref[...].astype(F32)
    rows[HALO:, :] = x_ref[...].astype(F32)


def before_silu(rows, full, cols, taps, length):
    start = HALO - (taps - 1)
    total = full[taps : taps + 1, cols] + full[0:1, cols] * rows[start : start + length, cols]
    for tap in range(1, taps):
        total = total + full[tap : tap + 1, cols] * rows[start + tap : start + tap + length, cols]
    return total


def pack_kernel(cw, cb, dtb, al, sk, gain, out):
    out[...] = jnp.zeros_like(out)
    taps, width = cw.shape
    out[0:taps, 0:width] = cw[...]
    out[taps : taps + 1, 0:width] = cb[...]
    out[taps + 1 : taps + 2, 0 : gain.shape[1]] = gain[...]
    for number, ref in enumerate((dtb, al, sk)):
        out[taps + 2 : taps + 3, number * LANES : number * LANES + ref.shape[1]] = ref[...]


def placement(position, width):
    start = position * width
    base = start // LANES * LANES
    return base, start - base


def front_kernel(
    taps, sizes, core, x, halo, pieces, dt, conv, full, gain, small, cols, rows_out, mine, other, decs, rows, states, wide
):
    length, channels = x.shape
    parts, _, piece_width = pieces.shape
    width, gain_width, heads_here = sizes
    heads = heads_here * parts
    pairs = heads // 2
    half = pairs // 2
    features = heads * P_SIZE
    fill_rows(rows, x, halo)
    full[...] = jnp.zeros_like(full)
    small[...] = jnp.zeros_like(small)
    for part in range(parts):
        base, shift = placement(part, width)
        piece = jnp.concatenate([pieces[part], jnp.zeros((SMALL, LANES), F32)], axis=1)
        if shift:
            piece = pltpu.roll(piece, shift, 1)
        full[:, base : base + piece_width + LANES] += piece
        gain[:, part * gain_width : (part + 1) * gain_width] = pieces[
            part, taps + 1 : taps + 2, 0:gain_width
        ]
        for number in range(3):
            row = pieces[part, taps + 2 : taps + 3, block(number)]
            if part:
                row = pltpu.roll(row, part * heads_here, 1)
            small[number : number + 1, :] += row
    wide[...] = jnp.zeros_like(wide)
    wide[:, 0:heads] = dt[...]
    raw = wide[...] + small[0:1, :]
    step = jnp.maximum(raw, 0.0) + jnp.log1p(jnp.exp(-jnp.abs(raw)))
    logs = -jnp.exp(small[1:2, :]) * step
    square = (length, length)
    lower = (iota(square, 0) >= iota(square, 1)).astype(F32)
    running = dot(lower, logs, precision=HIGH)
    running_t = running.T
    step_t = step.T
    last = jnp.broadcast_to(running_t[:, length - 1 : length], running_t.shape)
    tail_t = jnp.exp(last - running_t) * step_t
    cols[0] = step
    cols[1] = running
    rows_out[0] = step_t
    rows_out[1] = running_t
    rows_out[2] = tail_t
    wide[...] = jnp.exp(last)[:, 0:LANES]
    first = iota((half, LANES), 1) < P_SIZE
    for side in range(2):
        even = wide[pl.ds(2 * half * side, half, stride=2), :]
        odd = wide[pl.ds(2 * half * side + 1, half, stride=2), :]
        high, low = split(jnp.where(first, even, odd))
        decay_rows = jnp.zeros((DEC_ROWS // 2 - half, LANES), BF16)
        decs[side] = jnp.concatenate([high, decay_rows, low, decay_rows], axis=0)
    for position in list(range(pairs, channels // LANES)) + list(range(pairs)):
        here = block(position)
        pre = before_silu(rows, full, here, taps, length)
        out = (pre * sigmoid(pre)).astype(BF16)
        conv[:, here] = out
        if position == pairs:
            write_t = out.astype(F32).T[0:N, :]
        else:
            scaled = jnp.concatenate(
                [
                    (write_t * tail_t[2 * position + which : 2 * position + which + 1, :]).astype(BF16)
                    for which in range(2)
                ],
                axis=1,
            )
            start = position % half * N
            states[position // half, start : start + N, :] = dot(scaled, apart(out)).astype(BF16)
    end = half * N
    states[:, end : end + DEC_ROWS, :] = decs[...]
    mine[...] = states[core[0]]
    other[...] = states[1 - core[0]]


def head_weights(cols, rows_ref, head, causal, scores):
    gap = cols[1, :, head : head + 1] - rows_ref[1, head : head + 1, :]
    scaled = jnp.exp(jnp.where(causal, gap, -1e30)) * rows_ref[0, head : head + 1, :]
    return scaled, (scaled * scores).astype(BF16)


def intra_kernel(taps, x, halo, full, conv, cols, rows_ref, small, local, slope, rows):
    length, channels = x.shape
    features = local.shape[1]
    pairs = features // LANES
    write = conv[:, features : features + N]
    read = conv[:, features + N : features + 2 * N]
    scores = dot(read, write, (1, 1))
    square = (length, length)
    causal = iota(square, 0) >= iota(square, 1)
    for pair in range(pairs):
        weights = jnp.concatenate(
            [head_weights(cols, rows_ref, 2 * pair + which, causal, scores)[1] for which in range(2)],
            axis=1,
        )
        values = conv[:, block(pair)]
        skip = by_head(small[2:3, :], pair, (1, LANES))
        local[:, block(pair)] = dot(weights, apart(values)) + skip * values.astype(F32)
    fill_rows(rows, x, halo)
    for position in range(channels // LANES):
        here = block(position)
        pre = before_silu(rows, full, here, taps, length)
        gate = sigmoid(pre)
        slope[:, here] = gate * (1.0 + pre * (1.0 - gate))


def norm_kernel(
    core, local, conv, cols, gate, grad, gain, own, got, decs, mixed, stats, mine, other, entry, gated, silus, states
):
    length, features = local.shape
    pairs = features // LANES
    half = pairs // 2
    shape = (length, LANES)
    entry[core[0]] = own[...]
    entry[1 - core[0]] = got[...]
    read = conv[:, features + N : features + 2 * N]
    decay = jnp.exp(cols[1])
    square_sum = jnp.zeros(shape, F32)
    cross_sum = jnp.zeros(shape, F32)
    for pair in range(pairs):
        here = block(pair)
        start = pair % half * N
        carried = dot(read, entry[pair // half, start : start + N, :])
        mix = local[:, here] + by_head(decay, pair, shape) * carried
        mixed[:, here] = mix
        z = gate[:, here].astype(F32)
        silu = z * sigmoid(z)
        silus[:, here] = silu
        product = mix * silu
        gated[:, here] = product
        square_sum += product * product
        cross_sum += product * (grad[:, here].astype(F32) * gain[:, here])
    scale = lax.rsqrt(jnp.sum(square_sum, axis=1, keepdims=True) * (1.0 / features) + EPS)
    cross = jnp.sum(cross_sum, axis=1, keepdims=True)
    factor = scale * scale * scale * cross * (1.0 / features)
    lane = iota(shape, 1)
    stats[...] = jnp.where(lane == 0, scale, jnp.where(lane == 1, factor, 0.0))
    scale_wide = jnp.broadcast_to(scale, shape)
    factor_wide = jnp.broadcast_to(factor, shape)
    for pair in range(pairs):
        here = block(pair)
        grad_gated = scale_wide * (grad[:, here].astype(F32) * gain[:, here]) - factor_wide * gated[:, here]
        weighted = by_head(decay, pair, shape) * (grad_gated * silus[:, here])
        start = pair % half * N
        states[pair // half, start : start + N, :] = dot(read, weighted.astype(BF16), (0, 0)).astype(BF16)
    end = half * N
    states[:, end : end + DEC_ROWS, :] = decs[...]
    mine[...] = states[core[0]]
    other[...] = states[1 - core[0]]


def back_kernel(
    core, mixed, conv, cols, rows_ref, small, gate, grad, gain, stats, own, got, grad_gate, grad_values, sums, grad_gain, grad_small, grad_vecs, entry
):
    length, features = mixed.shape
    pairs = features // LANES
    half = pairs // 2
    shape = (length, LANES)
    entry[core[0]] = own[...]
    entry[1 - core[0]] = got[...]
    write = conv[:, features : features + N]
    read = conv[:, features + N : features + 2 * N]
    scores = dot(read, write, (1, 1))
    square = (length, length)
    causal = iota(square, 0) >= iota(square, 1)
    scale = jnp.broadcast_to(stats[:, 0:1], shape)
    factor = jnp.broadcast_to(stats[:, 1:2], shape)
    decay = jnp.exp(cols[1])
    read_grad = jnp.zeros((length, N), F32)
    score_grad = jnp.zeros(square, F32)
    out_sums = jnp.zeros(shape, F32)
    in_sums = jnp.zeros(shape, F32)
    skip_sums = jnp.zeros(shape, F32)
    first = iota(shape, 1) < P_SIZE
    for pair in range(pairs):
        here = block(pair)
        start = pair % half * N
        z = gate[:, here].astype(F32)
        sig = sigmoid(z)
        silu = z * sig
        mix = mixed[:, here]
        product = mix * silu
        grads = grad[:, here].astype(F32)
        gain_row = gain[:, here]
        grad_gain[:, here] = jnp.sum(grads * (product * scale), axis=0, keepdims=True)
        grad_gated = scale * (grads * gain_row) - factor * product
        grad_mix = grad_gated * silu
        grad_gate[:, here] = (grad_gated * mix * (sig * (1.0 + z * (1.0 - sig)))).astype(BF16)
        values = conv[:, here]
        values_wide = values.astype(F32)
        skip = by_head(small[2:3, :], pair, (1, LANES))
        rounded = grad_mix.astype(BF16)
        inner = mix - skip * values_wide
        out_sums += head_sums(rounded.astype(F32) * inner, pair)
        skip_sums += head_sums(grad_mix * values_wide, pair)
        weighted = (by_head(decay, pair, shape) * grad_mix).astype(BF16)
        read_grad += dot(weighted, entry[pair // half, start : start + N, :], (1, 1))
        scaled = [head_weights(cols, rows_ref, 2 * pair + which, causal, scores) for which in range(2)]
        weight_grad = dot(rounded, apart(values), (1, 1))
        score_grad += weight_grad[:, 0:length] * scaled[0][0] + weight_grad[:, length:] * scaled[1][0]
        both = dot(jnp.concatenate([scaled[0][1], scaled[1][1]], axis=1), rounded, (0, 0))
        value_grad = jnp.where(first, both[0:length], both[length:])
        in_sums += head_sums(values_wide * value_grad, pair)
        grad_values[:, here] = value_grad + skip * grad_mix
    sums[0] = out_sums
    sums[1] = in_sums
    high, low = split(score_grad)
    read_grad += dot(high, write) + dot(low, write)
    write_grad = dot(high, read, (0, 0)) + dot(low, read, (0, 0))
    grad_vecs[...] = jnp.concatenate([write_grad, read_grad], axis=1)
    grad_small[...] = jnp.zeros_like(grad_small)
    grad_small[2:3, :] = jnp.sum(skip_sums, axis=0, keepdims=True)


def close_kernel(
    taps, sizes, place, x, halo, full, conv, slope, cols, rows_ref, small, decs, entry_own, entry_got, leave_own, leave_got,
    grad_values, grad_vecs, sums, grad_gain, grad_small, grad_x, back, ending, grad_dt, *rest
):
    parts = len(rest) - 6
    outs, (entry, leave, rows, slopes, whole, cut) = rest[:parts], rest[parts:]
    core, position_here = place[0], place[1]
    length, channels = x.shape
    features = grad_values.shape[1]
    pairs = features // LANES
    half = pairs // 2
    width, gain_width, heads_here = sizes
    heads = heads_here * parts
    shape = (length, LANES)
    entry[core] = entry_own[...]
    entry[1 - core] = entry_got[...]
    leave[core] = leave_own[...]
    leave[1 - core] = leave_got[...]
    fill_rows(rows, x, halo)
    slopes[...] = jnp.zeros_like(slopes)
    whole[...] = jnp.zeros_like(whole)
    write = conv[:, features : features + N]
    step = cols[0]
    running = cols[1]
    last = running[length - 1 : length, :]
    tail = jnp.exp(last - running) * step
    state_sums = jnp.zeros(shape, F32)
    end_sums = jnp.zeros((8, LANES), F32)
    write_grad = jnp.zeros((length, N), F32)

    def through_conv(position, grad_out):
        here = block(position)
        grad_pre = grad_out.astype(BF16).astype(F32) * slope[:, here]
        slopes[HALO : HALO + length, here] = grad_pre
        start = HALO - (taps - 1)
        for tap in range(taps):
            whole[tap : tap + 1, here] = jnp.sum(
                grad_pre * rows[start + tap : start + tap + length, here], axis=0, keepdims=True
            )
        whole[taps : taps + 1, here] = jnp.sum(grad_pre, axis=0, keepdims=True)
        total = jnp.zeros((HALO + length, LANES), F32)
        for tap in range(taps):
            ahead = taps - 1 - tap
            total += full[tap : tap + 1, here] * slopes[ahead : ahead + HALO + length, here]
        back[:, here] = total[0:HALO].astype(BF16)
        grad_x[:, here] = total[HALO:].astype(BF16)
        ending[:, here] = total[length:]

    for pair in range(pairs):
        here = block(pair)
        start = pair % half * N
        leaving = leave[pair // half, start : start + N, :]
        values = conv[:, here].astype(F32)
        tail_wide = by_head(tail, pair, shape)
        state_grad = tail_wide * dot(write, leaving)
        state_sums += head_sums(values * state_grad, pair)
        write_grad += dot((tail_wide * values).astype(BF16), leaving, (1, 1))
        entering = entry[pair // half, start : start + N, :].astype(F32)
        overlap = jnp.sum(leaving.astype(F32) * entering, axis=0, keepdims=True)
        end_sums += head_sums(jnp.broadcast_to(overlap, (8, LANES)), pair)
        through_conv(pair, grad_values[:, here] + state_grad)
    vecs = grad_vecs[...]
    vecs = vecs + jnp.concatenate([write_grad, jnp.zeros_like(write_grad)], axis=1)
    through_conv(pairs, vecs)

    into = sums[1] + state_sums
    change = sums[0] - into
    end_grad = jnp.sum(state_sums, axis=0, keepdims=True) + jnp.exp(last) * end_sums[0:1, :]
    square = (length, length)
    upper = (iota(square, 0) <= iota(square, 1)).astype(F32)
    log_grad = dot(upper, change, precision=HIGH) + end_grad
    rate = jnp.exp(small[1:2, :])
    raw_grad = (into / step - rate * log_grad) * (1.0 - jnp.exp(-step))
    grad_dt[...] = raw_grad[:, 0:heads]
    vectors = (
        jnp.sum(raw_grad, axis=0, keepdims=True),
        jnp.sum(-rate * step * log_grad, axis=0, keepdims=True),
        grad_small[2:3, :],
    )
    piece_width = cut.shape[2]
    for part in range(parts):
        base, shift = placement(part, width)
        piece = whole[:, base : base + piece_width + LANES]
        if shift:
            piece = pltpu.roll(piece, piece_width + LANES - shift, 1)
        cut[part] = piece[:, 0:piece_width]
        cut[part, taps + 1 : taps + 2, 0:gain_width] = grad_gain[:, part * gain_width : (part + 1) * gain_width]
        for number, vector in enumerate(vectors):
            row = pltpu.roll(vector, LANES - part * heads_here, 1) if part else vector
            cut[part, taps + 2 : taps + 3, block(number)] = row
    for distance in range(parts):
        outs[distance][...] = cut[lax.rem(position_here + distance, parts)]


def patch_kernel(whole, ending, back, out):
    rows = ending.shape[0]
    keep = out.shape[0] - rows
    patched = ending[...] + back[...].astype(F32)
    out[...] = jnp.concatenate([whole[0:keep, :].astype(F32), patched], axis=0).astype(BF16)


def unpack_kernel(terms, *refs):
    total = refs[0][...]
    for ref in refs[1:terms]:
        total = total + ref[...]
    cw, cb, dtb, al, sk, gain = refs[terms:]
    taps, width = cw.shape
    cw[...] = total[0:taps, 0:width]
    cb[...] = total[taps : taps + 1, 0:width]
    gain[...] = total[taps + 1 : taps + 2, 0 : gain.shape[1]]
    for number, ref in enumerate((dtb, al, sk)):
        ref[...] = total[taps + 2 : taps + 3, number * LANES : number * LANES + ref.shape[1]]


def add_kernel(*refs):
    total = refs[0][...]
    for ref in refs[1:-1]:
        total = total + ref[...]
    refs[-1][...] = total


def parts_of(message):
    end = message.shape[0] - DEC_ROWS
    half = end // N
    state = message[0:end, :].astype(F32).reshape(half, N, LANES)
    middle = end + DEC_ROWS // 2
    decay = message[end:middle, :].astype(F32) + message[middle:, :].astype(F32)
    return state, decay


def joined(first, second):
    state, decay = second
    half = state.shape[0]
    return decay[0:half].reshape(half, 1, LANES) * first[0] + state, decay * first[1]


def store(out, value):
    state, decay = value
    end = state.shape[0] * N
    middle = end + DEC_ROWS // 2
    out[0:end, :] = state.reshape(end, LANES).astype(BF16)
    high, low = split(decay)
    out[end:middle, :] = high
    out[middle:, :] = low


def meet_kernel(role, mine, got, out):
    later = role[0] == 1
    a, b = mine[...], got[...]
    first, second = jnp.where(later, b, a), jnp.where(later, a, b)
    store(out, joined(parts_of(first), parts_of(second)))


def join_kernel(first, second, out):
    store(out, joined(parts_of(first[...]), parts_of(second[...])))


def enter_kernel(role, entering, mine, got, own, send):
    later = role[0] == 1
    a, b = mine[...], got[...]
    before = parts_of(entering[...])
    state, _ = joined(before, parts_of(jnp.where(later, b, a)))
    after = state.reshape(own.shape)
    start = before[0].reshape(own.shape)
    own[...] = jnp.where(later, after, start).astype(BF16)
    send[...] = jnp.where(later, start, after).astype(BF16)


def call(kernel, outs, args, scratch=(), scalars=0, megabytes=16, flops=0, name=None):
    specs = [pl.BlockSpec(memory_space=pltpu.SMEM)] * scalars
    specs += [pl.BlockSpec(memory_space=pltpu.VMEM)] * (len(args) - scalars)
    moved = sum(a.size * a.dtype.itemsize for a in args)
    moved += sum(o.size * o.dtype.itemsize for o in outs)
    return pl.pallas_call(
        kernel,
        out_shape=outs,
        in_specs=specs,
        out_specs=[pl.BlockSpec(memory_space=pltpu.VMEM)] * len(outs),
        scratch_shapes=list(scratch),
        compiler_params=pltpu.CompilerParams(vmem_limit_bytes=megabytes << 20),
        cost_estimate=pl.CostEstimate(flops=flops, bytes_accessed=moved, transcendentals=0),
        name=name,
    )(*args)


def like(shape, dtype=F32):
    return jax.ShapeDtypeStruct(shape, dtype)


def shift(value, axis, route):
    count = lax.axis_size(axis)
    pairs = [(i, route(i)) for i in range(count)]
    return lax.ppermute(value, axis, [(i, j) for i, j in pairs if 0 <= j < count])


def entering_states(mine, other, core, reverse):
    chips = lax.axis_size("seq") // 2
    sign = -1 if reverse else 1
    role = 1 - core if reverse else core
    message = like(mine.shape, BF16)
    half = like((mine.shape[0] - DEC_ROWS, LANES), BF16)
    got = shift(other, "seq", lambda i: i ^ 1)
    chip = call(meet_kernel, [message], [role, mine, got], scalars=1, name="meet")[0]
    before = shift(chip, "seq", lambda i: i + 2 * sign)
    window = 1
    while window < chips - 1:
        longer = call(join_kernel, [message], [before, chip], name="join")[0]
        distance = window + 1
        far = shift(longer, "seq", lambda i: i + 2 * distance * sign)
        before = call(join_kernel, [message], [far, before], name="join")[0]
        window = 2 * window + 1
    own, send = call(
        enter_kernel, [half, half], [role, before, mine, got], scalars=1, name="enter"
    )
    return own, shift(send, "seq", lambda i: i ^ 1)


def shards(
    conv_input, gate_input, dt_raw, grad_output, conv_weight, conv_bias, dt_bias, a_log, skip, norm_gain
):
    x, gate, dt, grad = conv_input[0], gate_input[0], dt_raw[0], grad_output[0]
    length, channels = x.shape
    features = gate.shape[1]
    heads = dt.shape[1]
    pairs = heads // 2
    half = pairs // 2
    taps, width = conv_weight.shape
    gain_width = norm_gain.shape[0]
    heads_here = dt_bias.shape[0]
    parts = lax.axis_size("fsdp")
    devices = lax.axis_size("seq")
    sizes = (width, gain_width, heads_here)
    piece_width = -(-width // LANES) * LANES
    place_base = placement(parts - 1, width)[0]
    full_width = place_base + piece_width + LANES
    core = jnp.reshape(lax.axis_index("seq") % 2, (1,)).astype(jnp.int32)
    fsdp_index = jnp.reshape(lax.axis_index("fsdp"), (1,)).astype(jnp.int32)
    place = jnp.concatenate([core, fsdp_index])

    halo = shift(x[length - HALO :], "seq", lambda i: i + 1)
    piece = call(
        pack_kernel,
        [like((SMALL, piece_width))],
        [
            conv_weight,
            conv_bias.reshape(1, -1),
            dt_bias.reshape(1, -1),
            a_log.reshape(1, -1),
            skip.reshape(1, -1),
            norm_gain.reshape(1, -1),
        ],
        name="pack",
    )[0]
    pieces = lax.all_gather(piece, "fsdp")

    message = half * N + DEC_ROWS
    conv, full, gain, small, cols, rows, mine, other, decs = call(
        functools.partial(front_kernel, taps, sizes),
        [
            like((length, channels), BF16),
            like((SMALL, full_width)),
            like((1, features)),
            like((8, LANES)),
            like((2, length, LANES)),
            like((3, LANES, length)),
            like((message, LANES), BF16),
            like((message, LANES), BF16),
            like((2, DEC_ROWS, LANES), BF16),
        ],
        [core, x, halo, pieces, dt],
        [
            pltpu.VMEM((HALO + length, channels), F32),
            pltpu.VMEM((2, message, LANES), BF16),
            pltpu.VMEM((length, LANES), F32),
        ],
        scalars=1,
        name="front",
    )
    local, slope = call(
        functools.partial(intra_kernel, taps),
        [like((length, features)), like((length, channels))],
        [x, halo, full, conv, cols, rows, small],
        [pltpu.VMEM((HALO + length, channels), F32)],
        flops=2 * length * length * features,
        name="intra",
    )
    entry_own, entry_got = entering_states(mine, other, core, False)
    mixed, stats, mine, other = call(
        norm_kernel,
        [
            like((length, features)),
            like((length, LANES)),
            like((message, LANES), BF16),
            like((message, LANES), BF16),
        ],
        [core, local, conv, cols, gate, grad, gain, entry_own, entry_got, decs],
        [
            pltpu.VMEM((2, half * N, LANES), BF16),
            pltpu.VMEM((length, features), F32),
            pltpu.VMEM((length, features), F32),
            pltpu.VMEM((2, message, LANES), BF16),
        ],
        scalars=1,
        name="norm",
    )
    leave_own, leave_got = entering_states(mine, other, core, True)
    grad_gate, grad_values, sums, grad_gain, grad_small, grad_vecs = call(
        back_kernel,
        [
            like((length, features), BF16),
            like((length, features)),
            like((2, length, LANES)),
            like((1, features)),
            like((8, LANES)),
            like((length, LANES)),
        ],
        [core, mixed, conv, cols, rows, small, gate, grad, gain, stats, entry_own, entry_got],
        [pltpu.VMEM((2, half * N, LANES), BF16)],
        scalars=1,
        flops=6 * length * length * features,
        name="back",
    )
    grad_x, back, ending, grad_dt, *shares = call(
        functools.partial(close_kernel, taps, sizes),
        [
            like((length, channels), BF16),
            like((HALO, channels), BF16),
            like((HALO, channels)),
            like((length, heads)),
        ]
        + [like((SMALL, piece_width))] * parts,
        [
            place, x, halo, full, conv, slope, cols, rows, small, decs, entry_own, entry_got, leave_own, leave_got,
            grad_values, grad_vecs, sums, grad_gain, grad_small,
        ],
        [
            pltpu.VMEM((2, half * N, LANES), BF16),
            pltpu.VMEM((2, half * N, LANES), BF16),
            pltpu.VMEM((HALO + length, channels), F32),
            pltpu.VMEM((2 * HALO + length, channels), F32),
            pltpu.VMEM((SMALL, full_width), F32),
            pltpu.VMEM((parts, SMALL, piece_width), F32),
        ],
        scalars=1,
        megabytes=24,
        name="close",
    )
    piece_like = like((SMALL, piece_width))
    terms = [shares[0]]
    for distance in range(1, parts):
        terms.append(shift(shares[distance], "fsdp", lambda i: (i + distance) % parts))
    back = shift(back, "seq", lambda i: i - 1)
    total = call(add_kernel, [piece_like], terms, name="add")[0]
    total = call(
        add_kernel, [piece_like], [total, shift(total, "seq", lambda i: i ^ 1)], name="add"
    )[0]
    chips = devices // 2
    if chips <= 4:
        terms = [total] + [
            shift(total, "seq", lambda i: (i + 2 * distance) % devices) for distance in range(1, chips)
        ]
    else:
        terms = [lax.psum(total, "seq") * 0.5]
    outputs = call(
        functools.partial(unpack_kernel, len(terms)),
        [
            like((taps, width)),
            like((1, width)),
            like((1, heads_here)),
            like((1, heads_here)),
            like((1, heads_here)),
            like((1, gain_width)),
        ],
        terms,
        name="unpack",
    )
    grad_x = pl.pallas_call(
        patch_kernel,
        grid=(1,),
        out_shape=like((length, channels), BF16),
        in_specs=[
            pl.BlockSpec((2 * HALO, channels), lambda i: (length // (2 * HALO) - 1, 0)),
            pl.BlockSpec((HALO, channels), lambda i: (0, 0)),
            pl.BlockSpec((HALO, channels), lambda i: (0, 0)),
        ],
        out_specs=pl.BlockSpec((2 * HALO, channels), lambda i: (length // (2 * HALO) - 1, 0)),
        input_output_aliases={0: 0},
        name="patch",
    )(grad_x, ending, back)
    cw, cb, dtb, al, sk, gn = outputs
    return (
        grad_x[None],
        grad_gate[None],
        grad_dt[None],
        cw,
        cb.reshape(-1),
        dtb.reshape(-1),
        al.reshape(-1),
        sk.reshape(-1),
        gn.reshape(-1),
    )


def solution(mesh):
    tokens = P("fsdp", "seq", None)
    in_specs = (tokens,) * 4 + (P(None, "fsdp"),) + (P("fsdp"),) * 5
    out_specs = (tokens,) * 3 + (P(None, "fsdp"),) + (P("fsdp"),) * 5
    return jax.shard_map(shards, mesh=mesh, in_specs=in_specs, out_specs=out_specs, check_vma=False)
```

```python
import functools

import jax
import jax.numpy as jnp
from jax import lax
from jax.experimental import pallas as pl
from jax.experimental.pallas import tpu as pltpu
from jax.sharding import PartitionSpec as P

P_SIZE = 64
N = 64
EPS = 1e-05
LANES = 2 * P_SIZE
HALO = 8
SMALL = 8
STREAMS = 2
FOLDS = 4
BACK_ROWS = 16
CUT = 16
DEC_ROWS = 16
F32, BF16 = jnp.float32, jnp.bfloat16
HIGH = lax.Precision.HIGHEST


def dot(a, b, over=(1, 0), precision=None):
    return lax.dot_general(
        a, b, (((over[0],), (over[1],)), ((), ())), precision=precision, preferred_element_type=F32
    )


def here_at():
    index = lax.axis_index("seq")
    return lax.rem(index, 2), lax.div(index, 2), lax.axis_index("fsdp")


def iota(shape, axis):
    return lax.broadcasted_iota(jnp.int32, shape, axis)


def sigmoid(x):
    return 0.5 * jnp.tanh(0.5 * x) + 0.5


def split(x):
    high = x.astype(BF16)
    return high, (x - high.astype(F32)).astype(BF16)


def block(position):
    return slice(position * LANES, (position + 1) * LANES)


def by_head(columns, pair, shape):
    first = jnp.broadcast_to(columns[:, 2 * pair : 2 * pair + 1], shape)
    second = jnp.broadcast_to(columns[:, 2 * pair + 1 : 2 * pair + 2], shape)
    return jnp.where(iota(shape, 1) < P_SIZE, first, second)


def apart(pair_block):
    first = iota(pair_block.shape, 1) < P_SIZE
    zero = jnp.zeros_like(pair_block)
    return jnp.concatenate(
        [jnp.where(first, pair_block, zero), jnp.where(first, zero, pair_block)], axis=0
    )


def head_sums(product, pair):
    shape = (LANES, LANES)
    pick = (iota(shape, 1) == 2 * pair + (iota(shape, 0) >= P_SIZE).astype(jnp.int32)).astype(BF16)
    high, low = split(product)
    return dot(jnp.concatenate([high, low], axis=1), jnp.concatenate([pick, pick], axis=0))


def before_silu(rows, full, cols, taps, length):
    start = HALO - (taps - 1)
    total = full[taps : taps + 1, cols] + full[0:1, cols] * rows[start : start + length, cols]
    for tap in range(1, taps):
        total = total + full[tap : tap + 1, cols] * rows[start + tap : start + tap + length, cols]
    return total


def open_kernel(x, dt, cw, cb, dtb, al, sk, gain, halo, out, own, late, raw, *rest):
    held, sems = rest[:-1], rest[-1]
    ending = x.at[pl.ds(x.shape[0] - late.shape[0], late.shape[0])]
    copies = [
        pltpu.make_async_copy(source, target, sems.at[number])
        for number, (source, target) in enumerate(
            zip((cw, cb, dtb, al, sk, gain, dt, ending), held + (raw, late))
        )
    ]
    for copy in copies:
        copy.start()
    out[...] = jnp.zeros_like(out)
    for copy in copies:
        copy.wait()
    halo[...] = late[...].astype(F32)[HALO:].astype(BF16)
    cw, cb, dtb, al, sk, gain = held
    taps, width = cw.shape
    out[0:taps, 0:width] = cw[...]
    out[taps : taps + 1, 0:width] = cb[...]
    out[taps + 1 : taps + 2, 0 : gain.shape[0]] = gain[...].reshape(1, -1)
    for number, ref in enumerate((dtb, al, sk)):
        out[taps + 2 : taps + 3, number * LANES : number * LANES + ref.shape[1]] = ref[...]
    own[0:SMALL, :] = out[...]
    own[SMALL:, :] = jnp.zeros((SMALL, own.shape[1]), F32)
    for group in range(raw.shape[0] // SMALL):
        own[SMALL:, block(group)] = raw[group * SMALL : (group + 1) * SMALL, :]


def placement(position, width):
    start = position * width
    base = start // LANES * LANES
    return base, start - base


def state_rows(pair, half):
    pair = pair % half
    return [slice((cut * half + pair) * CUT, (cut * half + pair + 1) * CUT) for cut in range(N // CUT)]


def put_state(states, pair, half, value):
    for cut, rows in enumerate(state_rows(pair, half)):
        states[rows, :] = value[cut * CUT : (cut + 1) * CUT]


def get_state(states, pair, half):
    return jnp.concatenate([states[rows, :] for rows in state_rows(pair, half)], axis=0)


def hand_out(states, decs, core, mine, other):
    end = states.shape[1] - DEC_ROWS
    states[:, end:, :] = decs[...]
    mine[...] = states[core]
    other[...] = states[1 - core]


def pack_decays(decays):
    high, low = split(decays)
    group = iota(decays.shape, 1) // (P_SIZE // 2)
    return jnp.where(lax.rem(group, 2) == 0, high.astype(F32), low.astype(F32)).astype(BF16)


def unpack_decays(packed):
    value = packed.astype(F32)
    group = iota(value.shape, 1) // (P_SIZE // 2)
    ahead = pltpu.roll(value, LANES - P_SIZE // 2, 1)
    behind = pltpu.roll(value, P_SIZE // 2, 1)
    return value + jnp.where(lax.rem(group, 2) == 0, ahead, behind)


def gather_kernel(taps, sizes, parts, length, own, *refs):
    given, refs = refs[: parts - 1], refs[parts - 1 :]
    full, gain, small, cols, rows_out, decs, wide, pieces = refs
    mine_at = here_at()[2]
    piece_width = pieces.shape[2]
    pieces[mine_at] = own[0:SMALL, :]
    for distance in range(1, parts):
        pieces[lax.rem(mine_at + parts - distance, parts)] = given[distance - 1][...]
    width, gain_width, heads_here = sizes
    heads = heads_here * parts
    half = heads // 4
    full[...] = jnp.zeros_like(full)
    small[...] = jnp.zeros_like(small)
    wide[...] = jnp.zeros_like(wide)
    for group in range(heads // SMALL):
        wide[group * SMALL : (group + 1) * SMALL, :] = own[SMALL:, block(group)]
    for part in range(parts):
        base, shift = placement(part, width)
        piece = jnp.concatenate([pieces[part], jnp.zeros((SMALL, LANES), F32)], axis=1)
        if shift:
            piece = pltpu.roll(piece, shift, 1)
        full[:, base : base + piece_width + LANES] += piece
        gain[:, part * gain_width : (part + 1) * gain_width] = pieces[
            part, taps + 1 : taps + 2, 0:gain_width
        ]
        for number in range(3):
            row = pieces[part, taps + 2 : taps + 3, block(number)]
            if part:
                row = pltpu.roll(row, part * heads_here, 1)
            small[number : number + 1, :] += row
    raw = wide[...].T + small[0:1, :]
    step = jnp.maximum(raw, 0.0) + jnp.log1p(jnp.exp(-jnp.abs(raw)))
    logs = -jnp.exp(small[1:2, :]) * step
    square = (length, length)
    lower = (iota(square, 0) >= iota(square, 1)).astype(F32)
    running = dot(lower, logs, precision=HIGH)
    running_t = running.T
    step_t = step.T
    last = jnp.broadcast_to(running_t[:, length - 1 : length], running_t.shape)
    cols[0] = step
    cols[1] = running
    rows_out[0] = step_t
    rows_out[1] = running_t
    rows_out[2] = jnp.exp(last - running_t) * step_t
    wide[...] = jnp.exp(last)[:, 0:LANES]
    first = iota((half, LANES), 1) < P_SIZE
    for side in range(2):
        even = wide[pl.ds(2 * half * side, half, stride=2), :]
        odd = wide[pl.ds(2 * half * side + 1, half, stride=2), :]
        decays = jnp.where(first, even, odd)
        decs[side] = pack_decays(
            jnp.concatenate([decays, jnp.zeros((DEC_ROWS - half, LANES), F32)], axis=0)
        )


def side_block(pair):
    return pl.ds(pl.multiple_of(pair * LANES, LANES), LANES)


def front_side(taps, side, rows, full, tails, decs, write_t, conv, out):
    length = conv.shape[0]
    half = (out.shape[0] - DEC_ROWS) // N
    scale = tails[2, pl.ds(side * 2 * half, 2 * half), :]
    for pair in range(half):
        here = side_block(side * half + pair)
        pre = before_silu(rows, full, here, taps, length)
        value = (pre * sigmoid(pre)).astype(BF16)
        conv[:, here] = value
        scaled = jnp.concatenate(
            [
                (write_t * scale[2 * pair + which : 2 * pair + which + 1, :]).astype(BF16)
                for which in range(2)
            ],
            axis=1,
        )
        put_state(out, pair, half, dot(scaled, apart(value)).astype(BF16))
    out[half * N :, :] = decs[side]


def front_kernel(taps, lifted, halo, full, tails, decs, rows, conv, write_out, other):
    core = here_at()[0]
    length, channels = conv.shape
    rows[0:HALO, :] = halo[...].astype(F32)
    here = block(channels // LANES - 1)
    pre = before_silu(rows, full, here, taps, length)
    vectors = (pre * sigmoid(pre)).astype(BF16)
    conv[:, here] = vectors
    write_t = vectors.astype(F32).T[0:N, :]
    write_out[...] = write_t
    front_side(taps, 1 - core, rows, full, tails, decs, write_t, conv, other)


def front_own_kernel(taps, conv_in, rows, full, tails, decs, write_t, conv, mine):
    front_side(taps, here_at()[0], rows, full, tails, decs, write_t[...], conv, mine)


def head_weights(cols, rows_ref, head, causal, scores):
    gap = cols[1, :, head : head + 1] - rows_ref[1, head : head + 1, :]
    scaled = jnp.exp(jnp.where(causal, gap, -1e30)) * rows_ref[0, head : head + 1, :]
    return scaled, (scaled * scores).astype(BF16)


def intra_kernel(taps, rows, full, conv, cols, rows_ref, small, local, slope):
    length, channels = conv.shape
    features = local.shape[1]
    pairs = features // LANES
    write = conv[:, features : features + N]
    read = conv[:, features + N : features + 2 * N]
    scores = dot(read, write, (1, 1))
    square = (length, length)
    causal = iota(square, 0) >= iota(square, 1)
    for pair in range(pairs):
        weights = jnp.concatenate(
            [head_weights(cols, rows_ref, 2 * pair + which, causal, scores)[1] for which in range(2)],
            axis=1,
        )
        values = conv[:, block(pair)]
        skip = by_head(small[2:3, :], pair, (1, LANES))
        local[:, block(pair)] = dot(weights, apart(values)) + skip * values.astype(F32)
    for position in range(channels // LANES):
        here = block(position)
        pre = before_silu(rows, full, here, taps, length)
        gate = sigmoid(pre)
        slope[:, here] = gate * (1.0 + pre * (1.0 - gate))


def side_columns(columns, side, half):
    return pltpu.roll(columns, lax.rem(LANES - 2 * half * side, LANES), 1)


def mix_side(side, local, conv, cols, gate, grad, gain, entry, mixed, gated, silus):
    length, features = local.shape
    half = features // LANES // 2
    shape = (length, LANES)
    read = conv[:, features + N : features + 2 * N]
    decay = side_columns(jnp.exp(cols[1]), side, half)
    square_sum = jnp.zeros(shape, F32)
    cross_sum = jnp.zeros(shape, F32)
    for pair in range(half):
        here = side_block(side * half + pair)
        carried = dot(read, get_state(entry, pair, half))
        mix = local[:, here] + by_head(decay, pair, shape) * carried
        mixed[:, here] = mix
        z = gate[:, here].astype(F32)
        silu = z * sigmoid(z)
        silus[:, here] = silu
        product = mix * silu
        gated[:, here] = product
        square_sum += product * product
        cross_sum += product * (grad[:, here].astype(F32) * gain[:, here])
    return square_sum, cross_sum


def norm_own_kernel(local, conv, cols, gate, grad, gain, entry, mixed, gated, silus, sums):
    square, cross = mix_side(
        here_at()[0], local, conv, cols, gate, grad, gain, entry, mixed, gated, silus
    )
    sums[0] = square
    sums[1] = cross


def back_state_side(side, stats, conv, cols, grad, gain, gated, silus, decs, out):
    length, features = gated.shape
    half = features // LANES // 2
    shape = (length, LANES)
    read = conv[:, features + N : features + 2 * N]
    decay = side_columns(jnp.exp(cols[1]), side, half)
    scale = jnp.broadcast_to(stats[:, 0:1], shape)
    factor = jnp.broadcast_to(stats[:, 1:2], shape)
    for pair in range(half):
        here = side_block(side * half + pair)
        grad_gated = scale * (grad[:, here].astype(F32) * gain[:, here]) - factor * gated[:, here]
        weighted = by_head(decay, pair, shape) * (grad_gated * silus[:, here])
        put_state(out, pair, half, dot(read, weighted.astype(BF16), (0, 0)).astype(BF16))
    out[half * N :, :] = decs[side]


def norm_kernel(
    mixed_in, gated_in, silus_in, local, conv, cols, gate, grad, gain, entry, sums, decs, mixed, gated, silus, stats, other
):
    length, features = local.shape
    side = 1 - here_at()[0]
    square, cross = mix_side(side, local, conv, cols, gate, grad, gain, entry, mixed, gated, silus)
    square = jnp.sum(square + sums[0], axis=1, keepdims=True)
    cross = jnp.sum(cross + sums[1], axis=1, keepdims=True)
    scale = lax.rsqrt(square * (1.0 / features) + EPS)
    factor = scale * scale * scale * cross * (1.0 / features)
    lane = iota((length, LANES), 1)
    values = jnp.where(lane == 0, scale, jnp.where(lane == 1, factor, 0.0))
    stats[...] = values
    back_state_side(side, values, conv, cols, grad, gain, gated, silus, decs, other)


def norm_last_kernel(stats, conv, cols, grad, gain, gated, silus, decs, mine):
    back_state_side(here_at()[0], stats[...], conv, cols, grad, gain, gated, silus, decs, mine)


def gate_kernel(
    mixed, conv, cols, small, gate, grad, gain, stats, own, got, grad_gate, grad_mixed, sums, grad_gain, grad_small, grad_read, entry
):
    core = here_at()[0]
    length, features = mixed.shape
    pairs = features // LANES
    half = pairs // 2
    shape = (length, LANES)
    entry[core] = own[...]
    entry[1 - core] = got[...]
    scale = jnp.broadcast_to(stats[:, 0:1], shape)
    factor = jnp.broadcast_to(stats[:, 1:2], shape)
    decay = jnp.exp(cols[1])
    read_grad = jnp.zeros((length, N), F32)
    out_sums = jnp.zeros(shape, F32)
    skip_sums = jnp.zeros(shape, F32)
    for pair in range(pairs):
        here = block(pair)
        z = gate[:, here].astype(F32)
        sig = sigmoid(z)
        silu = z * sig
        mix = mixed[:, here]
        product = mix * silu
        grads = grad[:, here].astype(F32)
        grad_gain[:, here] = jnp.sum(grads * (product * scale), axis=0, keepdims=True)
        grad_gated = scale * (grads * gain[:, here]) - factor * product
        grad_mix = grad_gated * silu
        grad_mixed[:, here] = grad_mix
        grad_gate[:, here] = (grad_gated * mix * (sig * (1.0 + z * (1.0 - sig)))).astype(BF16)
        values = conv[:, here].astype(F32)
        skip = by_head(small[2:3, :], pair, (1, LANES))
        rounded = grad_mix.astype(BF16).astype(F32)
        out_sums += head_sums(rounded * (mix - skip * values), pair)
        skip_sums += head_sums(grad_mix * values, pair)
        weighted = (by_head(decay, pair, shape) * grad_mix).astype(BF16)
        read_grad += dot(weighted, get_state(entry.at[pair // half], pair, half), (1, 1))
    sums[...] = out_sums
    grad_read[...] = jnp.concatenate([jnp.zeros_like(read_grad), read_grad], axis=1)
    grad_small[...] = jnp.zeros_like(grad_small)
    grad_small[2:3, :] = jnp.sum(skip_sums, axis=0, keepdims=True)


def back_kernel(grad_mixed, conv, cols, rows_ref, small, grad_read, grad_values, sums, grad_vecs):
    length, features = grad_mixed.shape
    pairs = features // LANES
    shape = (length, LANES)
    write = conv[:, features : features + N]
    read = conv[:, features + N : features + 2 * N]
    scores = dot(read, write, (1, 1))
    square = (length, length)
    causal = iota(square, 0) >= iota(square, 1)
    score_grad = jnp.zeros(square, F32)
    in_sums = jnp.zeros(shape, F32)
    first = iota(shape, 1) < P_SIZE
    for pair in range(pairs):
        here = block(pair)
        grad_mix = grad_mixed[:, here]
        values = conv[:, here]
        rounded = grad_mix.astype(BF16)
        scaled = [head_weights(cols, rows_ref, 2 * pair + which, causal, scores) for which in range(2)]
        weight_grad = dot(rounded, apart(values), (1, 1))
        score_grad += weight_grad[:, 0:length] * scaled[0][0] + weight_grad[:, length:] * scaled[1][0]
        both = dot(jnp.concatenate([scaled[0][1], scaled[1][1]], axis=1), rounded, (0, 0))
        value_grad = jnp.where(first, both[0:length], both[length:])
        in_sums += head_sums(values.astype(F32) * value_grad, pair)
        skip = by_head(small[2:3, :], pair, (1, LANES))
        grad_values[:, here] = value_grad + skip * grad_mix
    sums[...] = in_sums
    high, low = split(score_grad)
    read_grad = dot(high, write) + dot(low, write)
    write_grad = dot(high, read, (0, 0)) + dot(low, read, (0, 0))
    grad_vecs[...] = grad_read[...] + jnp.concatenate([write_grad, read_grad], axis=1)


def through_taps(taps, full, slopes, cols, start, count):
    total = full[0:1, cols] * slopes[start + taps - 1 : start + taps - 1 + count, cols]
    for tap in range(1, taps):
        ahead = start + taps - 1 - tap
        total = total + full[tap : tap + 1, cols] * slopes[ahead : ahead + count, cols]
    return total


def through_conv(taps, here, grad_out, rows, slope, slopes, whole):
    length = grad_out.shape[0]
    grad_pre = grad_out.astype(BF16).astype(F32) * slope[:, here]
    slopes[HALO : HALO + length, here] = grad_pre
    start = HALO - (taps - 1)
    for tap in range(taps):
        whole[tap : tap + 1, here] = jnp.sum(
            grad_pre * rows[start + tap : start + tap + length, here], axis=0, keepdims=True
        )
    whole[taps : taps + 1, here] = jnp.sum(grad_pre, axis=0, keepdims=True)


def close_side(taps, side, rows, conv, slope, cols, entry, leave, grad_values, slopes, whole):
    length, features = grad_values.shape
    half = features // LANES // 2
    shape = (length, LANES)
    write = conv[:, features : features + N]
    running = cols[1]
    tail = side_columns(jnp.exp(running[length - 1 : length, :] - running) * cols[0], side, half)
    state_sums = jnp.zeros(shape, F32)
    end_sums = jnp.zeros((8, LANES), F32)
    write_grad = jnp.zeros((length, N), F32)
    for pair in range(half):
        here = side_block(side * half + pair)
        leaving = get_state(leave, pair, half)
        values = conv[:, here].astype(F32)
        tail_wide = by_head(tail, pair, shape)
        state_grad = tail_wide * dot(write, leaving)
        state_sums += head_sums(values * state_grad, pair)
        write_grad += dot((tail_wide * values).astype(BF16), leaving, (1, 1))
        entering = get_state(entry, pair, half).astype(F32)
        overlap = jnp.sum(leaving.astype(F32) * entering, axis=0, keepdims=True)
        end_sums += head_sums(jnp.broadcast_to(overlap, (8, LANES)), pair)
        through_conv(taps, here, grad_values[:, here] + state_grad, rows, slope, slopes, whole)
    back = 2 * half * side
    return pltpu.roll(state_sums, back, 1), pltpu.roll(end_sums, back, 1), write_grad


def close_own_kernel(
    taps, rows, conv, slope, cols, entry, leave, grad_values, slopes, whole, state_out, end_out, write_out
):
    length, channels = conv.shape
    slopes[0:HALO, :] = jnp.zeros((HALO, channels), F32)
    slopes[HALO + length :, :] = jnp.zeros((HALO, channels), F32)
    whole[...] = jnp.zeros_like(whole)
    state_sums, end_sums, write_grad = close_side(
        taps, here_at()[0], rows, conv, slope, cols, entry, leave, grad_values, slopes, whole
    )
    state_out[...] = state_sums
    end_out[...] = end_sums
    write_out[...] = jnp.concatenate([write_grad, jnp.zeros_like(write_grad)], axis=1)


def close_kernel(
    taps, sizes, slopes_in, whole_in, rows, conv, slope, cols, small, entry, leave, grad_values, grad_vecs, out_sums, in_sums,
    grad_gain, grad_small, state_in, end_in, write_in, slopes, whole, grad_dt, *rest
):
    outs, cut = rest[:-1], rest[-1]
    parts = len(outs)
    core, _, position_here = here_at()
    length, channels = conv.shape
    width, gain_width, heads_here = sizes
    heads = heads_here * parts
    step = cols[0]
    last = cols[1, length - 1 : length, :]
    state_sums, end_sums, write_grad = close_side(
        taps, 1 - core, rows, conv, slope, cols, entry, leave, grad_values, slopes, whole
    )
    state_sums = state_sums + state_in[...]
    end_sums = end_sums + end_in[...]
    vecs = grad_vecs[...] + write_in[...]
    vecs = vecs + jnp.concatenate([write_grad, jnp.zeros_like(write_grad)], axis=1)
    through_conv(taps, block(channels // LANES - 1), vecs, rows, slope, slopes, whole)

    into = in_sums[...] + state_sums
    change = out_sums[...] - into
    end_grad = jnp.sum(state_sums, axis=0, keepdims=True) + jnp.exp(last) * end_sums[0:1, :]
    square = (length, length)
    upper = (iota(square, 0) <= iota(square, 1)).astype(F32)
    log_grad = dot(upper, change, precision=HIGH) + end_grad
    rate = jnp.exp(small[1:2, :])
    raw_grad = (into / step - rate * log_grad) * (1.0 - jnp.exp(-step))
    grad_dt[...] = raw_grad.T[0:heads, :]
    vectors = (
        jnp.sum(raw_grad, axis=0, keepdims=True),
        jnp.sum(-rate * step * log_grad, axis=0, keepdims=True),
        grad_small[2:3, :],
    )
    piece_width = cut.shape[2]
    for part in range(parts):
        base, shift = placement(part, width)
        piece = whole[:, base : base + piece_width + LANES]
        if shift:
            piece = pltpu.roll(piece, piece_width + LANES - shift, 1)
        cut[part] = piece[:, 0:piece_width]
        cut[part, taps + 1 : taps + 2, 0:gain_width] = grad_gain[:, part * gain_width : (part + 1) * gain_width]
        for number, vector in enumerate(vectors):
            row = pltpu.roll(vector, LANES - part * heads_here, 1) if part else vector
            cut[part, taps + 2 : taps + 3, block(number)] = row
    for distance in range(parts):
        outs[distance][...] = cut[lax.rem(position_here + distance, parts)]


def input_kernel(taps, full, slopes, grad_x, ending, back):
    length, channels = grad_x.shape
    folded = back.shape[1] // LANES
    back[...] = jnp.zeros_like(back)
    for position in range(channels // LANES):
        here = block(position)
        total = through_taps(taps, full, slopes, here, HALO, length)
        grad_x[:, here] = total.astype(BF16)
        ending[:, here] = total[length - 2 * HALO :]
        ahead = through_taps(taps, full, slopes, here, 0, HALO)
        for tap in range(taps - 1):
            at = tap * FOLDS + position // folded
            back[at : at + 1, block(position % folded)] = ahead[HALO - taps + 1 + tap : HALO - taps + 2 + tap]


def unpack_kernel(terms, chips, taps, grad_in, ending, from_core, from_chip, *refs):
    given, refs = refs[:terms], refs[terms:]
    core, chip, _ = here_at()
    grad_x, cw, cb, dtb, al, sk, gain, late, sem = refs
    rows = late.shape[0]
    channels = ending.shape[1]
    folded = from_core.shape[1] // LANES
    inside = core == 0
    later = jnp.where(inside, from_core[SMALL:, :], from_chip[SMALL:, :])
    later = jnp.where(jnp.logical_or(inside, chip < chips - 1), later, 0.0)
    padding = jnp.zeros((rows - taps + 1, LANES), F32)
    for position in range(channels // LANES):
        here = block(position)
        lines = [
            later[tap * FOLDS + position // folded : tap * FOLDS + position // folded + 1, block(position % folded)]
            for tap in range(taps - 1)
        ]
        late[:, here] = (ending[:, here] + jnp.concatenate([padding] + lines, axis=0)).astype(BF16)
    copy = pltpu.make_async_copy(late, grad_x.at[pl.ds(grad_x.shape[0] - rows, rows)], sem)
    copy.start()
    total = given[0][0:SMALL, :]
    for ref in given[1:]:
        total = total + ref[0:SMALL, :]
    width = cw.shape[1]
    cw[...] = total[0:taps, 0:width]
    cb[...] = total[taps, 0:width]
    gain[...] = total[taps + 1, 0 : gain.shape[0]]
    for number, ref in enumerate((dtb, al, sk)):
        ref[...] = total[taps + 2 : taps + 3, number * LANES : number * LANES + ref.shape[1]]
    copy.wait()


def add_kernel(*refs):
    *terms, back, out = refs
    total = terms[0][...]
    for ref in terms[1:]:
        total = total + ref[...]
    out[0:SMALL, :] = total
    out[SMALL:, :] = back[...]


def add_pair_kernel(own, other, out, alone):
    total = own[0:SMALL, :] + other[0:SMALL, :]
    out[0:SMALL, :] = total
    out[SMALL:, :] = other[SMALL:, :]
    alone[...] = total


def parts_of(message):
    end = message.shape[0] - DEC_ROWS
    return message[0:end, :].astype(F32), unpack_decays(message[end:, :])


def decayed(state, decay, half):
    cuts = state.shape[0] // (half * CUT)
    split_rows = state.reshape(cuts, half, CUT, LANES)
    return (split_rows * decay[0:half].reshape(1, half, 1, LANES)).reshape(state.shape)


def joined(first, second, half):
    state, decay = second
    return decayed(first[0], decay, half) + state, decay * first[1]


def store(out, value):
    state, decay = value
    end = state.shape[0]
    out[0:end, :] = state.astype(BF16)
    out[end:, :] = pack_decays(decay)


def ordered(later, a, b):
    return jnp.where(later, b, a), jnp.where(later, a, b)


def meet_kernel(half, reverse, mine, got, out):
    later = here_at()[0] == (0 if reverse else 1)
    first, second = ordered(later, mine[...], got[...])
    store(out, joined(parts_of(first), parts_of(second), half))


def join_kernel(half, first, second, out):
    store(out, joined(parts_of(first[...]), parts_of(second[...]), half))


def meet_chain_kernel(half, reverse, mine, got, decay_out, *outs):
    later = here_at()[0] == (0 if reverse else 1)
    rows = outs[0].shape[0]
    end = rows * len(outs)
    early, late = ordered(later, mine[end:, :], got[end:, :])
    early, late = unpack_decays(early), unpack_decays(late)
    decay_out[...] = early * late
    for number, out in enumerate(outs):
        here = slice(number * rows, (number + 1) * rows)
        first, second = ordered(later, mine[here, :], got[here, :])
        out[...] = (decayed(first.astype(F32), late, half) + second.astype(F32)).astype(BF16)


def pass_kernel(half, before, own, decay, out):
    state = decayed(before[...].astype(F32), decay[...], half)
    out[...] = (state + own[...].astype(F32)).astype(BF16)


def enter_chain_kernel(half, reverse, streams, *refs):
    given, (mine, got, own, send) = refs[:-4], refs[-4:]
    later = here_at()[0] == (0 if reverse else 1)
    rows = given[0].shape[0]
    end = rows * streams
    decay = unpack_decays(ordered(later, mine[end:, :], got[end:, :])[0])
    for number in range(streams):
        here = slice(number * rows, (number + 1) * rows)
        start = given[number][...].astype(F32)
        for ref in given[streams + number :: streams]:
            start = start + ref[...].astype(F32)
        first = ordered(later, mine[here, :], got[here, :])[0]
        after = decayed(start, decay, half) + first.astype(F32)
        own[here, :] = jnp.where(later, after, start).astype(BF16)
        send[here, :] = jnp.where(later, start, after).astype(BF16)


def enter_kernel(half, reverse, entering, mine, got, own, send):
    later = here_at()[0] == (0 if reverse else 1)
    end = own.shape[0]
    start = entering[0:end, :].astype(F32)
    first = ordered(later, mine[...], got[...])[0]
    state, decay = parts_of(first)
    after = decayed(start, decay, half) + state
    own[...] = jnp.where(later, after, start).astype(BF16)
    send[...] = jnp.where(later, start, after).astype(BF16)


def call(kernel, outs, args, scratch=(), megabytes=8, flops=0, name=None, fetched=(), aliases=None):
    specs = [
        pl.BlockSpec(
            memory_space=pltpu.HBM if number in fetched else pltpu.VMEM
        )
        for number in range(len(args))
    ]
    fetched_out = [out for given, out in (aliases or {}).items() if given in fetched]
    moved = sum(a.size * a.dtype.itemsize for a in args)
    moved += sum(o.size * o.dtype.itemsize for o in outs)
    return pl.pallas_call(
        kernel,
        out_shape=outs,
        in_specs=specs,
        out_specs=[
            pl.BlockSpec(memory_space=pltpu.HBM if number in fetched_out else pltpu.VMEM)
            for number in range(len(outs))
        ],
        input_output_aliases=aliases or {},
        scratch_shapes=list(scratch),
        compiler_params=pltpu.CompilerParams(vmem_limit_bytes=megabytes << 20),
        cost_estimate=pl.CostEstimate(flops=flops, bytes_accessed=moved, transcendentals=0),
        name=name,
    )(*args)


def like(shape, dtype=F32):
    return jax.ShapeDtypeStruct(shape, dtype)


def shift(value, axis, route):
    count = lax.axis_size(axis)
    pairs = [(i, route(i)) for i in range(count)]
    return lax.ppermute(value, axis, [(i, j) for i, j in pairs if 0 <= j < count])


def between_chips(value, routes):
    return shift(value, "seq", lambda i: 2 * routes[i // 2] + i % 2 if i // 2 in routes else -1)


def entering_states(mine, got, half, reverse, beside):
    chips = lax.axis_size("seq") // 2
    entry = like((mine.shape[0] - DEC_ROWS, LANES), BF16)
    if 1 < chips <= 4:
        order = list(range(chips))[::-1] if reverse else list(range(chips))
        stream = like((entry.shape[0] // STREAMS, LANES), BF16)
        decay, *chip = call(
            functools.partial(meet_chain_kernel, half, reverse),
            [like((DEC_ROWS, LANES))] + [stream] * STREAMS,
            [mine, got],
            name="meet",
        )
        arrived = []
        moving = chip
        for hop in range(chips - 1):
            route = {order[hop]: order[hop + 1]}
            landed = [between_chips(part, route) for part in moving]
            if hop < len(beside):
                landed[0] = beside[hop](moving, landed[0])
            arrived += landed
            if hop < chips - 2:
                moving = [
                    call(functools.partial(pass_kernel, half), [stream], [part, own, decay], name="pass")[0]
                    for part, own in zip(landed, chip)
                ]
        own, send = call(
            functools.partial(enter_chain_kernel, half, reverse, STREAMS),
            [entry, entry],
            arrived + [mine, got],
            name="enter",
        )
        return own, shift(send, "seq", lambda i: i ^ 1)
    sign = -1 if reverse else 1
    message = like(mine.shape, BF16)
    chip = call(functools.partial(meet_kernel, half, reverse), [message], [mine, got], name="meet")[0]
    before = shift(chip, "seq", lambda i: i + 2 * sign)
    before = beside[0]([chip], before)
    join = functools.partial(join_kernel, half)
    window = 1
    while window < chips - 1:
        longer = call(join, [message], [before, chip], name="join")[0]
        distance = window + 1
        far = shift(longer, "seq", lambda i: i + 2 * distance * sign)
        before = call(join, [message], [far, before], name="join")[0]
        window = 2 * window + 1
    before = beside[1]([before], before)
    own, send = call(
        functools.partial(enter_kernel, half, reverse),
        [entry, entry],
        [before, mine, got],
        name="enter",
    )
    return own, shift(send, "seq", lambda i: i ^ 1)


def after(value, *signals):
    return lax.optimization_barrier((value, *signals))[0]


def shards(
    conv_input, gate_input, dt_raw, grad_output, conv_weight, conv_bias, dt_bias, a_log, skip, norm_gain
):
    gate, grad = gate_input[0], grad_output[0]
    dt = dt_raw[0].T
    length, channels = conv_input.shape[1:]
    features = gate.shape[1]
    heads = dt.shape[0]
    half = heads // 4
    taps, width = conv_weight.shape
    gain_width = norm_gain.shape[0]
    heads_here = dt_bias.shape[0]
    parts = lax.axis_size("fsdp")
    devices = lax.axis_size("seq")
    sizes = (width, gain_width, heads_here)
    piece_width = -(-width // LANES) * LANES
    full_width = placement(parts - 1, width)[0] + piece_width + LANES
    piece_like = like((SMALL, piece_width))
    shares = [
        conv_weight,
        conv_bias.reshape(1, -1),
        dt_bias.reshape(1, -1),
        a_log.reshape(1, -1),
        skip.reshape(1, -1),
        norm_gain,
    ]

    x = conv_input[0]
    halo, piece, own = call(
        open_kernel,
        [like((HALO, channels), BF16), piece_like, like((2 * SMALL, piece_width))],
        [x, dt] + shares,
        [pltpu.VMEM((2 * HALO, channels), BF16), pltpu.VMEM(dt.shape, F32)]
        + [pltpu.VMEM(share.shape, F32) for share in shares]
        + [pltpu.SemaphoreType.DMA((len(shares) + 2,))],
        fetched=range(len(shares) + 2),
        megabytes=60,
        name="open",
    )
    pieces = [shift(piece, "fsdp", lambda i: (i + distance) % parts) for distance in range(1, parts)]
    halo = shift(halo, "seq", lambda i: i + 1)
    lifted = jnp.pad(after(x, piece).astype(F32), ((HALO, 0), (0, 0)))

    message = like((half * N + DEC_ROWS, LANES), BF16)
    entry = pltpu.VMEM((2, half * N, LANES), BF16)
    full, gain, small, cols, rows, decs = call(
        functools.partial(gather_kernel, taps, sizes, parts, length),
        [
            like((SMALL, full_width)),
            like((1, features)),
            like((8, LANES)),
            like((2, length, LANES)),
            like((3, LANES, length)),
            like((2, DEC_ROWS, LANES), BF16),
        ],
        [own] + pieces,
        [pltpu.VMEM((LANES, LANES), F32), pltpu.VMEM((parts, SMALL, piece_width), F32)],
        name="gather",
    )
    padded, conv, write_t, other = call(
        functools.partial(front_kernel, taps),
        [like(lifted.shape), like((length, channels), BF16), like((N, length)), message],
        [lifted, halo, full, rows, decs],
        name="front",
        aliases={0: 0},
    )
    got = shift(other, "seq", lambda i: i ^ 1)
    conv, mine = call(
        functools.partial(front_own_kernel, taps),
        [like((length, channels), BF16), message],
        [conv, padded, full, rows, decs, write_t],
        name="own",
        aliases={0: 0},
    )
    work = {}

    def intra(signal, value):
        work["local"], work["slope"] = call(
            functools.partial(intra_kernel, taps),
            [like((length, features)), like((length, channels))],
            [padded, full, after(conv, *signal), cols, rows, small],
            flops=2 * length * length * features,
            name="intra",
        )
        return after(value, work["local"])

    def nothing(signal, value):
        return value

    entry_own, entry_got = entering_states(mine, got, half, False, (intra, nothing))
    wide = like((length, features))
    square = like((length, LANES))
    mixed, gated, silus, sums = call(
        norm_own_kernel,
        [wide, wide, wide, like((2, length, LANES))],
        [work["local"], conv, cols, gate, grad, gain, entry_own],
        name="norm_own",
    )
    mixed, gated, silus, stats, other = call(
        norm_kernel,
        [wide, wide, wide, square, message],
        [mixed, gated, silus, work["local"], conv, cols, gate, grad, gain, entry_got, sums, decs],
        name="norm",
        aliases={0: 0, 1: 1, 2: 2},
    )
    got = shift(other, "seq", lambda i: i ^ 1)
    mine = call(
        norm_last_kernel,
        [message],
        [stats, conv, cols, grad, gain, gated, silus, decs],
        name="norm_last",
    )[0]

    def gates(signal, value):
        work["gates"] = call(
            gate_kernel,
            [
                like((length, features), BF16),
                like((length, features)),
                like((length, LANES)),
                like((1, features)),
                like((8, LANES)),
                like((length, LANES)),
            ],
            [mixed, after(conv, *signal), cols, small, gate, grad, gain, stats, entry_own, entry_got],
            [entry],
                flops=2 * length * length * features,
            name="gates",
        )
        return after(value, work["gates"][0])

    def back(signal, value):
        grad_mixed, grad_read = work["gates"][1], work["gates"][5]
        work["back"] = call(
            back_kernel,
            [like((length, features)), like((length, LANES)), like((length, LANES))],
            [after(grad_mixed, *signal), conv, cols, rows, small, grad_read],
            flops=4 * length * length * features,
            name="back",
        )
        return after(value, work["back"][0])

    leave_own, leave_got = entering_states(mine, got, half, True, (gates, back))
    grad_gate, _, out_sums, grad_gain, grad_small, _ = work["gates"]
    grad_values, in_sums, grad_vecs = work["back"]
    slopes, whole, state_sums, end_sums, write_grad = call(
        functools.partial(close_own_kernel, taps),
        [like((2 * HALO + length, channels)), like((SMALL, full_width)), square, like((8, LANES)), square],
        [padded, conv, work["slope"], cols, entry_own, leave_own, grad_values],
        name="close_own",
    )
    slopes, whole, grad_dt, *shares = call(
        functools.partial(close_kernel, taps, sizes),
        [like(slopes.shape), like(whole.shape), like((heads, length))] + [piece_like] * parts,
        [slopes, whole, padded, conv, work["slope"], cols, small, entry_got, leave_got, grad_values, grad_vecs, out_sums]
        + [in_sums, grad_gain, grad_small, state_sums, end_sums, write_grad],
        [pltpu.VMEM((parts, SMALL, piece_width), F32)],
        name="close",
        aliases={0: 0, 1: 1},
    )
    terms = [shares[0]]
    for distance in range(1, parts):
        terms.append(shift(shares[distance], "fsdp", lambda i: (i + distance) % parts))
    grad_x, ending, earlier = call(
        functools.partial(input_kernel, taps),
        [like((length, channels), BF16), like((2 * HALO, channels)), like((BACK_ROWS, piece_width))],
        [full, slopes],
        flops=length * channels * 16,
        name="inputs",
    )
    terms[1] = after(terms[1], ending)
    bundle = like((SMALL + BACK_ROWS, piece_width))
    total = call(add_kernel, [bundle], terms + [earlier], name="add")[0]
    partner = shift(total, "seq", lambda i: i ^ 1)
    total, alone = call(add_pair_kernel, [bundle, piece_like], [total, partner], name="add")
    chips = devices // 2
    behind = between_chips(total, {i: (i - 1) % chips for i in range(chips)})
    if chips <= 4:
        terms = [alone] + [
            between_chips(alone, {i: (i + distance) % chips for i in range(chips)})
            for distance in range(1, chips - 1)
        ]
        terms += [behind] if chips > 1 else []
    else:
        terms = [lax.psum(alone, "seq") * 0.5]
    grad_x, cw, cb, dtb, al, sk, gn = call(
        functools.partial(unpack_kernel, len(terms), chips, taps),
        [
            like((length, channels), BF16),
            like((taps, width)),
            like((width,)),
            like((1, heads_here)),
            like((1, heads_here)),
            like((1, heads_here)),
            like((gain_width,)),
        ],
        [grad_x, ending, partner, behind] + terms,
        [pltpu.VMEM((2 * HALO, channels), BF16), pltpu.SemaphoreType.DMA],
        fetched=(0,),
        aliases={0: 0},
        name="unpack",
    )
    return (
        grad_x[None],
        grad_gate[None],
        grad_dt.T[None],
        cw,
        cb,
        dtb.reshape(-1),
        al.reshape(-1),
        sk.reshape(-1),
        gn,
    )


def solution(mesh):
    tokens = P("fsdp", "seq", None)
    in_specs = (tokens,) * 4 + (P(None, "fsdp"),) + (P("fsdp"),) * 5
    out_specs = (tokens,) * 3 + (P(None, "fsdp"),) + (P("fsdp"),) * 5
    return jax.shard_map(shards, mesh=mesh, in_specs=in_specs, out_specs=out_specs, check_vma=False)
```

```python
import functools

import jax
import jax.numpy as jnp
from jax import lax
from jax.experimental import pallas as pl
from jax.experimental.pallas import tpu as pltpu
from jax.sharding import PartitionSpec as P

P_SIZE = 64
N = 64
EPS = 1e-05
LANES = 2 * P_SIZE
HALO = 8
SMALL = 8
STREAMS = 2
FOLDS = 4
BACK_ROWS = 16
DEC_ROWS = 16
F32, BF16 = jnp.float32, jnp.bfloat16


def dot(a, b, over=(1, 0)):
    return lax.dot_general(
        a, b, (((over[0],), (over[1],)), ((), ())), preferred_element_type=F32
    )


def here_at():
    index = lax.axis_index("seq")
    return lax.rem(index, 2), lax.div(index, 2), lax.axis_index("fsdp")


def iota(shape, axis):
    return lax.broadcasted_iota(jnp.int32, shape, axis)


def sigmoid(x):
    return 0.5 * jnp.tanh(0.5 * x) + 0.5


def split(x):
    high = x.astype(BF16)
    return high, (x - high.astype(F32)).astype(BF16)


def dot_parts(ones, value, parts):
    pieces = []
    for _ in range(parts):
        piece = value.astype(BF16)
        pieces.append(piece)
        value = value - piece.astype(F32)
    ones = ones.astype(BF16)
    return dot(jnp.concatenate([ones] * parts, axis=1), jnp.concatenate(pieces, axis=0))


def block(position):
    return slice(position * LANES, (position + 1) * LANES)


def by_head(columns, pair, shape):
    first = jnp.broadcast_to(columns[:, 2 * pair : 2 * pair + 1], shape)
    second = jnp.broadcast_to(columns[:, 2 * pair + 1 : 2 * pair + 2], shape)
    return jnp.where(iota(shape, 1) < P_SIZE, first, second)


def apart(pair_block):
    first = iota(pair_block.shape, 1) < P_SIZE
    zero = jnp.zeros_like(pair_block)
    return jnp.concatenate(
        [jnp.where(first, pair_block, zero), jnp.where(first, zero, pair_block)], axis=0
    )


def head_sums(product, pair, parts=2):
    shape = (LANES, LANES)
    pick = (iota(shape, 1) == 2 * pair + (iota(shape, 0) >= P_SIZE).astype(jnp.int32)).astype(BF16)
    if parts == 1:
        return dot(product.astype(BF16), pick)
    high, low = split(product)
    return dot(jnp.concatenate([high, low], axis=1), jnp.concatenate([pick, pick], axis=0))


def before_silu(rows, full, cols, taps, length):
    start = HALO - (taps - 1)
    total = full[taps : taps + 1, cols] + full[0:1, cols] * rows[start : start + length, cols]
    for tap in range(1, taps):
        total = total + full[tap : tap + 1, cols] * rows[start + tap : start + tap + length, cols]
    return total


def open_kernel(x, dt, cw, cb, dtb, al, sk, gain, halo, out, own, late, raw, *rest):
    held, sems = rest[:-1], rest[-1]
    ending = x.at[pl.ds(x.shape[0] - late.shape[0], late.shape[0])]
    copies = [
        pltpu.make_async_copy(source, target, sems.at[number])
        for number, (source, target) in enumerate(
            zip((cw, cb, dtb, al, sk, gain, dt, ending), held + (raw, late))
        )
    ]
    for copy in copies:
        copy.start()
    out[...] = jnp.zeros_like(out)
    for copy in copies:
        copy.wait()
    halo[...] = late[...].astype(F32)[HALO:].astype(BF16)
    cw, cb, dtb, al, sk, gain = held
    taps, width = cw.shape
    out[0:taps, 0:width] = cw[...]
    out[taps : taps + 1, 0:width] = cb[...]
    out[taps + 1 : taps + 2, 0 : gain.shape[0]] = gain[...].reshape(1, -1)
    for number, ref in enumerate((dtb, al, sk)):
        out[taps + 2 : taps + 3, number * LANES : number * LANES + ref.shape[1]] = ref[...]
    own[0:SMALL, :] = out[...]
    own[SMALL:, :] = jnp.zeros((SMALL, own.shape[1]), F32)
    for group in range(raw.shape[0] // SMALL):
        own[SMALL:, block(group)] = raw[group * SMALL : (group + 1) * SMALL, :]


def peer(position, distance, parts):
    if parts & (parts - 1) == 0:
        return position ^ distance
    return (position + distance) % parts


def peer_back(position, distance, parts):
    if parts & (parts - 1) == 0:
        return position ^ distance
    return lax.rem(position + parts - distance, parts)


def placement(position, width):
    start = position * width
    base = start // LANES * LANES
    return base, start - base


def put_state(states, pair, value):
    states[pair * N : (pair + 1) * N, :] = value


def get_state(states, pair):
    return states[pair * N : (pair + 1) * N, :]


def pack_decays(decays):
    high, low = split(decays)
    group = iota(decays.shape, 1) // (P_SIZE // 2)
    return jnp.where(lax.rem(group, 2) == 0, high.astype(F32), low.astype(F32)).astype(BF16)


def unpack_decays(packed):
    value = packed.astype(F32)
    group = iota(value.shape, 1) // (P_SIZE // 2)
    ahead = pltpu.roll(value, LANES - P_SIZE // 2, 1)
    behind = pltpu.roll(value, P_SIZE // 2, 1)
    return value + jnp.where(lax.rem(group, 2) == 0, ahead, behind)


def gather_kernel(taps, sizes, parts, length, own, *refs):
    given, refs = refs[: parts - 1], refs[parts - 1 :]
    full, gain, small, cols, rows_out, decs, wide, pieces = refs
    mine_at = here_at()[2]
    piece_width = pieces.shape[2]
    pieces[mine_at] = own[0:SMALL, :]
    for distance in range(1, parts):
        pieces[peer_back(mine_at, distance, parts)] = given[distance - 1][...]
    width, gain_width, heads_here = sizes
    heads = heads_here * parts
    half = heads // 4
    full[...] = jnp.zeros_like(full)
    small[...] = jnp.zeros_like(small)
    wide[...] = jnp.zeros_like(wide)
    for group in range(heads // SMALL):
        wide[group * SMALL : (group + 1) * SMALL, :] = own[SMALL:, block(group)]
    for part in range(parts):
        base, shift = placement(part, width)
        piece = jnp.concatenate([pieces[part], jnp.zeros((SMALL, LANES), F32)], axis=1)
        if shift:
            piece = pltpu.roll(piece, shift, 1)
        full[:, base : base + piece_width + LANES] += piece
        gain[:, part * gain_width : (part + 1) * gain_width] = pieces[
            part, taps + 1 : taps + 2, 0:gain_width
        ]
        for number in range(3):
            row = pieces[part, taps + 2 : taps + 3, block(number)]
            if part:
                row = pltpu.roll(row, part * heads_here, 1)
            small[number : number + 1, :] += row
    raw = wide[...].T + small[0:1, :]
    step = jnp.maximum(raw, 0.0) + jnp.log1p(jnp.exp(-jnp.abs(raw)))
    logs = -jnp.exp(small[1:2, :]) * step
    square = (length, length)
    lower = iota(square, 0) >= iota(square, 1)
    running = dot_parts(lower, logs, 3)
    running_t = running.T
    step_t = step.T
    last = jnp.broadcast_to(running_t[:, length - 1 : length], running_t.shape)
    cols[0] = step
    cols[1] = running
    rows_out[0] = step_t
    rows_out[1] = running_t
    rows_out[2] = jnp.exp(last - running_t) * step_t
    wide[...] = jnp.exp(last)[:, 0:LANES]
    group = half // STREAMS
    first = iota((group, LANES), 1) < P_SIZE
    for number in range(2 * STREAMS):
        even = wide[pl.ds(2 * group * number, group, stride=2), :]
        odd = wide[pl.ds(2 * group * number + 1, group, stride=2), :]
        decays = jnp.where(first, even, odd)
        decs[number] = pack_decays(
            jnp.concatenate([decays, jnp.zeros((DEC_ROWS - group, LANES), F32)], axis=0)
        )


def side_block(pair):
    return pl.ds(pl.multiple_of(pair * LANES, LANES), LANES)


def front_group(taps, number, rows, full, tails, decs, write_t, conv, out):
    length = conv.shape[0]
    group = (out.shape[0] - DEC_ROWS) // N
    scale = tails[2, pl.ds(number * 2 * group, 2 * group), :]
    for pair in range(group):
        here = side_block(number * group + pair)
        pre = before_silu(rows, full, here, taps, length)
        value = (pre * sigmoid(pre)).astype(BF16)
        conv[:, here] = value
        scaled = jnp.concatenate(
            [
                (write_t * scale[2 * pair + which : 2 * pair + which + 1, :]).astype(BF16)
                for which in range(2)
            ],
            axis=1,
        )
        put_state(out, pair, dot(scaled, apart(value)).astype(BF16))
    out[group * N :, :] = decs[number]


def front_kernel(taps, lifted, halo, full, tails, decs, rows, conv, write_out, out):
    length, channels = conv.shape
    rows[0:HALO, :] = halo[...].astype(F32)
    here = block(channels // LANES - 1)
    pre = before_silu(rows, full, here, taps, length)
    vectors = (pre * sigmoid(pre)).astype(BF16)
    conv[:, here] = vectors
    write_t = vectors.astype(F32).T[0:N, :]
    write_out[...] = write_t
    front_group(taps, group_at(False, 0), rows, full, tails, decs, write_t, conv, out)


def group_at(own, stream):
    core = here_at()[0]
    return (core if own else 1 - core) * STREAMS + stream


def front_next_kernel(taps, own, streams, conv_in, rows, full, tails, decs, write_t, conv, *outs):
    for stream, out in zip(streams, outs):
        front_group(taps, group_at(own, stream), rows, full, tails, decs, write_t[...], conv, out)


def head_weights(cols, rows_ref, head, causal, scores):
    gap = cols[1, :, head : head + 1] - rows_ref[1, head : head + 1, :]
    scaled = jnp.exp(jnp.where(causal, gap, -1e30)) * rows_ref[0, head : head + 1, :]
    return scaled, (scaled * scores).astype(BF16)


def factor_kernel(cols, gate, grad, gain, silus, grown, decays):
    length, features = gate.shape
    decay = jnp.exp(cols[1])
    for pair in range(features // LANES):
        here = block(pair)
        z = gate[:, here].astype(F32)
        silus[:, here] = z * sigmoid(z)
        grown[:, here] = grad[:, here].astype(F32) * gain[:, here]
        decays[:, here] = by_head(decay, pair, (length, LANES))


def intra_kernel(taps, rows, full, conv, cols, rows_ref, small, local, slope):
    length, channels = conv.shape
    features = local.shape[1]
    pairs = features // LANES
    write = conv[:, features : features + N]
    read = conv[:, features + N : features + 2 * N]
    scores = dot(read, write, (1, 1))
    square = (length, length)
    causal = iota(square, 0) >= iota(square, 1)
    for pair in range(pairs):
        weights = jnp.concatenate(
            [head_weights(cols, rows_ref, 2 * pair + which, causal, scores)[1] for which in range(2)],
            axis=1,
        )
        values = conv[:, block(pair)]
        skip = by_head(small[2:3, :], pair, (1, LANES))
        here = block(pair)
        local[:, here] = dot(weights, apart(values)) + skip * values.astype(F32)
    for position in range(channels // LANES):
        here = block(position)
        pre = before_silu(rows, full, here, taps, length)
        gate = sigmoid(pre)
        slope[:, here] = gate * (1.0 + pre * (1.0 - gate))


def mix_side(own, local, conv, silus, grown, decays, entries, mixed, gated):
    length, features = local.shape
    shape = (length, LANES)
    read = conv[:, features + N : features + 2 * N]
    square_sum = jnp.zeros(shape, F32)
    cross_sum = jnp.zeros(shape, F32)
    for stream, entry in enumerate(entries):
        number = group_at(own, stream)
        group = entry.shape[0] // N
        for pair in range(group):
            here = side_block(number * group + pair)
            carried = dot(read, get_state(entry, pair))
            mix = local[:, here] + decays[:, here] * carried
            mixed[:, here] = mix
            product = mix * silus[:, here]
            gated[:, here] = product
            square_sum += product * product
            cross_sum += product * grown[:, here]
    return square_sum, cross_sum


def mix_kernel(local, conv, silus, grown, decays, *refs):
    entries, (mixed, gated, sums) = refs[:STREAMS], refs[STREAMS:]
    square, cross = mix_side(True, local, conv, silus, grown, decays, entries, mixed, gated)
    sums[0] = square
    sums[1] = cross


def back_state(number, stats, conv, silus, grown, decays, gated, decs, out):
    length, features = gated.shape
    group = (out.shape[0] - DEC_ROWS) // N
    shape = (length, LANES)
    read = conv[:, features + N : features + 2 * N]
    scale = jnp.broadcast_to(stats[:, 0:1], shape)
    factor = jnp.broadcast_to(stats[:, 1:2], shape)
    for pair in range(group):
        here = side_block(number * group + pair)
        grad_gated = scale * grown[:, here] - factor * gated[:, here]
        weighted = decays[:, here] * (grad_gated * silus[:, here])
        put_state(out, pair, dot(read, weighted.astype(BF16), (0, 0)).astype(BF16))
    out[group * N :, :] = decs[number]


def norm_kernel(mixed_in, gated_in, local, conv, silus, grown, decays, sums, decs, *refs):
    entries, (mixed, gated, stats, out) = refs[:STREAMS], refs[STREAMS:]
    length, features = local.shape
    square, cross = mix_side(False, local, conv, silus, grown, decays, entries, mixed, gated)
    square = jnp.sum(square + sums[0], axis=1, keepdims=True)
    cross = jnp.sum(cross + sums[1], axis=1, keepdims=True)
    scale = lax.rsqrt(square * (1.0 / features) + EPS)
    factor = scale * scale * scale * cross * (1.0 / features)
    lane = iota((length, LANES), 1)
    values = jnp.where(lane == 0, scale, jnp.where(lane == 1, factor, 0.0))
    stats[...] = values
    back_state(group_at(False, 0), values, conv, silus, grown, decays, gated, decs, out)


def norm_next_kernel(own, streams, stats, conv, silus, grown, decays, gated, decs, *outs):
    for stream, out in zip(streams, outs):
        back_state(group_at(own, stream), stats[...], conv, silus, grown, decays, gated, decs, out)


def gate_kernel(
    mixed, conv, cols, small, gate, grad, gain, stats, *refs
):
    given, refs = refs[: 2 * STREAMS], refs[2 * STREAMS :]
    grad_gate, grad_mixed, sums, grad_gain, grad_small, grad_read, entry = refs
    length, features = mixed.shape
    pairs = features // LANES
    group = pairs // (2 * STREAMS)
    shape = (length, LANES)
    for number, ref in enumerate(given):
        entry[group_at(number < STREAMS, number % STREAMS)] = ref[...]
    scale = jnp.broadcast_to(stats[:, 0:1], shape)
    factor = jnp.broadcast_to(stats[:, 1:2], shape)
    decay = jnp.exp(cols[1])
    read_grad = jnp.zeros((length, N), F32)
    out_sums = jnp.zeros(shape, F32)
    skip_sums = jnp.zeros(shape, F32)
    for pair in range(pairs):
        here = block(pair)
        z = gate[:, here].astype(F32)
        sig = sigmoid(z)
        silu = z * sig
        mix = mixed[:, here]
        product = mix * silu
        grads = grad[:, here].astype(F32)
        grad_gain[:, here] = jnp.sum(grads * (product * scale), axis=0, keepdims=True)
        grad_gated = scale * (grads * gain[:, here]) - factor * product
        grad_mix = grad_gated * silu
        grad_mixed[:, here] = grad_mix
        grad_gate[:, here] = (grad_gated * mix * (sig * (1.0 + z * (1.0 - sig)))).astype(BF16)
        values = conv[:, here].astype(F32)
        skip = by_head(small[2:3, :], pair, (1, LANES))
        rounded = grad_mix.astype(BF16).astype(F32)
        out_sums += head_sums(rounded * (mix - skip * values), pair)
        skip_sums += head_sums(grad_mix * values, pair)
        weighted = (by_head(decay, pair, shape) * grad_mix).astype(BF16)
        read_grad += dot(weighted, get_state(entry.at[pair // group], pair % group), (1, 1))
    sums[...] = out_sums
    grad_read[...] = jnp.concatenate([jnp.zeros_like(read_grad), read_grad], axis=1)
    grad_small[...] = jnp.zeros_like(grad_small)
    grad_small[2:3, :] = jnp.sum(skip_sums, axis=0, keepdims=True)


def back_kernel(grad_mixed, conv, cols, rows_ref, small, grad_read, grad_values, sums, grad_vecs):
    length, features = grad_mixed.shape
    pairs = features // LANES
    shape = (length, LANES)
    write = conv[:, features : features + N]
    read = conv[:, features + N : features + 2 * N]
    scores = dot(read, write, (1, 1))
    square = (length, length)
    causal = iota(square, 0) >= iota(square, 1)
    score_grad = jnp.zeros(square, F32)
    in_sums = jnp.zeros(shape, F32)
    first = iota(shape, 1) < P_SIZE
    for pair in range(pairs):
        here = block(pair)
        grad_mix = grad_mixed[:, here]
        values = conv[:, here]
        rounded = grad_mix.astype(BF16)
        scaled = [head_weights(cols, rows_ref, 2 * pair + which, causal, scores) for which in range(2)]
        weight_grad = dot(rounded, apart(values), (1, 1))
        score_grad += weight_grad[:, 0:length] * scaled[0][0] + weight_grad[:, length:] * scaled[1][0]
        both = dot(jnp.concatenate([scaled[0][1], scaled[1][1]], axis=1), rounded, (0, 0))
        value_grad = jnp.where(first, both[0:length], both[length:])
        in_sums += head_sums(values.astype(F32) * value_grad, pair)
        skip = by_head(small[2:3, :], pair, (1, LANES))
        grad_values[:, here] = value_grad + skip * grad_mix
    sums[...] = in_sums
    high, low = split(score_grad)
    read_grad = dot(high, write) + dot(low, write)
    write_grad = dot(high, read, (0, 0)) + dot(low, read, (0, 0))
    grad_vecs[...] = grad_read[...] + jnp.concatenate([write_grad, read_grad], axis=1)


def through_taps(taps, full, slopes, cols, start, count):
    total = full[0:1, cols] * slopes[start + taps - 1 : start + taps - 1 + count, cols]
    for tap in range(1, taps):
        ahead = start + taps - 1 - tap
        total = total + full[tap : tap + 1, cols] * slopes[ahead : ahead + count, cols]
    return total


def through_conv(taps, here, grad_out, rows, slope, slopes, whole):
    length = grad_out.shape[0]
    grad_pre = grad_out.astype(BF16).astype(F32) * slope[:, here]
    slopes[HALO : HALO + length, here] = grad_pre
    start = HALO - (taps - 1)
    for tap in range(taps):
        whole[tap : tap + 1, here] = jnp.sum(
            grad_pre * rows[start + tap : start + tap + length, here], axis=0, keepdims=True
        )
    whole[taps : taps + 1, here] = jnp.sum(grad_pre, axis=0, keepdims=True)


def close_group(taps, number, rows, conv, slope, cols, entry, leave, grad_values, slopes, whole):
    length, features = grad_values.shape
    group = leave.shape[0] // N
    shape = (length, LANES)
    write = conv[:, features : features + N]
    running = cols[1]
    tail = jnp.exp(running[length - 1 : length, :] - running) * cols[0]
    tail = pltpu.roll(tail, lax.rem(LANES - 2 * group * number, LANES), 1)
    state_sums = jnp.zeros(shape, F32)
    end_sums = jnp.zeros((8, LANES), F32)
    write_grad = jnp.zeros((length, N), F32)
    for pair in range(group):
        here = side_block(number * group + pair)
        leaving = get_state(leave, pair)
        values = conv[:, here].astype(F32)
        tail_wide = by_head(tail, pair, shape)
        state_grad = tail_wide * dot(write, leaving)
        state_sums += head_sums(values * state_grad, pair)
        write_grad += dot((tail_wide * values).astype(BF16), leaving, (1, 1))
        entering = get_state(entry, pair).astype(F32)
        overlap = jnp.sum(leaving.astype(F32) * entering, axis=0, keepdims=True)
        end_sums += head_sums(jnp.broadcast_to(overlap, (8, LANES)), pair)
        through_conv(taps, here, grad_values[:, here] + state_grad, rows, slope, slopes, whole)
    back = 2 * group * number
    write_grad = jnp.concatenate([write_grad, jnp.zeros_like(write_grad)], axis=1)
    return pltpu.roll(state_sums, back, 1), pltpu.roll(end_sums, back, 1), write_grad


def close_side(taps, own, rows, conv, slope, cols, entries, leaves, grad_values, slopes, whole):
    totals = None
    for stream, (entry, leave) in enumerate(zip(entries, leaves)):
        sums = close_group(
            taps, group_at(own, stream), rows, conv, slope, cols, entry, leave, grad_values, slopes, whole
        )
        totals = sums if totals is None else [a + b for a, b in zip(totals, sums)]
    return totals


def close_own_kernel(taps, rows, conv, slope, cols, grad_values, *refs):
    given, (slopes, whole, state_out, end_out, write_out) = refs[: 2 * STREAMS], refs[2 * STREAMS :]
    length, channels = conv.shape
    slopes[0:HALO, :] = jnp.zeros((HALO, channels), F32)
    slopes[HALO + length :, :] = jnp.zeros((HALO, channels), F32)
    whole[...] = jnp.zeros_like(whole)
    state_out[...], end_out[...], write_out[...] = close_side(
        taps, True, rows, conv, slope, cols, given[:STREAMS], given[STREAMS:], grad_values, slopes, whole
    )


def close_kernel(
    taps, sizes, slopes_in, whole_in, rows, conv, slope, cols, small, grad_values, grad_vecs, out_sums, in_sums,
    grad_gain, grad_small, state_in, end_in, write_in, *rest
):
    given, (slopes, whole, grad_dt, *outs, cut) = rest[: 2 * STREAMS], rest[2 * STREAMS :]
    parts = len(outs)
    position_here = here_at()[2]
    length, channels = conv.shape
    width, gain_width, heads_here = sizes
    heads = heads_here * parts
    step = cols[0]
    last = cols[1, length - 1 : length, :]
    state_sums, end_sums, write_grad = close_side(
        taps, False, rows, conv, slope, cols, given[:STREAMS], given[STREAMS:], grad_values, slopes, whole
    )
    state_sums = state_sums + state_in[...]
    end_sums = end_sums + end_in[...]
    vecs = grad_vecs[...] + (write_in[...] + write_grad)
    through_conv(taps, block(channels // LANES - 1), vecs, rows, slope, slopes, whole)

    into = in_sums[...] + state_sums
    change = out_sums[...] - into
    end_grad = jnp.sum(state_sums, axis=0, keepdims=True) + jnp.exp(last) * end_sums[0:1, :]
    square = (length, length)
    upper = iota(square, 0) <= iota(square, 1)
    log_grad = dot_parts(upper, change, 3) + end_grad
    rate = jnp.exp(small[1:2, :])
    raw_grad = (into / step - rate * log_grad) * (1.0 - jnp.exp(-step))
    grad_dt[...] = raw_grad.T[0:heads, :]
    vectors = (
        jnp.sum(raw_grad, axis=0, keepdims=True),
        jnp.sum(-rate * step * log_grad, axis=0, keepdims=True),
        grad_small[2:3, :],
    )
    piece_width = cut.shape[2]
    for part in range(parts):
        base, shift = placement(part, width)
        piece = whole[:, base : base + piece_width + LANES]
        if shift:
            piece = pltpu.roll(piece, piece_width + LANES - shift, 1)
        cut[part] = piece[:, 0:piece_width]
        cut[part, taps + 1 : taps + 2, 0:gain_width] = grad_gain[:, part * gain_width : (part + 1) * gain_width]
        for number, vector in enumerate(vectors):
            row = pltpu.roll(vector, LANES - part * heads_here, 1) if part else vector
            cut[part, taps + 2 : taps + 3, block(number)] = row
    for distance in range(parts):
        outs[distance][...] = cut[lax.rem(position_here + distance, parts)]


def input_kernel(taps, full, slopes, grad_x, ending):
    length, channels = grad_x.shape
    for position in range(channels // LANES):
        here = block(position)
        total = through_taps(taps, full, slopes, here, HALO, length)
        grad_x[:, here] = total.astype(BF16)
        ending[:, here] = total[length - 2 * HALO :]


def before_kernel(taps, full, slopes, back):
    channels = slopes.shape[1]
    folded = back.shape[1] // LANES
    back[...] = jnp.zeros_like(back)
    for position in range(channels // LANES):
        here = block(position)
        ahead = through_taps(taps, full, slopes, here, 0, HALO)
        for tap in range(taps - 1):
            at = tap * FOLDS + position // folded
            back[at : at + 1, block(position % folded)] = ahead[HALO - taps + 1 + tap : HALO - taps + 2 + tap]


def unpack_kernel(terms, chips, taps, grad_in, ending, from_core, from_chip, *refs):
    given, refs = refs[:terms], refs[terms:]
    core, chip, _ = here_at()
    grad_x, cw, cb, dtb, al, sk, gain, late, sem = refs
    rows = late.shape[0]
    channels = ending.shape[1]
    folded = from_core.shape[1] // LANES
    inside = core == 0
    later = jnp.where(inside, from_core[SMALL:, :], from_chip[SMALL:, :])
    later = jnp.where(jnp.logical_or(inside, chip < chips - 1), later, 0.0)
    padding = jnp.zeros((rows - taps + 1, LANES), F32)
    for position in range(channels // LANES):
        here = block(position)
        lines = [
            later[tap * FOLDS + position // folded : tap * FOLDS + position // folded + 1, block(position % folded)]
            for tap in range(taps - 1)
        ]
        late[:, here] = (ending[:, here] + jnp.concatenate([padding] + lines, axis=0)).astype(BF16)
    copy = pltpu.make_async_copy(late, grad_x.at[pl.ds(grad_x.shape[0] - rows, rows)], sem)
    copy.start()
    total = given[0][0:SMALL, :]
    for ref in given[1:]:
        total = total + ref[0:SMALL, :]
    width = cw.shape[1]
    cw[...] = total[0:taps, 0:width]
    cb[...] = total[taps, 0:width]
    gain[...] = total[taps + 1, 0 : gain.shape[0]]
    for number, ref in enumerate((dtb, al, sk)):
        ref[...] = total[taps + 2 : taps + 3, number * LANES : number * LANES + ref.shape[1]]
    copy.wait()


def add_kernel(*refs):
    *terms, back, out = refs
    total = terms[0][...]
    for ref in terms[1:]:
        total = total + ref[...]
    out[0:SMALL, :] = total
    out[SMALL:, :] = back[...]


def add_pair_kernel(own, other, out, alone):
    total = own[0:SMALL, :] + other[0:SMALL, :]
    out[0:SMALL, :] = total
    out[SMALL:, :] = other[SMALL:, :]
    alone[...] = total


def parts_of(message):
    end = message.shape[0] - DEC_ROWS
    return message[0:end, :].astype(F32), unpack_decays(message[end:, :])


def decayed(state, decay):
    group = state.shape[0] // N
    split_rows = state.reshape(group, N, LANES)
    return (split_rows * decay[0:group].reshape(group, 1, LANES)).reshape(state.shape)


def joined(first, second):
    state, decay = second
    return decayed(first[0], decay) + state, decay * first[1]


def store(out, value):
    state, decay = value
    end = state.shape[0]
    out[0:end, :] = state.astype(BF16)
    out[end:, :] = pack_decays(decay)


def ordered(later, a, b):
    return jnp.where(later, b, a), jnp.where(later, a, b)


def meet_kernel(reverse, mine, got, out, decay):
    later = here_at()[0] == (0 if reverse else 1)
    first, second = ordered(later, mine[...], got[...])
    whole = joined(parts_of(first), parts_of(second))
    store(out, whole)
    decay[...] = whole[1]


def join_kernel(first, second, out):
    store(out, joined(parts_of(first[...]), parts_of(second[...])))


def pass_kernel(before, own, decay, out):
    end = out.shape[0]
    state = decayed(before[0:end, :].astype(F32), decay[...])
    out[...] = (state + own[0:end, :].astype(F32)).astype(BF16)


def enter_kernel(reverse, *refs):
    given, (mine, got, own, send) = refs[:-4], refs[-4:]
    later = here_at()[0] == (0 if reverse else 1)
    end = own.shape[0]
    start = given[0][0:end, :].astype(F32)
    for ref in given[1:]:
        start = start + ref[0:end, :].astype(F32)
    state, decay = parts_of(ordered(later, mine[...], got[...])[0])
    after = decayed(start, decay) + state
    own[...] = jnp.where(later, after, start).astype(BF16)
    send[...] = jnp.where(later, start, after).astype(BF16)


def call(kernel, outs, args, scratch=(), megabytes=8, flops=0, name=None, fetched=(), aliases=None):
    specs = [
        pl.BlockSpec(
            memory_space=pltpu.HBM if number in fetched else pltpu.VMEM
        )
        for number in range(len(args))
    ]
    fetched_out = [out for given, out in (aliases or {}).items() if given in fetched]
    moved = sum(a.size * a.dtype.itemsize for a in args)
    moved += sum(o.size * o.dtype.itemsize for o in outs)
    return pl.pallas_call(
        kernel,
        out_shape=outs,
        in_specs=specs,
        out_specs=[
            pl.BlockSpec(memory_space=pltpu.HBM if number in fetched_out else pltpu.VMEM)
            for number in range(len(outs))
        ],
        input_output_aliases=aliases or {},
        scratch_shapes=list(scratch),
        compiler_params=pltpu.CompilerParams(vmem_limit_bytes=megabytes << 20),
        cost_estimate=pl.CostEstimate(flops=flops, bytes_accessed=moved, transcendentals=0),
        name=name,
    )(*args)


def like(shape, dtype=F32):
    return jax.ShapeDtypeStruct(shape, dtype)


def shift(value, axis, route):
    count = lax.axis_size(axis)
    pairs = [(i, route(i)) for i in range(count)]
    return lax.ppermute(value, axis, [(i, j) for i, j in pairs if 0 <= j < count])


def between_chips(value, routes):
    return shift(value, "seq", lambda i: 2 * routes[i // 2] + i % 2 if i // 2 in routes else -1)


def entering_states(own_states, got, reverse, beside):
    chips = lax.axis_size("seq") // 2
    message = like(got[0].shape, BF16)
    entry = like((got[0].shape[0] - DEC_ROWS, LANES), BF16)
    chip, decays, mine = [], [], []
    for stream, other in enumerate(got):
        mine.append(own_states(stream, chip))
        whole, decay = call(
            functools.partial(meet_kernel, reverse),
            [message, like((DEC_ROWS, LANES))],
            [mine[-1], other],
            name="meet",
        )
        chip.append(whole)
        decays.append(decay)
    if 1 < chips <= 4:
        order = list(range(chips))[::-1] if reverse else list(range(chips))
        arrived = [[] for _ in chip]
        moving = chip
        for hop in range(chips - 1):
            route = {order[hop]: order[hop + 1]}
            landed = [between_chips(part, route) for part in moving]
            if hop < len(beside):
                landed = beside[hop](moving, landed)
            for stream, part in zip(arrived, landed):
                stream.append(part)
            if hop < chips - 2:
                moving = [
                    call(pass_kernel, [entry], list(parts), name="pass")[0] for parts in zip(landed, chip, decays)
                ]
    else:
        sign = -1 if reverse else 1
        before = [shift(part, "seq", lambda i: i + 2 * sign) for part in chip]
        before = beside[1](chip, beside[0](chip, before))
        window = 1
        while window < chips - 1:
            distance = window + 1
            longer = [call(join_kernel, [message], pair, name="join")[0] for pair in zip(before, chip)]
            far = [shift(part, "seq", lambda i: i + 2 * distance * sign) for part in longer]
            before = [call(join_kernel, [message], pair, name="join")[0] for pair in zip(far, before)]
            window = 2 * window + 1
        arrived = [[part] for part in before]
    owns, others = [], []
    for parts, a, b in zip(arrived, mine, got):
        own, send = call(functools.partial(enter_kernel, reverse), [entry, entry], parts + [a, b], name="enter")
        owns.append(own)
        others.append(shift(send, "seq", lambda i: i ^ 1))
    return owns, others


def after(value, *signals):
    return lax.optimization_barrier((value, *signals))[0]


def shards(
    conv_input, gate_input, dt_raw, grad_output, conv_weight, conv_bias, dt_bias, a_log, skip, norm_gain
):
    gate, grad = gate_input[0], grad_output[0]
    dt = dt_raw[0].T
    length, channels = conv_input.shape[1:]
    features = gate.shape[1]
    heads = dt.shape[0]
    half = heads // 4
    taps, width = conv_weight.shape
    gain_width = norm_gain.shape[0]
    heads_here = dt_bias.shape[0]
    parts = lax.axis_size("fsdp")
    devices = lax.axis_size("seq")
    sizes = (width, gain_width, heads_here)
    piece_width = -(-width // LANES) * LANES
    full_width = placement(parts - 1, width)[0] + piece_width + LANES
    piece_like = like((SMALL, piece_width))
    shares = [
        conv_weight,
        conv_bias.reshape(1, -1),
        dt_bias.reshape(1, -1),
        a_log.reshape(1, -1),
        skip.reshape(1, -1),
        norm_gain,
    ]

    x = conv_input[0]
    halo, piece, own = call(
        open_kernel,
        [like((HALO, channels), BF16), piece_like, like((2 * SMALL, piece_width))],
        [x, dt] + shares,
        [pltpu.VMEM((2 * HALO, channels), BF16), pltpu.VMEM(dt.shape, F32)]
        + [pltpu.VMEM(share.shape, F32) for share in shares]
        + [pltpu.SemaphoreType.DMA((len(shares) + 2,))],
        fetched=range(len(shares) + 2),
        megabytes=60,
        name="open",
    )
    pieces = [shift(piece, "fsdp", lambda i: peer(i, distance, parts)) for distance in range(1, parts)]
    halo = shift(halo, "seq", lambda i: i + 1)
    lifted = jnp.pad(after(x, piece).astype(F32), ((HALO, 0), (0, 0)))

    group = half // STREAMS
    message = like((group * N + DEC_ROWS, LANES), BF16)
    entry = pltpu.VMEM((2 * STREAMS, group * N, LANES), BF16)
    wide = like((length, features))
    square = like((length, LANES))
    full, gain, small, cols, rows, decs = call(
        functools.partial(gather_kernel, taps, sizes, parts, length),
        [
            like((SMALL, full_width)),
            like((1, features)),
            like((8, LANES)),
            like((2, length, LANES)),
            like((3, LANES, length)),
            like((2 * STREAMS, DEC_ROWS, LANES), BF16),
        ],
        [own] + pieces,
        [pltpu.VMEM((LANES, LANES), F32), pltpu.VMEM((parts, SMALL, piece_width), F32)],
        name="gather",
    )
    conv_like = like((length, channels), BF16)
    padded, conv, write_t, other = call(
        functools.partial(front_kernel, taps),
        [like(lifted.shape), conv_like, like((N, length)), message],
        [lifted, halo, full, rows, decs],
        name="front",
        aliases={0: 0},
    )
    got = [shift(other, "seq", lambda i: i ^ 1)]
    for stream in range(1, STREAMS):
        conv, other = call(
            functools.partial(front_next_kernel, taps, False, (stream,)),
            [conv_like, message],
            [conv, padded, full, rows, decs, write_t],
            name="front",
            aliases={0: 0},
        )
        got.append(shift(other, "seq", lambda i: i ^ 1))
    held = [conv]

    def own_first(stream, signals):
        held[0], mine = call(
            functools.partial(front_next_kernel, taps, True, (stream,)),
            [conv_like, message],
            [after(held[0], *signals), padded, full, rows, decs, write_t],
            name="own",
            aliases={0: 0},
        )
        return mine

    work = {}

    def intra(signal, value):
        work["local"], work["slope"] = call(
            functools.partial(intra_kernel, taps),
            [wide, like((length, channels))],
            [padded, full, after(held[0], *signal), cols, rows, small],
            flops=2 * length * length * features,
            name="intra",
        )
        return [after(part, work["local"]) for part in value]

    def factors(signal, value):
        work["factors"] = call(
            factor_kernel,
            [wide] * 3,
            [after(cols, *signal), gate, grad, gain],
            flops=length * features * 16,
            name="factors",
        )
        return [after(part, work["factors"][0]) for part in value]

    sums_like = like((2, length, LANES))

    entry_own, entry_got = entering_states(own_first, got, False, (intra, factors))
    conv = held[0]
    silus, grown, decays = work["factors"]
    given = [work["local"], conv, silus, grown, decays]
    mixed, gated, sums = call(mix_kernel, [wide, wide, sums_like], given + entry_own, name="mix")
    mixed, gated, stats, other = call(
        norm_kernel,
        [wide, wide, square, message],
        [mixed, gated] + given + [sums, decs] + entry_got,
        name="norm",
        aliases={0: 0, 1: 1},
    )
    got = [shift(other, "seq", lambda i: i ^ 1)]
    given = [conv, silus, grown, decays, gated, decs]

    def norm_next(own, stream, signals):
        return call(
            functools.partial(norm_next_kernel, own, (stream,)),
            [message],
            [after(stats, *signals)] + given,
            name="norm_next",
        )[0]

    for stream in range(1, STREAMS):
        got.append(shift(norm_next(False, stream, []), "seq", lambda i: i ^ 1))

    def gates(signal, value):
        work["gates"] = call(
            gate_kernel,
            [
                like((length, features), BF16),
                like((length, features)),
                like((length, LANES)),
                like((1, features)),
                like((8, LANES)),
                like((length, LANES)),
            ],
            [mixed, after(conv, *signal), cols, small, gate, grad, gain, stats] + entry_own + entry_got,
            [entry],
                flops=2 * length * length * features,
            name="gates",
        )
        return [after(part, work["gates"][0]) for part in value]

    def back(signal, value):
        grad_mixed, grad_read = work["gates"][1], work["gates"][5]
        work["back"] = call(
            back_kernel,
            [like((length, features)), like((length, LANES)), like((length, LANES))],
            [after(grad_mixed, *signal), conv, cols, rows, small, grad_read],
            flops=4 * length * length * features,
            name="back",
        )
        return [after(part, work["back"][0]) for part in value]

    shapes = [like((2 * HALO + length, channels)), like((SMALL, full_width)), square, like((8, LANES)), square]
    fixed = [padded, conv, work["slope"], cols]

    leave_own, leave_got = entering_states(functools.partial(norm_next, True), got, True, (gates, back))
    grad_gate, _, out_sums, grad_gain, grad_small, _ = work["gates"]
    grad_values, in_sums, grad_vecs = work["back"]
    slopes, whole, *sums = call(
        functools.partial(close_own_kernel, taps),
        shapes,
        fixed + [grad_values] + entry_own + leave_own,
        name="close_own",
    )
    slopes, whole, grad_dt, *shares = call(
        functools.partial(close_kernel, taps, sizes),
        shapes[:2] + [like((heads, length))] + [piece_like] * parts,
        [slopes, whole] + fixed + [small, grad_values, grad_vecs, out_sums, in_sums, grad_gain, grad_small]
        + sums + entry_got + leave_got,
        [pltpu.VMEM((parts, SMALL, piece_width), F32)],
        name="close",
        aliases={0: 0, 1: 1},
    )
    terms = [shares[0]]
    for distance in range(1, parts):
        terms.append(shift(shares[distance], "fsdp", lambda i: (i + distance) % parts))
    earlier = call(
        functools.partial(before_kernel, taps), [like((BACK_ROWS, piece_width))], [full, slopes], name="before"
    )[0]
    bundle = like((SMALL + BACK_ROWS, piece_width))
    total = call(add_kernel, [bundle], terms + [earlier], name="add")[0]
    partner = shift(total, "seq", lambda i: i ^ 1)
    total, alone = call(add_pair_kernel, [bundle, piece_like], [total, partner], name="add")
    chips = devices // 2
    behind = between_chips(total, {i: (i - 1) % chips for i in range(chips)})
    if chips <= 4:
        terms = [alone] + [
            between_chips(alone, {i: (i + distance) % chips for i in range(chips)})
            for distance in range(1, chips - 1)
        ]
        terms += [behind] if chips > 1 else []
    else:
        terms = [lax.psum(alone, "seq") * 0.5]
    grad_x, ending = call(
        functools.partial(input_kernel, taps),
        [like((length, channels), BF16), like((2 * HALO, channels))],
        [full, after(slopes, alone)],
        flops=length * channels * 16,
        name="inputs",
    )
    grad_x, cw, cb, dtb, al, sk, gn = call(
        functools.partial(unpack_kernel, len(terms), chips, taps),
        [
            like((length, channels), BF16),
            like((taps, width)),
            like((width,)),
            like((1, heads_here)),
            like((1, heads_here)),
            like((1, heads_here)),
            like((gain_width,)),
        ],
        [grad_x, ending, partner, behind] + terms,
        [pltpu.VMEM((2 * HALO, channels), BF16), pltpu.SemaphoreType.DMA],
        fetched=(0,),
        aliases={0: 0},
        name="unpack",
    )
    return (
        grad_x[None],
        grad_gate[None],
        grad_dt.T[None],
        cw,
        cb,
        dtb.reshape(-1),
        al.reshape(-1),
        sk.reshape(-1),
        gn,
    )


def solution(mesh):
    tokens = P("fsdp", "seq", None)
    in_specs = (tokens,) * 4 + (P(None, "fsdp"),) + (P("fsdp"),) * 5
    out_specs = (tokens,) * 3 + (P(None, "fsdp"),) + (P("fsdp"),) * 5
    return jax.shard_map(shards, mesh=mesh, in_specs=in_specs, out_specs=out_specs, check_vma=False)
```

```python
import functools

import jax
import jax.numpy as jnp
from jax import lax
from jax.experimental import pallas as pl
from jax.experimental.pallas import tpu as pltpu
from jax.sharding import PartitionSpec as P

P_SIZE = 64
N = 64
EPS = 1e-05
LANES = 2 * P_SIZE
HALO = 8
SMALL = 8
STREAMS = 2
FOLDS = 4
BACK_ROWS = 16
DEC_ROWS = 16
F32, BF16 = jnp.float32, jnp.bfloat16


def dot(a, b, over=(1, 0)):
    return lax.dot_general(
        a, b, (((over[0],), (over[1],)), ((), ())), preferred_element_type=F32
    )


def here_at():
    index = lax.axis_index("seq")
    return lax.rem(index, 2), lax.div(index, 2), lax.axis_index("fsdp")


def iota(shape, axis):
    return lax.broadcasted_iota(jnp.int32, shape, axis)


def sigmoid(x):
    return 0.5 * jnp.tanh(0.5 * x) + 0.5


def split(x):
    high = x.astype(BF16)
    return high, (x - high.astype(F32)).astype(BF16)


def dot_parts(ones, value, parts):
    pieces = []
    for _ in range(parts):
        piece = value.astype(BF16)
        pieces.append(piece)
        value = value - piece.astype(F32)
    ones = ones.astype(BF16)
    return dot(jnp.concatenate([ones] * parts, axis=1), jnp.concatenate(pieces, axis=0))


def block(position):
    return slice(position * LANES, (position + 1) * LANES)


def by_head(columns, pair, shape):
    first = jnp.broadcast_to(columns[:, 2 * pair : 2 * pair + 1], shape)
    second = jnp.broadcast_to(columns[:, 2 * pair + 1 : 2 * pair + 2], shape)
    return jnp.where(iota(shape, 1) < P_SIZE, first, second)


def apart(pair_block):
    first = iota(pair_block.shape, 1) < P_SIZE
    zero = jnp.zeros_like(pair_block)
    return jnp.concatenate(
        [jnp.where(first, pair_block, zero), jnp.where(first, zero, pair_block)], axis=0
    )


def head_sums(product, pair, parts=2):
    shape = (LANES, LANES)
    pick = (iota(shape, 1) == 2 * pair + (iota(shape, 0) >= P_SIZE).astype(jnp.int32)).astype(BF16)
    if parts == 1:
        return dot(product.astype(BF16), pick)
    high, low = split(product)
    return dot(jnp.concatenate([high, low], axis=1), jnp.concatenate([pick, pick], axis=0))


def before_silu(rows, full, cols, taps, length):
    start = HALO - (taps - 1)
    total = full[taps : taps + 1, cols] + full[0:1, cols] * rows[start : start + length, cols]
    for tap in range(1, taps):
        total = total + full[tap : tap + 1, cols] * rows[start + tap : start + tap + length, cols]
    return total


def open_kernel(x, dt, cw, cb, dtb, al, sk, gain, halo, out, own, late, raw, *rest):
    held, sems = rest[:-1], rest[-1]
    ending = x.at[pl.ds(x.shape[0] - late.shape[0], late.shape[0])]
    copies = [
        pltpu.make_async_copy(source, target, sems.at[number])
        for number, (source, target) in enumerate(
            zip((cw, cb, dtb, al, sk, gain, dt, ending), held + (raw, late))
        )
    ]
    for copy in copies:
        copy.start()
    out[...] = jnp.zeros_like(out)
    for copy in copies:
        copy.wait()
    halo[...] = late[...].astype(F32)[HALO:].astype(BF16)
    cw, cb, dtb, al, sk, gain = held
    taps, width = cw.shape
    out[0:taps, 0:width] = cw[...]
    out[taps : taps + 1, 0:width] = cb[...]
    out[taps + 1 : taps + 2, 0 : gain.shape[0]] = gain[...].reshape(1, -1)
    for number, ref in enumerate((dtb, al, sk)):
        out[taps + 2 : taps + 3, number * LANES : number * LANES + ref.shape[1]] = ref[...]
    own[0:SMALL, :] = out[...]
    own[SMALL:, :] = jnp.zeros((SMALL, own.shape[1]), F32)
    for group in range(raw.shape[0] // SMALL):
        own[SMALL:, block(group)] = raw[group * SMALL : (group + 1) * SMALL, :]


def peer(position, distance, parts):
    if parts & (parts - 1) == 0:
        return position ^ distance
    return (position + distance) % parts


def peer_back(position, distance, parts):
    if parts & (parts - 1) == 0:
        return position ^ distance
    return lax.rem(position + parts - distance, parts)


def placement(position, width):
    start = position * width
    base = start // LANES * LANES
    return base, start - base


def put_state(states, pair, value):
    states[pair * N : (pair + 1) * N, :] = value


def get_state(states, pair):
    return states[pair * N : (pair + 1) * N, :]


def pack_decays(decays):
    high, low = split(decays)
    group = iota(decays.shape, 1) // (P_SIZE // 2)
    return jnp.where(lax.rem(group, 2) == 0, high.astype(F32), low.astype(F32)).astype(BF16)


def unpack_decays(packed):
    value = packed.astype(F32)
    group = iota(value.shape, 1) // (P_SIZE // 2)
    ahead = pltpu.roll(value, LANES - P_SIZE // 2, 1)
    behind = pltpu.roll(value, P_SIZE // 2, 1)
    return value + jnp.where(lax.rem(group, 2) == 0, ahead, behind)


def gather_kernel(taps, sizes, parts, length, own, *refs):
    given, refs = refs[: parts - 1], refs[parts - 1 :]
    full, gain, small, cols, rows_out, decs, wide, pieces = refs
    mine_at = here_at()[2]
    piece_width = pieces.shape[2]
    pieces[mine_at] = own[0:SMALL, :]
    for distance in range(1, parts):
        pieces[peer_back(mine_at, distance, parts)] = given[distance - 1][...]
    width, gain_width, heads_here = sizes
    heads = heads_here * parts
    half = heads // 4
    full[...] = jnp.zeros_like(full)
    small[...] = jnp.zeros_like(small)
    wide[...] = jnp.zeros_like(wide)
    for group in range(heads // SMALL):
        wide[group * SMALL : (group + 1) * SMALL, :] = own[SMALL:, block(group)]
    for part in range(parts):
        base, shift = placement(part, width)
        piece = jnp.concatenate([pieces[part], jnp.zeros((SMALL, LANES), F32)], axis=1)
        if shift:
            piece = pltpu.roll(piece, shift, 1)
        full[:, base : base + piece_width + LANES] += piece
        gain[:, part * gain_width : (part + 1) * gain_width] = pieces[
            part, taps + 1 : taps + 2, 0:gain_width
        ]
        for number in range(3):
            row = pieces[part, taps + 2 : taps + 3, block(number)]
            if part:
                row = pltpu.roll(row, part * heads_here, 1)
            small[number : number + 1, :] += row
    raw = wide[...].T + small[0:1, :]
    step = jnp.maximum(raw, 0.0) + jnp.log1p(jnp.exp(-jnp.abs(raw)))
    logs = -jnp.exp(small[1:2, :]) * step
    square = (length, length)
    lower = iota(square, 0) >= iota(square, 1)
    running = dot_parts(lower, logs, 3)
    running_t = running.T
    step_t = step.T
    last = jnp.broadcast_to(running_t[:, length - 1 : length], running_t.shape)
    cols[0] = step
    cols[1] = running
    rows_out[0] = step_t
    rows_out[1] = running_t
    rows_out[2] = jnp.exp(last - running_t) * step_t
    wide[...] = jnp.exp(last)[:, 0:LANES]
    group = half // STREAMS
    first = iota((group, LANES), 1) < P_SIZE
    for number in range(2 * STREAMS):
        even = wide[pl.ds(2 * group * number, group, stride=2), :]
        odd = wide[pl.ds(2 * group * number + 1, group, stride=2), :]
        decays = jnp.where(first, even, odd)
        decs[number] = pack_decays(
            jnp.concatenate([decays, jnp.zeros((DEC_ROWS - group, LANES), F32)], axis=0)
        )


def side_block(pair):
    return pl.ds(pl.multiple_of(pair * LANES, LANES), LANES)


def front_group(taps, number, rows, full, tails, decs, write_t, conv, out):
    length = conv.shape[0]
    group = (out.shape[0] - DEC_ROWS) // N
    scale = tails[2, pl.ds(number * 2 * group, 2 * group), :]
    for pair in range(group):
        here = side_block(number * group + pair)
        pre = before_silu(rows, full, here, taps, length)
        value = (pre * sigmoid(pre)).astype(BF16)
        conv[:, here] = value
        scaled = jnp.concatenate(
            [
                (write_t * scale[2 * pair + which : 2 * pair + which + 1, :]).astype(BF16)
                for which in range(2)
            ],
            axis=1,
        )
        put_state(out, pair, dot(scaled, apart(value)).astype(BF16))
    out[group * N :, :] = decs[number]


def front_kernel(taps, lifted, halo, full, tails, decs, rows, conv, write_out, out):
    length, channels = conv.shape
    rows[0:HALO, :] = halo[...].astype(F32)
    here = block(channels // LANES - 1)
    pre = before_silu(rows, full, here, taps, length)
    vectors = (pre * sigmoid(pre)).astype(BF16)
    conv[:, here] = vectors
    write_t = vectors.astype(F32).T[0:N, :]
    write_out[...] = write_t
    front_group(taps, group_at(False, 0), rows, full, tails, decs, write_t, conv, out)


def group_at(own, stream):
    core = here_at()[0]
    return (core if own else 1 - core) * STREAMS + stream


def front_next_kernel(taps, own, streams, conv_in, rows, full, tails, decs, write_t, conv, *outs):
    for stream, out in zip(streams, outs):
        front_group(taps, group_at(own, stream), rows, full, tails, decs, write_t[...], conv, out)


def head_weights(cols, rows_ref, head, causal, scores):
    gap = cols[1, :, head : head + 1] - rows_ref[1, head : head + 1, :]
    scaled = jnp.exp(jnp.where(causal, gap, -1e30)) * rows_ref[0, head : head + 1, :]
    return scaled, (scaled * scores).astype(BF16)


def factor_kernel(cols, gate, grad, gain, rows, silus, grown, decays, picks, shifted):
    length, features = gate.shape
    taps = shifted.shape[0] + 1
    for tap in range(taps - 1):
        start = HALO - taps + 1 + tap
        shifted[tap] = rows[start : start + length, :]
    decay = jnp.exp(cols[1])
    picks[...] = (iota(picks.shape, 1) == iota(picks.shape, 0) // P_SIZE).astype(BF16)
    for pair in range(features // LANES):
        here = block(pair)
        z = gate[:, here].astype(F32)
        silus[:, here] = z * sigmoid(z)
        grown[:, here] = grad[:, here].astype(F32) * gain[:, here]
        decays[:, here] = by_head(decay, pair, (length, LANES))


def intra_kernel(taps, rows, full, conv, cols, rows_ref, small, local, slope):
    length, channels = conv.shape
    features = local.shape[1]
    pairs = features // LANES
    write = conv[:, features : features + N]
    read = conv[:, features + N : features + 2 * N]
    scores = dot(read, write, (1, 1))
    square = (length, length)
    causal = iota(square, 0) >= iota(square, 1)
    for pair in range(pairs):
        weights = jnp.concatenate(
            [head_weights(cols, rows_ref, 2 * pair + which, causal, scores)[1] for which in range(2)],
            axis=1,
        )
        values = conv[:, block(pair)]
        skip = by_head(small[2:3, :], pair, (1, LANES))
        here = block(pair)
        local[:, here] = dot(weights, apart(values)) + skip * values.astype(F32)
    for position in range(channels // LANES):
        here = block(position)
        pre = before_silu(rows, full, here, taps, length)
        gate = sigmoid(pre)
        slope[:, here] = gate * (1.0 + pre * (1.0 - gate))


def mix_side(own, local, conv, silus, grown, decays, entries, mixed, gated):
    length, features = local.shape
    shape = (length, LANES)
    read = conv[:, features + N : features + 2 * N]
    square_sum = jnp.zeros(shape, F32)
    cross_sum = jnp.zeros(shape, F32)
    for stream, entry in enumerate(entries):
        number = group_at(own, stream)
        group = entry.shape[0] // N
        for pair in range(group):
            here = side_block(number * group + pair)
            carried = dot(read, get_state(entry, pair))
            mix = local[:, here] + decays[:, here] * carried
            mixed[:, here] = mix
            product = mix * silus[:, here]
            gated[:, here] = product
            square_sum += product * product
            cross_sum += product * grown[:, here]
    return square_sum, cross_sum


def mix_kernel(local, conv, silus, grown, decays, *refs):
    entries, (mixed, gated, sums) = refs[:STREAMS], refs[STREAMS:]
    square, cross = mix_side(True, local, conv, silus, grown, decays, entries, mixed, gated)
    sums[0] = square
    sums[1] = cross


def back_state(number, stats, conv, silus, grown, decays, gated, decs, out):
    length, features = gated.shape
    group = (out.shape[0] - DEC_ROWS) // N
    shape = (length, LANES)
    read = conv[:, features + N : features + 2 * N]
    scale = jnp.broadcast_to(stats[:, 0:1], shape)
    factor = jnp.broadcast_to(stats[:, 1:2], shape)
    for pair in range(group):
        here = side_block(number * group + pair)
        grad_gated = scale * grown[:, here] - factor * gated[:, here]
        weighted = decays[:, here] * (grad_gated * silus[:, here])
        put_state(out, pair, dot(read, weighted.astype(BF16), (0, 0)).astype(BF16))
    out[group * N :, :] = decs[number]


def norm_kernel(mixed_in, gated_in, local, conv, silus, grown, decays, sums, decs, *refs):
    entries, (mixed, gated, stats, out) = refs[:STREAMS], refs[STREAMS:]
    length, features = local.shape
    square, cross = mix_side(False, local, conv, silus, grown, decays, entries, mixed, gated)
    square = jnp.sum(square + sums[0], axis=1, keepdims=True)
    cross = jnp.sum(cross + sums[1], axis=1, keepdims=True)
    scale = lax.rsqrt(square * (1.0 / features) + EPS)
    factor = scale * scale * scale * cross * (1.0 / features)
    lane = iota((length, LANES), 1)
    values = jnp.where(lane == 0, scale, jnp.where(lane == 1, factor, 0.0))
    stats[...] = values
    back_state(group_at(False, 0), values, conv, silus, grown, decays, gated, decs, out)


def norm_next_kernel(own, streams, stats, conv, silus, grown, decays, gated, decs, *outs):
    for stream, out in zip(streams, outs):
        back_state(group_at(own, stream), stats[...], conv, silus, grown, decays, gated, decs, out)


def gate_kernel(
    mixed, conv, cols, small, gate, grad, gain, stats, *refs
):
    given, refs = refs[: 2 * STREAMS], refs[2 * STREAMS :]
    grad_gate, grad_mixed, sums, grad_gain, grad_small, grad_read, entry = refs
    length, features = mixed.shape
    pairs = features // LANES
    group = pairs // (2 * STREAMS)
    shape = (length, LANES)
    for number, ref in enumerate(given):
        entry[group_at(number < STREAMS, number % STREAMS)] = ref[...]
    scale = jnp.broadcast_to(stats[:, 0:1], shape)
    factor = jnp.broadcast_to(stats[:, 1:2], shape)
    decay = jnp.exp(cols[1])
    read_grad = jnp.zeros((length, N), F32)
    out_sums = jnp.zeros(shape, F32)
    skip_sums = jnp.zeros(shape, F32)
    for pair in range(pairs):
        here = block(pair)
        z = gate[:, here].astype(F32)
        sig = sigmoid(z)
        silu = z * sig
        mix = mixed[:, here]
        product = mix * silu
        grads = grad[:, here].astype(F32)
        grad_gain[:, here] = jnp.sum(grads * (product * scale), axis=0, keepdims=True)
        grad_gated = scale * (grads * gain[:, here]) - factor * product
        grad_mix = grad_gated * silu
        grad_mixed[:, here] = grad_mix
        grad_gate[:, here] = (grad_gated * mix * (sig * (1.0 + z * (1.0 - sig)))).astype(BF16)
        values = conv[:, here].astype(F32)
        skip = by_head(small[2:3, :], pair, (1, LANES))
        rounded = grad_mix.astype(BF16).astype(F32)
        out_sums += head_sums(rounded * (mix - skip * values), pair)
        skip_sums += head_sums(grad_mix * values, pair)
        weighted = (by_head(decay, pair, shape) * grad_mix).astype(BF16)
        read_grad += dot(weighted, get_state(entry.at[pair // group], pair % group), (1, 1))
    sums[...] = out_sums
    grad_read[...] = jnp.concatenate([jnp.zeros_like(read_grad), read_grad], axis=1)
    grad_small[...] = jnp.zeros_like(grad_small)
    grad_small[2:3, :] = jnp.sum(skip_sums, axis=0, keepdims=True)


def back_kernel(grad_mixed, conv, cols, rows_ref, small, grad_read, grad_values, sums, grad_vecs):
    length, features = grad_mixed.shape
    pairs = features // LANES
    shape = (length, LANES)
    write = conv[:, features : features + N]
    read = conv[:, features + N : features + 2 * N]
    scores = dot(read, write, (1, 1))
    square = (length, length)
    causal = iota(square, 0) >= iota(square, 1)
    score_grad = jnp.zeros(square, F32)
    in_sums = jnp.zeros(shape, F32)
    first = iota(shape, 1) < P_SIZE
    for pair in range(pairs):
        here = block(pair)
        grad_mix = grad_mixed[:, here]
        values = conv[:, here]
        rounded = grad_mix.astype(BF16)
        scaled = [head_weights(cols, rows_ref, 2 * pair + which, causal, scores) for which in range(2)]
        weight_grad = dot(rounded, apart(values), (1, 1))
        score_grad += weight_grad[:, 0:length] * scaled[0][0] + weight_grad[:, length:] * scaled[1][0]
        both = dot(jnp.concatenate([scaled[0][1], scaled[1][1]], axis=1), rounded, (0, 0))
        value_grad = jnp.where(first, both[0:length], both[length:])
        in_sums += head_sums(values.astype(F32) * value_grad, pair)
        skip = by_head(small[2:3, :], pair, (1, LANES))
        grad_values[:, here] = value_grad + skip * grad_mix
    sums[...] = in_sums
    high, low = split(score_grad)
    read_grad = dot(high, write) + dot(low, write)
    write_grad = dot(high, read, (0, 0)) + dot(low, read, (0, 0))
    grad_vecs[...] = grad_read[...] + jnp.concatenate([write_grad, read_grad], axis=1)


def through_taps(taps, full, slopes, cols, start, count):
    total = full[0:1, cols] * slopes[start + taps - 1 : start + taps - 1 + count, cols]
    for tap in range(1, taps):
        ahead = start + taps - 1 - tap
        total = total + full[tap : tap + 1, cols] * slopes[ahead : ahead + count, cols]
    return total


def through_conv(taps, here, grad_out, rows, shifted, slope, slopes, whole):
    length = grad_out.shape[0]
    grad_pre = grad_out.astype(BF16).astype(F32) * slope[:, here]
    slopes[HALO : HALO + length, here] = grad_pre
    for tap in range(taps):
        given = shifted[tap, :, here] if tap < taps - 1 else rows[HALO : HALO + length, here]
        whole[tap : tap + 1, here] = jnp.sum(grad_pre * given, axis=0, keepdims=True)
    whole[taps : taps + 1, here] = jnp.sum(grad_pre, axis=0, keepdims=True)


def close_side(taps, own, rows, shifted, conv, slope, cols, picks, entries, leaves, grad_values, slopes, whole, scratch):
    products, holds, leavings, overlaps = scratch
    length, features = grad_values.shape
    half = features // LANES // 2
    group = half // STREAMS
    shape = (length, LANES)
    side = here_at()[0] if own else 1 - here_at()[0]
    write = conv[:, features : features + N]
    running = cols[1]
    tail = jnp.exp(running[length - 1 : length, :] - running) * cols[0]
    tail = pltpu.roll(tail, lax.rem(LANES - 2 * half * side, LANES), 1)
    for pair in range(half):
        here = side_block(side * half + pair)
        local = block(pair)
        leaving = get_state(leaves[pair // group], pair % group)
        values = conv[:, here].astype(F32)
        tail_wide = by_head(tail, pair, shape)
        state_grad = tail_wide * dot(write, leaving)
        products[:, local] = (values * state_grad).astype(BF16)
        holds[:, local] = (tail_wide * values).astype(BF16)
        leavings[:, local] = leaving
        entering = get_state(entries[pair // group], pair % group).astype(F32)
        overlap = jnp.sum(leaving.astype(F32) * entering, axis=0, keepdims=True)
        overlaps[:, local] = jnp.broadcast_to(overlap, (8, LANES))
        through_conv(taps, here, grad_values[:, here] + state_grad, rows, shifted, slope, slopes, whole)
    back = 2 * half * side
    choose = picks[...]
    state_sums = dot(products[...], choose)
    high, low = split(overlaps[...])
    end_sums = dot(high, choose) + dot(low, choose)
    write_grad = dot(holds[...], leavings[...], (1, 1))
    write_grad = jnp.concatenate([write_grad, jnp.zeros_like(write_grad)], axis=1)
    return pltpu.roll(state_sums, back, 1), pltpu.roll(end_sums, back, 1), write_grad


def close_own_kernel(taps, rows, shifted, conv, slope, cols, picks, grad_values, *refs):
    given, (slopes, whole, state_out, end_out, write_out, *scratch) = refs[: 2 * STREAMS], refs[2 * STREAMS :]
    length, channels = conv.shape
    slopes[0:HALO, :] = jnp.zeros((HALO, channels), F32)
    slopes[HALO + length :, :] = jnp.zeros((HALO, channels), F32)
    whole[...] = jnp.zeros_like(whole)
    state_out[...], end_out[...], write_out[...] = close_side(
        taps, True, rows, shifted, conv, slope, cols, picks, given[:STREAMS], given[STREAMS:], grad_values, slopes, whole, scratch
    )


def close_kernel(
    taps, sizes, slopes_in, whole_in, rows, shifted, conv, slope, cols, picks, small, grad_values, grad_vecs, out_sums, in_sums,
    grad_gain, grad_small, state_in, end_in, write_in, *rest
):
    given, rest, scratch = rest[: 2 * STREAMS], rest[2 * STREAMS : -4], rest[-4:]
    slopes, whole, grad_dt, *outs, cut = rest
    parts = len(outs)
    position_here = here_at()[2]
    length, channels = conv.shape
    width, gain_width, heads_here = sizes
    heads = heads_here * parts
    step = cols[0]
    last = cols[1, length - 1 : length, :]
    state_sums, end_sums, write_grad = close_side(
        taps, False, rows, shifted, conv, slope, cols, picks, given[:STREAMS], given[STREAMS:], grad_values, slopes, whole, scratch
    )
    state_sums = state_sums + state_in[...]
    end_sums = end_sums + end_in[...]
    vecs = grad_vecs[...] + (write_in[...] + write_grad)
    through_conv(taps, block(channels // LANES - 1), vecs, rows, shifted, slope, slopes, whole)

    into = in_sums[...] + state_sums
    change = out_sums[...] - into
    end_grad = jnp.sum(state_sums, axis=0, keepdims=True) + jnp.exp(last) * end_sums[0:1, :]
    square = (length, length)
    upper = iota(square, 0) <= iota(square, 1)
    log_grad = dot_parts(upper, change, 2) + end_grad
    rate = jnp.exp(small[1:2, :])
    raw_grad = (into / step - rate * log_grad) * (1.0 - jnp.exp(-step))
    grad_dt[...] = raw_grad.T[0:heads, :]
    vectors = (
        jnp.sum(raw_grad, axis=0, keepdims=True),
        jnp.sum(-rate * step * log_grad, axis=0, keepdims=True),
        grad_small[2:3, :],
    )
    piece_width = cut.shape[2]
    for part in range(parts):
        base, shift = placement(part, width)
        piece = whole[:, base : base + piece_width + LANES]
        if shift:
            piece = pltpu.roll(piece, piece_width + LANES - shift, 1)
        cut[part] = piece[:, 0:piece_width]
        cut[part, taps + 1 : taps + 2, 0:gain_width] = grad_gain[:, part * gain_width : (part + 1) * gain_width]
        for number, vector in enumerate(vectors):
            row = pltpu.roll(vector, LANES - part * heads_here, 1) if part else vector
            cut[part, taps + 2 : taps + 3, block(number)] = row
    for distance in range(parts):
        outs[distance][...] = cut[lax.rem(position_here + distance, parts)]


def input_kernel(taps, full, slopes, grad_x, ending):
    length, channels = grad_x.shape
    for position in range(channels // LANES):
        here = block(position)
        total = through_taps(taps, full, slopes, here, HALO, length)
        grad_x[:, here] = total.astype(BF16)
        ending[:, here] = total[length - 2 * HALO :]


def before_kernel(taps, full, slopes, back):
    channels = slopes.shape[1]
    folded = back.shape[1] // LANES
    back[...] = jnp.zeros_like(back)
    for position in range(channels // LANES):
        here = block(position)
        ahead = through_taps(taps, full, slopes, here, 0, HALO)
        for tap in range(taps - 1):
            at = tap * FOLDS + position // folded
            back[at : at + 1, block(position % folded)] = ahead[HALO - taps + 1 + tap : HALO - taps + 2 + tap]


def unpack_kernel(terms, chips, taps, grad_in, ending, from_core, from_chip, *refs):
    given, refs = refs[:terms], refs[terms:]
    core, chip, _ = here_at()
    grad_x, cw, cb, dtb, al, sk, gain, late, sem = refs
    rows = late.shape[0]
    channels = ending.shape[1]
    folded = from_core.shape[1] // LANES
    inside = core == 0
    later = jnp.where(inside, from_core[SMALL:, :], from_chip[SMALL:, :])
    later = jnp.where(jnp.logical_or(inside, chip < chips - 1), later, 0.0)
    padding = jnp.zeros((rows - taps + 1, LANES), F32)
    for position in range(channels // LANES):
        here = block(position)
        lines = [
            later[tap * FOLDS + position // folded : tap * FOLDS + position // folded + 1, block(position % folded)]
            for tap in range(taps - 1)
        ]
        late[:, here] = (ending[:, here] + jnp.concatenate([padding] + lines, axis=0)).astype(BF16)
    copy = pltpu.make_async_copy(late, grad_x.at[pl.ds(grad_x.shape[0] - rows, rows)], sem)
    copy.start()
    total = given[0][0:SMALL, :]
    for ref in given[1:]:
        total = total + ref[0:SMALL, :]
    width = cw.shape[1]
    cw[...] = total[0:taps, 0:width]
    cb[...] = total[taps, 0:width]
    gain[...] = total[taps + 1, 0 : gain.shape[0]]
    for number, ref in enumerate((dtb, al, sk)):
        ref[...] = total[taps + 2 : taps + 3, number * LANES : number * LANES + ref.shape[1]]
    copy.wait()


def add_kernel(*refs):
    *terms, back, out = refs
    total = terms[0][...]
    for ref in terms[1:]:
        total = total + ref[...]
    out[0:SMALL, :] = total
    out[SMALL:, :] = back[...]


def add_pair_kernel(own, other, out, alone):
    total = own[0:SMALL, :] + other[0:SMALL, :]
    out[0:SMALL, :] = total
    out[SMALL:, :] = other[SMALL:, :]
    alone[...] = total


def parts_of(message):
    end = message.shape[0] - DEC_ROWS
    return message[0:end, :].astype(F32), unpack_decays(message[end:, :])


def decayed(state, decay):
    group = state.shape[0] // N
    split_rows = state.reshape(group, N, LANES)
    return (split_rows * decay[0:group].reshape(group, 1, LANES)).reshape(state.shape)


def joined(first, second):
    state, decay = second
    return decayed(first[0], decay) + state, decay * first[1]


def store(out, value):
    state, decay = value
    end = state.shape[0]
    out[0:end, :] = state.astype(BF16)
    out[end:, :] = pack_decays(decay)


def ordered(later, a, b):
    return jnp.where(later, b, a), jnp.where(later, a, b)


def meet_kernel(reverse, mine, got, out, decay):
    later = here_at()[0] == (0 if reverse else 1)
    first, second = ordered(later, mine[...], got[...])
    whole = joined(parts_of(first), parts_of(second))
    store(out, whole)
    decay[...] = whole[1]


def join_kernel(first, second, out):
    store(out, joined(parts_of(first[...]), parts_of(second[...])))


def pass_kernel(before, own, decay, out):
    end = out.shape[0]
    state = decayed(before[0:end, :].astype(F32), decay[...])
    out[...] = (state + own[0:end, :].astype(F32)).astype(BF16)


def enter_kernel(reverse, *refs):
    given, (mine, got, own, send) = refs[:-4], refs[-4:]
    later = here_at()[0] == (0 if reverse else 1)
    end = own.shape[0]
    start = given[0][0:end, :].astype(F32)
    for ref in given[1:]:
        start = start + ref[0:end, :].astype(F32)
    state, decay = parts_of(ordered(later, mine[...], got[...])[0])
    after = decayed(start, decay) + state
    own[...] = jnp.where(later, after, start).astype(BF16)
    send[...] = jnp.where(later, start, after).astype(BF16)


def call(kernel, outs, args, scratch=(), megabytes=8, flops=0, name=None, fetched=(), aliases=None):
    specs = [
        pl.BlockSpec(
            memory_space=pltpu.HBM if number in fetched else pltpu.VMEM
        )
        for number in range(len(args))
    ]
    fetched_out = [out for given, out in (aliases or {}).items() if given in fetched]
    moved = sum(a.size * a.dtype.itemsize for a in args)
    moved += sum(o.size * o.dtype.itemsize for o in outs)
    return pl.pallas_call(
        kernel,
        out_shape=outs,
        in_specs=specs,
        out_specs=[
            pl.BlockSpec(memory_space=pltpu.HBM if number in fetched_out else pltpu.VMEM)
            for number in range(len(outs))
        ],
        input_output_aliases=aliases or {},
        scratch_shapes=list(scratch),
        compiler_params=pltpu.CompilerParams(vmem_limit_bytes=megabytes << 20),
        cost_estimate=pl.CostEstimate(flops=flops, bytes_accessed=moved, transcendentals=0),
        name=name,
    )(*args)


def like(shape, dtype=F32):
    return jax.ShapeDtypeStruct(shape, dtype)


def shift(value, axis, route):
    count = lax.axis_size(axis)
    pairs = [(i, route(i)) for i in range(count)]
    return lax.ppermute(value, axis, [(i, j) for i, j in pairs if 0 <= j < count])


def between_chips(value, routes):
    return shift(value, "seq", lambda i: 2 * routes[i // 2] + i % 2 if i // 2 in routes else -1)


def entering_states(own_states, got, reverse, beside):
    chips = lax.axis_size("seq") // 2
    message = like(got[0].shape, BF16)
    entry = like((got[0].shape[0] - DEC_ROWS, LANES), BF16)
    chip, decays, mine = [], [], []
    for stream, other in enumerate(got):
        mine.append(own_states(stream, chip))
        whole, decay = call(
            functools.partial(meet_kernel, reverse),
            [message, like((DEC_ROWS, LANES))],
            [mine[-1], other],
            name="meet",
        )
        chip.append(whole)
        decays.append(decay)
    if 1 < chips <= 4:
        order = list(range(chips))[::-1] if reverse else list(range(chips))
        arrived = [[] for _ in chip]
        moving = chip
        for hop in range(chips - 1):
            route = {order[hop]: order[hop + 1]}
            landed = [between_chips(part, route) for part in moving]
            if hop < len(beside):
                landed = beside[hop](moving, landed)
            for stream, part in zip(arrived, landed):
                stream.append(part)
            if hop < chips - 2:
                moving = [
                    call(pass_kernel, [entry], list(parts), name="pass")[0] for parts in zip(landed, chip, decays)
                ]
    else:
        sign = -1 if reverse else 1
        before = [shift(part, "seq", lambda i: i + 2 * sign) for part in chip]
        before = beside[1](chip, beside[0](chip, before))
        window = 1
        while window < chips - 1:
            distance = window + 1
            longer = [call(join_kernel, [message], pair, name="join")[0] for pair in zip(before, chip)]
            far = [shift(part, "seq", lambda i: i + 2 * distance * sign) for part in longer]
            before = [call(join_kernel, [message], pair, name="join")[0] for pair in zip(far, before)]
            window = 2 * window + 1
        arrived = [[part] for part in before]
    owns, others = [], []
    for parts, a, b in zip(arrived, mine, got):
        own, send = call(functools.partial(enter_kernel, reverse), [entry, entry], parts + [a, b], name="enter")
        owns.append(own)
        others.append(shift(send, "seq", lambda i: i ^ 1))
    return owns, others


def after(value, *signals):
    return lax.optimization_barrier((value, *signals))[0]


def shards(
    conv_input, gate_input, dt_raw, grad_output, conv_weight, conv_bias, dt_bias, a_log, skip, norm_gain
):
    gate, grad = gate_input[0], grad_output[0]
    dt = dt_raw[0].T
    length, channels = conv_input.shape[1:]
    features = gate.shape[1]
    heads = dt.shape[0]
    half = heads // 4
    taps, width = conv_weight.shape
    gain_width = norm_gain.shape[0]
    heads_here = dt_bias.shape[0]
    parts = lax.axis_size("fsdp")
    devices = lax.axis_size("seq")
    sizes = (width, gain_width, heads_here)
    piece_width = -(-width // LANES) * LANES
    full_width = placement(parts - 1, width)[0] + piece_width + LANES
    piece_like = like((SMALL, piece_width))
    shares = [
        conv_weight,
        conv_bias.reshape(1, -1),
        dt_bias.reshape(1, -1),
        a_log.reshape(1, -1),
        skip.reshape(1, -1),
        norm_gain,
    ]

    x = conv_input[0]
    halo, piece, own = call(
        open_kernel,
        [like((HALO, channels), BF16), piece_like, like((2 * SMALL, piece_width))],
        [x, dt] + shares,
        [pltpu.VMEM((2 * HALO, channels), BF16), pltpu.VMEM(dt.shape, F32)]
        + [pltpu.VMEM(share.shape, F32) for share in shares]
        + [pltpu.SemaphoreType.DMA((len(shares) + 2,))],
        fetched=range(len(shares) + 2),
        megabytes=60,
        name="open",
    )
    pieces = [shift(piece, "fsdp", lambda i: peer(i, distance, parts)) for distance in range(1, parts)]
    halo = shift(halo, "seq", lambda i: i + 1)
    lifted = jnp.pad(after(x, piece).astype(F32), ((HALO, 0), (0, 0)))

    group = half // STREAMS
    message = like((group * N + DEC_ROWS, LANES), BF16)
    entry = pltpu.VMEM((2 * STREAMS, group * N, LANES), BF16)
    wide = like((length, features))
    square = like((length, LANES))
    full, gain, small, cols, rows, decs = call(
        functools.partial(gather_kernel, taps, sizes, parts, length),
        [
            like((SMALL, full_width)),
            like((1, features)),
            like((8, LANES)),
            like((2, length, LANES)),
            like((3, LANES, length)),
            like((2 * STREAMS, DEC_ROWS, LANES), BF16),
        ],
        [own] + pieces,
        [pltpu.VMEM((LANES, LANES), F32), pltpu.VMEM((parts, SMALL, piece_width), F32)],
        name="gather",
    )
    conv_like = like((length, channels), BF16)
    padded, conv, write_t, other = call(
        functools.partial(front_kernel, taps),
        [like(lifted.shape), conv_like, like((N, length)), message],
        [lifted, halo, full, rows, decs],
        name="front",
        aliases={0: 0},
    )
    got = [shift(other, "seq", lambda i: i ^ 1)]
    for stream in range(1, STREAMS):
        conv, other = call(
            functools.partial(front_next_kernel, taps, False, (stream,)),
            [conv_like, message],
            [conv, padded, full, rows, decs, write_t],
            name="front",
            aliases={0: 0},
        )
        got.append(shift(other, "seq", lambda i: i ^ 1))
    held = [conv]

    def own_first(stream, signals):
        held[0], mine = call(
            functools.partial(front_next_kernel, taps, True, (stream,)),
            [conv_like, message],
            [after(held[0], *signals), padded, full, rows, decs, write_t],
            name="own",
            aliases={0: 0},
        )
        return mine

    work = {}

    def intra(signal, value):
        work["local"], work["slope"] = call(
            functools.partial(intra_kernel, taps),
            [wide, like((length, channels))],
            [padded, full, after(held[0], *signal), cols, rows, small],
            flops=2 * length * length * features,
            name="intra",
        )
        return [after(part, work["local"]) for part in value]

    def factors(signal, value):
        *work["factors"], work["picks"], work["shifted"] = call(
            factor_kernel,
            [wide] * 3 + [like((half * LANES, LANES), BF16), like((taps - 1, length, channels))],
            [after(cols, *signal), gate, grad, gain, padded],
            flops=length * features * 16,
            name="factors",
        )
        return [after(part, work["factors"][0]) for part in value]

    sums_like = like((2, length, LANES))

    entry_own, entry_got = entering_states(own_first, got, False, (intra, factors))
    conv = held[0]
    silus, grown, decays = work["factors"]
    given = [work["local"], conv, silus, grown, decays]
    mixed, gated, sums = call(mix_kernel, [wide, wide, sums_like], given + entry_own, name="mix")
    mixed, gated, stats, other = call(
        norm_kernel,
        [wide, wide, square, message],
        [mixed, gated] + given + [sums, decs] + entry_got,
        name="norm",
        aliases={0: 0, 1: 1},
    )
    got = [shift(other, "seq", lambda i: i ^ 1)]
    given = [conv, silus, grown, decays, gated, decs]

    def norm_next(own, stream, signals):
        return call(
            functools.partial(norm_next_kernel, own, (stream,)),
            [message],
            [after(stats, *signals)] + given,
            name="norm_next",
        )[0]

    for stream in range(1, STREAMS):
        got.append(shift(norm_next(False, stream, []), "seq", lambda i: i ^ 1))

    def gates(signal, value):
        work["gates"] = call(
            gate_kernel,
            [
                like((length, features), BF16),
                like((length, features)),
                like((length, LANES)),
                like((1, features)),
                like((8, LANES)),
                like((length, LANES)),
            ],
            [mixed, after(conv, *signal), cols, small, gate, grad, gain, stats] + entry_own + entry_got,
            [entry],
                flops=2 * length * length * features,
            name="gates",
        )
        return [after(part, work["gates"][0]) for part in value]

    def back(signal, value):
        grad_mixed, grad_read = work["gates"][1], work["gates"][5]
        work["back"] = call(
            back_kernel,
            [like((length, features)), like((length, LANES)), like((length, LANES))],
            [after(grad_mixed, *signal), conv, cols, rows, small, grad_read],
            flops=4 * length * length * features,
            name="back",
        )
        return [after(part, work["back"][0]) for part in value]

    shapes = [like((2 * HALO + length, channels)), like((SMALL, full_width)), square, like((8, LANES)), square]
    fixed = [padded, work["shifted"], conv, work["slope"], cols, work["picks"]]
    side = half * LANES
    scratch = [pltpu.VMEM((length, side), BF16)] * 2 + [pltpu.VMEM((N, side), BF16), pltpu.VMEM((8, side), F32)]

    leave_own, leave_got = entering_states(functools.partial(norm_next, True), got, True, (gates, back))
    grad_gate, _, out_sums, grad_gain, grad_small, _ = work["gates"]
    grad_values, in_sums, grad_vecs = work["back"]
    slopes, whole, *sums = call(
        functools.partial(close_own_kernel, taps),
        shapes,
        fixed + [grad_values] + entry_own + leave_own,
        scratch,
        name="close_own",
    )
    slopes, whole, grad_dt, *shares = call(
        functools.partial(close_kernel, taps, sizes),
        shapes[:2] + [like((heads, length))] + [piece_like] * parts,
        [slopes, whole] + fixed + [small, grad_values, grad_vecs, out_sums, in_sums, grad_gain, grad_small]
        + sums + entry_got + leave_got,
        [pltpu.VMEM((parts, SMALL, piece_width), F32)] + scratch,
        name="close",
        aliases={0: 0, 1: 1},
    )
    terms = [shares[0]]
    for distance in range(1, parts):
        terms.append(shift(shares[distance], "fsdp", lambda i: (i + distance) % parts))
    earlier = call(
        functools.partial(before_kernel, taps), [like((BACK_ROWS, piece_width))], [full, slopes], name="before"
    )[0]
    bundle = like((SMALL + BACK_ROWS, piece_width))
    total = call(add_kernel, [bundle], terms + [earlier], name="add")[0]
    partner = shift(total, "seq", lambda i: i ^ 1)
    total, alone = call(add_pair_kernel, [bundle, piece_like], [total, partner], name="add")
    chips = devices // 2
    behind = between_chips(total, {i: (i - 1) % chips for i in range(chips)})
    if chips <= 4:
        terms = [alone] + [
            between_chips(alone, {i: (i + distance) % chips for i in range(chips)})
            for distance in range(1, chips - 1)
        ]
        terms += [behind] if chips > 1 else []
    else:
        terms = [lax.psum(alone, "seq") * 0.5]
    grad_x, ending = call(
        functools.partial(input_kernel, taps),
        [like((length, channels), BF16), like((2 * HALO, channels))],
        [full, after(slopes, alone)],
        flops=length * channels * 16,
        name="inputs",
    )
    grad_x, cw, cb, dtb, al, sk, gn = call(
        functools.partial(unpack_kernel, len(terms), chips, taps),
        [
            like((length, channels), BF16),
            like((taps, width)),
            like((width,)),
            like((1, heads_here)),
            like((1, heads_here)),
            like((1, heads_here)),
            like((gain_width,)),
        ],
        [grad_x, ending, partner, behind] + terms,
        [pltpu.VMEM((2 * HALO, channels), BF16), pltpu.SemaphoreType.DMA],
        fetched=(0,),
        aliases={0: 0},
        name="unpack",
    )
    return (
        grad_x[None],
        grad_gate[None],
        grad_dt.T[None],
        cw,
        cb,
        dtb.reshape(-1),
        al.reshape(-1),
        sk.reshape(-1),
        gn,
    )


def solution(mesh):
    tokens = P("fsdp", "seq", None)
    in_specs = (tokens,) * 4 + (P(None, "fsdp"),) + (P("fsdp"),) * 5
    out_specs = (tokens,) * 3 + (P(None, "fsdp"),) + (P("fsdp"),) * 5
    return jax.shard_map(shards, mesh=mesh, in_specs=in_specs, out_specs=out_specs, check_vma=False)
```

```python
import functools

import jax
import jax.numpy as jnp
from jax import lax
from jax.experimental import pallas as pl
from jax.experimental.pallas import tpu as pltpu
from jax.sharding import PartitionSpec as P

P_SIZE = 64
N = 64
EPS = 1e-05
LANES = 2 * P_SIZE
HALO = 8
SMALL = 8
STREAMS = 2
FOLDS = 4
BACK_ROWS = 16
DEC_ROWS = 16
F32, BF16 = jnp.float32, jnp.bfloat16


def dot(a, b, over=(1, 0)):
    return lax.dot_general(
        a, b, (((over[0],), (over[1],)), ((), ())), preferred_element_type=F32
    )


def here_at():
    index = lax.axis_index("seq")
    return lax.rem(index, 2), lax.div(index, 2), lax.axis_index("fsdp")


def iota(shape, axis):
    return lax.broadcasted_iota(jnp.int32, shape, axis)


def sigmoid(x):
    return 0.5 * jnp.tanh(0.5 * x) + 0.5


def split(x):
    high = x.astype(BF16)
    return high, (x - high.astype(F32)).astype(BF16)


def dot_parts(ones, value, parts):
    pieces = []
    for _ in range(parts):
        piece = value.astype(BF16)
        pieces.append(piece)
        value = value - piece.astype(F32)
    ones = ones.astype(BF16)
    return dot(jnp.concatenate([ones] * parts, axis=1), jnp.concatenate(pieces, axis=0))


def block(position):
    return slice(position * LANES, (position + 1) * LANES)


def by_head(columns, pair, shape):
    first = jnp.broadcast_to(columns[:, 2 * pair : 2 * pair + 1], shape)
    second = jnp.broadcast_to(columns[:, 2 * pair + 1 : 2 * pair + 2], shape)
    return jnp.where(iota(shape, 1) < P_SIZE, first, second)


def apart(pair_block):
    first = iota(pair_block.shape, 1) < P_SIZE
    zero = jnp.zeros_like(pair_block)
    return jnp.concatenate(
        [jnp.where(first, pair_block, zero), jnp.where(first, zero, pair_block)], axis=0
    )


def head_sums(product, pair, parts=2):
    shape = (LANES, LANES)
    pick = (iota(shape, 1) == 2 * pair + (iota(shape, 0) >= P_SIZE).astype(jnp.int32)).astype(BF16)
    if parts == 1:
        return dot(product.astype(BF16), pick)
    high, low = split(product)
    return dot(jnp.concatenate([high, low], axis=1), jnp.concatenate([pick, pick], axis=0))


def before_silu(rows, full, cols, taps, length):
    start = HALO - (taps - 1)
    total = full[taps : taps + 1, cols] + full[0:1, cols] * rows[start : start + length, cols]
    for tap in range(1, taps):
        total = total + full[tap : tap + 1, cols] * rows[start + tap : start + tap + length, cols]
    return total


def open_kernel(x, dt, cw, cb, dtb, al, sk, gain, halo, out, own, late, raw, *rest):
    held, sems = rest[:-1], rest[-1]
    ending = x.at[pl.ds(x.shape[0] - late.shape[0], late.shape[0])]
    copies = [
        pltpu.make_async_copy(source, target, sems.at[number])
        for number, (source, target) in enumerate(
            zip((cw, cb, dtb, al, sk, gain, dt, ending), held + (raw, late))
        )
    ]
    for copy in copies:
        copy.start()
    out[...] = jnp.zeros_like(out)
    for copy in copies:
        copy.wait()
    halo[...] = late[...].astype(F32)[HALO:].astype(BF16)
    cw, cb, dtb, al, sk, gain = held
    taps, width = cw.shape
    out[0:taps, 0:width] = cw[...]
    out[taps : taps + 1, 0:width] = cb[...]
    out[taps + 1 : taps + 2, 0 : gain.shape[0]] = gain[...].reshape(1, -1)
    for number, ref in enumerate((dtb, al, sk)):
        out[taps + 2 : taps + 3, number * LANES : number * LANES + ref.shape[1]] = ref[...]
    own[0:SMALL, :] = out[...]
    own[SMALL:, :] = jnp.zeros((SMALL, own.shape[1]), F32)
    for group in range(raw.shape[0] // SMALL):
        own[SMALL:, block(group)] = raw[group * SMALL : (group + 1) * SMALL, :]


def peer(position, distance, parts):
    if parts & (parts - 1) == 0:
        return position ^ distance
    return (position + distance) % parts


def peer_back(position, distance, parts):
    if parts & (parts - 1) == 0:
        return position ^ distance
    return lax.rem(position + parts - distance, parts)


def placement(position, width):
    start = position * width
    base = start // LANES * LANES
    return base, start - base


def put_state(states, pair, value):
    states[pair * N : (pair + 1) * N, :] = value


def get_state(states, pair):
    return states[pair * N : (pair + 1) * N, :]


def pack_decays(decays):
    high, low = split(decays)
    group = iota(decays.shape, 1) // (P_SIZE // 2)
    return jnp.where(lax.rem(group, 2) == 0, high.astype(F32), low.astype(F32)).astype(BF16)


def unpack_decays(packed):
    value = packed.astype(F32)
    group = iota(value.shape, 1) // (P_SIZE // 2)
    ahead = pltpu.roll(value, LANES - P_SIZE // 2, 1)
    behind = pltpu.roll(value, P_SIZE // 2, 1)
    return value + jnp.where(lax.rem(group, 2) == 0, ahead, behind)


def gather_kernel(taps, sizes, parts, length, own, *refs):
    given, refs = refs[: parts - 1], refs[parts - 1 :]
    full, gain, small, cols, rows_out, decs, wide, pieces = refs
    mine_at = here_at()[2]
    piece_width = pieces.shape[2]
    pieces[mine_at] = own[0:SMALL, :]
    for distance in range(1, parts):
        pieces[peer_back(mine_at, distance, parts)] = given[distance - 1][...]
    width, gain_width, heads_here = sizes
    heads = heads_here * parts
    half = heads // 4
    full[...] = jnp.zeros_like(full)
    small[...] = jnp.zeros_like(small)
    wide[...] = jnp.zeros_like(wide)
    for group in range(heads // SMALL):
        wide[group * SMALL : (group + 1) * SMALL, :] = own[SMALL:, block(group)]
    for part in range(parts):
        base, shift = placement(part, width)
        piece = jnp.concatenate([pieces[part], jnp.zeros((SMALL, LANES), F32)], axis=1)
        if shift:
            piece = pltpu.roll(piece, shift, 1)
        full[:, base : base + piece_width + LANES] += piece
        gain[:, part * gain_width : (part + 1) * gain_width] = pieces[
            part, taps + 1 : taps + 2, 0:gain_width
        ]
        for number in range(3):
            row = pieces[part, taps + 2 : taps + 3, block(number)]
            if part:
                row = pltpu.roll(row, part * heads_here, 1)
            small[number : number + 1, :] += row
    raw = wide[...].T + small[0:1, :]
    step = jnp.maximum(raw, 0.0) + jnp.log1p(jnp.exp(-jnp.abs(raw)))
    logs = -jnp.exp(small[1:2, :]) * step
    square = (length, length)
    lower = iota(square, 0) >= iota(square, 1)
    running = dot_parts(lower, logs, 3)
    running_t = running.T
    step_t = step.T
    last = jnp.broadcast_to(running_t[:, length - 1 : length], running_t.shape)
    cols[0] = step
    cols[1] = running
    rows_out[0] = step_t
    rows_out[1] = running_t
    rows_out[2] = jnp.exp(last - running_t) * step_t
    wide[...] = jnp.exp(last)[:, 0:LANES]
    group = half // STREAMS
    first = iota((group, LANES), 1) < P_SIZE
    for number in range(2 * STREAMS):
        even = wide[pl.ds(2 * group * number, group, stride=2), :]
        odd = wide[pl.ds(2 * group * number + 1, group, stride=2), :]
        decays = jnp.where(first, even, odd)
        decs[number] = pack_decays(
            jnp.concatenate([decays, jnp.zeros((DEC_ROWS - group, LANES), F32)], axis=0)
        )


def side_block(pair):
    return pl.ds(pl.multiple_of(pair * LANES, LANES), LANES)


def front_group(taps, number, rows, full, tails, decs, write_t, conv, out):
    length = conv.shape[0]
    group = (out.shape[0] - DEC_ROWS) // N
    scale = tails[2, pl.ds(number * 2 * group, 2 * group), :]
    for pair in range(group):
        here = side_block(number * group + pair)
        pre = before_silu(rows, full, here, taps, length)
        value = (pre * sigmoid(pre)).astype(BF16)
        conv[:, here] = value
        scaled = jnp.concatenate(
            [
                (write_t * scale[2 * pair + which : 2 * pair + which + 1, :]).astype(BF16)
                for which in range(2)
            ],
            axis=1,
        )
        put_state(out, pair, dot(scaled, apart(value)).astype(BF16))
    out[group * N :, :] = decs[number]


def front_kernel(taps, lifted, halo, full, tails, decs, rows, conv, write_out, out):
    length, channels = conv.shape
    rows[0:HALO, :] = halo[...].astype(F32)
    here = block(channels // LANES - 1)
    pre = before_silu(rows, full, here, taps, length)
    vectors = (pre * sigmoid(pre)).astype(BF16)
    conv[:, here] = vectors
    write_t = vectors.astype(F32).T[0:N, :]
    write_out[...] = write_t
    front_group(taps, group_at(False, 0), rows, full, tails, decs, write_t, conv, out)


def group_at(own, stream):
    core = here_at()[0]
    return (core if own else 1 - core) * STREAMS + stream


def front_next_kernel(taps, own, streams, conv_in, rows, full, tails, decs, write_t, conv, *outs):
    for stream, out in zip(streams, outs):
        front_group(taps, group_at(own, stream), rows, full, tails, decs, write_t[...], conv, out)


def head_weights(cols, rows_ref, head, causal, scores):
    gap = cols[1, :, head : head + 1] - rows_ref[1, head : head + 1, :]
    scaled = jnp.exp(jnp.where(causal, gap, -1e30)) * rows_ref[0, head : head + 1, :]
    return scaled, (scaled * scores).astype(BF16)


def factor_kernel(cols, gate, grad, gain, rows, silus, grown, decays, picks, shifted):
    length, features = gate.shape
    taps = shifted.shape[0] + 1
    for tap in range(taps - 1):
        start = HALO - taps + 1 + tap
        shifted[tap] = rows[start : start + length, :]
    decay = jnp.exp(cols[1])
    picks[...] = (iota(picks.shape, 1) == iota(picks.shape, 0) // P_SIZE).astype(BF16)
    for pair in range(features // LANES):
        here = block(pair)
        z = gate[:, here].astype(F32)
        silus[:, here] = z * sigmoid(z)
        grown[:, here] = grad[:, here].astype(F32) * gain[:, here]
        decays[:, here] = by_head(decay, pair, (length, LANES))


def intra_kernel(taps, rows, full, conv, cols, rows_ref, small, local, slope):
    length, channels = conv.shape
    features = local.shape[1]
    pairs = features // LANES
    write = conv[:, features : features + N]
    read = conv[:, features + N : features + 2 * N]
    scores = dot(read, write, (1, 1))
    square = (length, length)
    causal = iota(square, 0) >= iota(square, 1)
    for pair in range(pairs):
        weights = jnp.concatenate(
            [head_weights(cols, rows_ref, 2 * pair + which, causal, scores)[1] for which in range(2)],
            axis=1,
        )
        values = conv[:, block(pair)]
        skip = by_head(small[2:3, :], pair, (1, LANES))
        here = block(pair)
        local[:, here] = dot(weights, apart(values)) + skip * values.astype(F32)
    for position in range(channels // LANES):
        here = block(position)
        pre = before_silu(rows, full, here, taps, length)
        gate = sigmoid(pre)
        slope[:, here] = gate * (1.0 + pre * (1.0 - gate))


def mix_side(own, local, conv, silus, grown, decays, entries, mixed, gated):
    length, features = local.shape
    shape = (length, LANES)
    read = conv[:, features + N : features + 2 * N]
    square_sum = jnp.zeros(shape, F32)
    cross_sum = jnp.zeros(shape, F32)
    for stream, entry in enumerate(entries):
        number = group_at(own, stream)
        group = entry.shape[0] // N
        for pair in range(group):
            here = side_block(number * group + pair)
            carried = dot(read, get_state(entry, pair))
            mix = local[:, here] + decays[:, here] * carried
            mixed[:, here] = mix
            product = mix * silus[:, here]
            gated[:, here] = product
            square_sum += product * product
            cross_sum += product * grown[:, here]
    return square_sum, cross_sum


def mix_kernel(local, conv, silus, grown, decays, *refs):
    entries, (mixed, gated, sums) = refs[:STREAMS], refs[STREAMS:]
    square, cross = mix_side(True, local, conv, silus, grown, decays, entries, mixed, gated)
    sums[0] = square
    sums[1] = cross


def back_state(number, stats, conv, silus, grown, decays, gated, decs, out):
    length, features = gated.shape
    group = (out.shape[0] - DEC_ROWS) // N
    shape = (length, LANES)
    read = conv[:, features + N : features + 2 * N]
    scale = jnp.broadcast_to(stats[:, 0:1], shape)
    factor = jnp.broadcast_to(stats[:, 1:2], shape)
    for pair in range(group):
        here = side_block(number * group + pair)
        grad_gated = scale * grown[:, here] - factor * gated[:, here]
        weighted = decays[:, here] * (grad_gated * silus[:, here])
        put_state(out, pair, dot(read, weighted.astype(BF16), (0, 0)).astype(BF16))
    out[group * N :, :] = decs[number]


def norm_kernel(mixed_in, gated_in, local, conv, silus, grown, decays, sums, decs, *refs):
    entries, (mixed, gated, stats, out) = refs[:STREAMS], refs[STREAMS:]
    length, features = local.shape
    square, cross = mix_side(False, local, conv, silus, grown, decays, entries, mixed, gated)
    square = jnp.sum(square + sums[0], axis=1, keepdims=True)
    cross = jnp.sum(cross + sums[1], axis=1, keepdims=True)
    scale = lax.rsqrt(square * (1.0 / features) + EPS)
    factor = scale * scale * scale * cross * (1.0 / features)
    lane = iota((length, LANES), 1)
    values = jnp.where(lane == 0, scale, jnp.where(lane == 1, factor, 0.0))
    stats[...] = values
    back_state(group_at(False, 0), values, conv, silus, grown, decays, gated, decs, out)


def norm_next_kernel(own, streams, stats, conv, silus, grown, decays, gated, decs, *outs):
    for stream, out in zip(streams, outs):
        back_state(group_at(own, stream), stats[...], conv, silus, grown, decays, gated, decs, out)


def gate_kernel(
    mixed, conv, cols, small, gate, grad, gain, stats, *refs
):
    given, refs = refs[: 2 * STREAMS], refs[2 * STREAMS :]
    grad_gate, grad_mixed, sums, grad_gain, grad_small, grad_read, entry = refs
    length, features = mixed.shape
    pairs = features // LANES
    group = pairs // (2 * STREAMS)
    shape = (length, LANES)
    for number, ref in enumerate(given):
        entry[group_at(number < STREAMS, number % STREAMS)] = ref[...]
    scale = jnp.broadcast_to(stats[:, 0:1], shape)
    factor = jnp.broadcast_to(stats[:, 1:2], shape)
    decay = jnp.exp(cols[1])
    read_grad = jnp.zeros((length, N), F32)
    out_sums = jnp.zeros(shape, F32)
    skip_sums = jnp.zeros(shape, F32)
    for pair in range(pairs):
        here = block(pair)
        z = gate[:, here].astype(F32)
        sig = sigmoid(z)
        silu = z * sig
        mix = mixed[:, here]
        product = mix * silu
        grads = grad[:, here].astype(F32)
        grad_gain[:, here] = jnp.sum(grads * (product * scale), axis=0, keepdims=True)
        grad_gated = scale * (grads * gain[:, here]) - factor * product
        grad_mix = grad_gated * silu
        grad_mixed[:, here] = grad_mix
        grad_gate[:, here] = (grad_gated * mix * (sig * (1.0 + z * (1.0 - sig)))).astype(BF16)
        values = conv[:, here].astype(F32)
        skip = by_head(small[2:3, :], pair, (1, LANES))
        rounded = grad_mix.astype(BF16).astype(F32)
        out_sums += head_sums(rounded * (mix - skip * values), pair)
        skip_sums += head_sums(grad_mix * values, pair)
        weighted = (by_head(decay, pair, shape) * grad_mix).astype(BF16)
        read_grad += dot(weighted, get_state(entry.at[pair // group], pair % group), (1, 1))
    sums[...] = out_sums
    grad_read[...] = jnp.concatenate([jnp.zeros_like(read_grad), read_grad], axis=1)
    grad_small[...] = jnp.zeros_like(grad_small)
    grad_small[2:3, :] = jnp.sum(skip_sums, axis=0, keepdims=True)


def back_kernel(grad_mixed, conv, cols, rows_ref, small, grad_read, grad_values, sums, grad_vecs):
    length, features = grad_mixed.shape
    pairs = features // LANES
    shape = (length, LANES)
    write = conv[:, features : features + N]
    read = conv[:, features + N : features + 2 * N]
    scores = dot(read, write, (1, 1))
    square = (length, length)
    causal = iota(square, 0) >= iota(square, 1)
    score_grad = jnp.zeros(square, F32)
    in_sums = jnp.zeros(shape, F32)
    first = iota(shape, 1) < P_SIZE
    for pair in range(pairs):
        here = block(pair)
        grad_mix = grad_mixed[:, here]
        values = conv[:, here]
        rounded = grad_mix.astype(BF16)
        scaled = [head_weights(cols, rows_ref, 2 * pair + which, causal, scores) for which in range(2)]
        weight_grad = dot(rounded, apart(values), (1, 1))
        score_grad += weight_grad[:, 0:length] * scaled[0][0] + weight_grad[:, length:] * scaled[1][0]
        both = dot(jnp.concatenate([scaled[0][1], scaled[1][1]], axis=1), rounded, (0, 0))
        value_grad = jnp.where(first, both[0:length], both[length:])
        in_sums += head_sums(values.astype(F32) * value_grad, pair)
        skip = by_head(small[2:3, :], pair, (1, LANES))
        grad_values[:, here] = value_grad + skip * grad_mix
    sums[...] = in_sums
    high, low = split(score_grad)
    read_grad = dot(high, write) + dot(low, write)
    write_grad = dot(high, read, (0, 0)) + dot(low, read, (0, 0))
    grad_vecs[...] = grad_read[...] + jnp.concatenate([write_grad, read_grad], axis=1)


def through_taps(taps, full, slopes, cols, start, count):
    total = full[0:1, cols] * slopes[start + taps - 1 : start + taps - 1 + count, cols]
    for tap in range(1, taps):
        ahead = start + taps - 1 - tap
        total = total + full[tap : tap + 1, cols] * slopes[ahead : ahead + count, cols]
    return total


def through_conv(taps, here, grad_out, rows, shifted, slope, slopes, whole):
    length = grad_out.shape[0]
    grad_pre = grad_out.astype(BF16).astype(F32) * slope[:, here]
    slopes[HALO : HALO + length, here] = grad_pre
    for tap in range(taps):
        given = shifted[tap, :, here] if tap < taps - 1 else rows[HALO : HALO + length, here]
        whole[tap : tap + 1, here] = jnp.sum(grad_pre * given, axis=0, keepdims=True)
    whole[taps : taps + 1, here] = jnp.sum(grad_pre, axis=0, keepdims=True)


def close_side(taps, own, rows, shifted, conv, slope, cols, picks, entries, leaves, grad_values, slopes, whole, scratch):
    products, holds, leavings, overlaps = scratch
    length, features = grad_values.shape
    half = features // LANES // 2
    group = half // STREAMS
    shape = (length, LANES)
    side = here_at()[0] if own else 1 - here_at()[0]
    write = conv[:, features : features + N]
    running = cols[1]
    tail = jnp.exp(running[length - 1 : length, :] - running) * cols[0]
    tail = pltpu.roll(tail, lax.rem(LANES - 2 * half * side, LANES), 1)
    for pair in range(half):
        here = side_block(side * half + pair)
        local = block(pair)
        leaving = get_state(leaves[pair // group], pair % group)
        values = conv[:, here].astype(F32)
        tail_wide = by_head(tail, pair, shape)
        state_grad = tail_wide * dot(write, leaving)
        products[:, local] = (values * state_grad).astype(BF16)
        holds[:, local] = (tail_wide * values).astype(BF16)
        leavings[:, local] = leaving
        entering = get_state(entries[pair // group], pair % group).astype(F32)
        overlap = jnp.sum(leaving.astype(F32) * entering, axis=0, keepdims=True)
        overlaps[:, local] = jnp.broadcast_to(overlap, (8, LANES))
        through_conv(taps, here, grad_values[:, here] + state_grad, rows, shifted, slope, slopes, whole)
    back = 2 * half * side
    choose = picks[...]
    state_sums = dot(products[...], choose)
    high, low = split(overlaps[...])
    end_sums = dot(high, choose) + dot(low, choose)
    write_grad = dot(holds[...], leavings[...], (1, 1))
    write_grad = jnp.concatenate([write_grad, jnp.zeros_like(write_grad)], axis=1)
    return pltpu.roll(state_sums, back, 1), pltpu.roll(end_sums, back, 1), write_grad


def close_own_kernel(taps, rows, shifted, conv, slope, cols, picks, grad_values, *refs):
    given, (slopes, whole, state_out, end_out, write_out, *scratch) = refs[: 2 * STREAMS], refs[2 * STREAMS :]
    length, channels = conv.shape
    slopes[0:HALO, :] = jnp.zeros((HALO, channels), F32)
    slopes[HALO + length :, :] = jnp.zeros((HALO, channels), F32)
    whole[...] = jnp.zeros_like(whole)
    state_out[...], end_out[...], write_out[...] = close_side(
        taps, True, rows, shifted, conv, slope, cols, picks, given[:STREAMS], given[STREAMS:], grad_values, slopes, whole, scratch
    )


def close_kernel(
    taps, sizes, slopes_in, whole_in, rows, shifted, conv, slope, cols, picks, small, grad_values, grad_vecs, out_sums, in_sums,
    grad_gain, grad_small, state_in, end_in, write_in, *rest
):
    given, rest, scratch = rest[: 2 * STREAMS], rest[2 * STREAMS : -4], rest[-4:]
    slopes, whole, grad_raw, *outs, cut = rest
    parts = len(outs)
    position_here = here_at()[2]
    length, channels = conv.shape
    width, gain_width, heads_here = sizes
    step = cols[0]
    last = cols[1, length - 1 : length, :]
    state_sums, end_sums, write_grad = close_side(
        taps, False, rows, shifted, conv, slope, cols, picks, given[:STREAMS], given[STREAMS:], grad_values, slopes, whole, scratch
    )
    state_sums = state_sums + state_in[...]
    end_sums = end_sums + end_in[...]
    vecs = grad_vecs[...] + (write_in[...] + write_grad)
    through_conv(taps, block(channels // LANES - 1), vecs, rows, shifted, slope, slopes, whole)

    into = in_sums[...] + state_sums
    change = out_sums[...] - into
    end_grad = jnp.sum(state_sums, axis=0, keepdims=True) + jnp.exp(last) * end_sums[0:1, :]
    square = (length, length)
    upper = iota(square, 0) <= iota(square, 1)
    log_grad = dot_parts(upper, change, 2) + end_grad
    rate = jnp.exp(small[1:2, :])
    raw_grad = (into / step - rate * log_grad) * (1.0 - jnp.exp(-step))
    grad_raw[...] = raw_grad
    vectors = (
        jnp.sum(raw_grad, axis=0, keepdims=True),
        jnp.sum(-rate * step * log_grad, axis=0, keepdims=True),
        grad_small[2:3, :],
    )
    piece_width = cut.shape[2]
    for part in range(parts):
        base, shift = placement(part, width)
        piece = whole[:, base : base + piece_width + LANES]
        if shift:
            piece = pltpu.roll(piece, piece_width + LANES - shift, 1)
        cut[part] = piece[:, 0:piece_width]
        cut[part, taps + 1 : taps + 2, 0:gain_width] = grad_gain[:, part * gain_width : (part + 1) * gain_width]
        for number, vector in enumerate(vectors):
            row = pltpu.roll(vector, LANES - part * heads_here, 1) if part else vector
            cut[part, taps + 2 : taps + 3, block(number)] = row
    for distance in range(parts):
        outs[distance][...] = cut[lax.rem(position_here + distance, parts)]


def input_kernel(taps, full, slopes, grad_raw, grad_x, ending, grad_dt):
    grad_dt[...] = grad_raw[...].T[0 : grad_dt.shape[0], :]
    length, channels = grad_x.shape
    for position in range(channels // LANES):
        here = block(position)
        total = through_taps(taps, full, slopes, here, HALO, length)
        grad_x[:, here] = total.astype(BF16)
        ending[:, here] = total[length - 2 * HALO :]


def before_kernel(taps, full, slopes, back):
    channels = slopes.shape[1]
    folded = back.shape[1] // LANES
    back[...] = jnp.zeros_like(back)
    for position in range(channels // LANES):
        here = block(position)
        ahead = through_taps(taps, full, slopes, here, 0, HALO)
        for tap in range(taps - 1):
            at = tap * FOLDS + position // folded
            back[at : at + 1, block(position % folded)] = ahead[HALO - taps + 1 + tap : HALO - taps + 2 + tap]


def patch_kernel(chips, taps, grad_in, ending, from_core, from_chip, grad_x, late, sem):
    core, chip, _ = here_at()
    rows = late.shape[0]
    channels = ending.shape[1]
    folded = from_core.shape[1] // LANES
    inside = core == 0
    later = jnp.where(inside, from_core[SMALL:, :], from_chip[SMALL:, :])
    later = jnp.where(jnp.logical_or(inside, chip < chips - 1), later, 0.0)
    padding = jnp.zeros((rows - taps + 1, LANES), F32)
    for position in range(channels // LANES):
        here = block(position)
        lines = [
            later[tap * FOLDS + position // folded : tap * FOLDS + position // folded + 1, block(position % folded)]
            for tap in range(taps - 1)
        ]
        late[:, here] = (ending[:, here] + jnp.concatenate([padding] + lines, axis=0)).astype(BF16)
    copy = pltpu.make_async_copy(late, grad_x.at[pl.ds(grad_x.shape[0] - rows, rows)], sem)
    copy.start()
    copy.wait()


def unpack_kernel(terms, taps, *refs):
    given, (cw, cb, dtb, al, sk, gain) = refs[:terms], refs[terms:]
    total = given[0][0:SMALL, :]
    for ref in given[1:]:
        total = total + ref[0:SMALL, :]
    width = cw.shape[1]
    cw[...] = total[0:taps, 0:width]
    cb[...] = total[taps, 0:width]
    gain[...] = total[taps + 1, 0 : gain.shape[0]]
    for number, ref in enumerate((dtb, al, sk)):
        ref[...] = total[taps + 2 : taps + 3, number * LANES : number * LANES + ref.shape[1]]


def add_kernel(*refs):
    *terms, back, out = refs
    total = terms[0][...]
    for ref in terms[1:]:
        total = total + ref[...]
    out[0:SMALL, :] = total
    out[SMALL:, :] = back[...]


def add_pair_kernel(own, other, out, alone):
    total = own[0:SMALL, :] + other[0:SMALL, :]
    out[0:SMALL, :] = total
    out[SMALL:, :] = other[SMALL:, :]
    alone[...] = total


def parts_of(message):
    end = message.shape[0] - DEC_ROWS
    return message[0:end, :].astype(F32), unpack_decays(message[end:, :])


def decayed(state, decay):
    group = state.shape[0] // N
    split_rows = state.reshape(group, N, LANES)
    return (split_rows * decay[0:group].reshape(group, 1, LANES)).reshape(state.shape)


def joined(first, second):
    state, decay = second
    return decayed(first[0], decay) + state, decay * first[1]


def store(out, value):
    state, decay = value
    end = state.shape[0]
    out[0:end, :] = state.astype(BF16)
    out[end:, :] = pack_decays(decay)


def ordered(later, a, b):
    return jnp.where(later, b, a), jnp.where(later, a, b)


def meet_kernel(reverse, mine, got, out, decay):
    later = here_at()[0] == (0 if reverse else 1)
    first, second = ordered(later, mine[...], got[...])
    whole = joined(parts_of(first), parts_of(second))
    store(out, whole)
    decay[...] = whole[1]


def join_kernel(first, second, out):
    store(out, joined(parts_of(first[...]), parts_of(second[...])))


def pass_kernel(before, own, decay, out):
    end = out.shape[0]
    state = decayed(before[0:end, :].astype(F32), decay[...])
    out[...] = (state + own[0:end, :].astype(F32)).astype(BF16)


def enter_kernel(reverse, *refs):
    given, (mine, got, own, send) = refs[:-4], refs[-4:]
    later = here_at()[0] == (0 if reverse else 1)
    end = own.shape[0]
    start = given[0][0:end, :].astype(F32)
    for ref in given[1:]:
        start = start + ref[0:end, :].astype(F32)
    state, decay = parts_of(ordered(later, mine[...], got[...])[0])
    after = decayed(start, decay) + state
    own[...] = jnp.where(later, after, start).astype(BF16)
    send[...] = jnp.where(later, start, after).astype(BF16)


def call(kernel, outs, args, scratch=(), megabytes=8, flops=0, name=None, fetched=(), aliases=None):
    specs = [
        pl.BlockSpec(
            memory_space=pltpu.HBM if number in fetched else pltpu.VMEM
        )
        for number in range(len(args))
    ]
    fetched_out = [out for given, out in (aliases or {}).items() if given in fetched]
    moved = sum(a.size * a.dtype.itemsize for a in args)
    moved += sum(o.size * o.dtype.itemsize for o in outs)
    return pl.pallas_call(
        kernel,
        out_shape=outs,
        in_specs=specs,
        out_specs=[
            pl.BlockSpec(memory_space=pltpu.HBM if number in fetched_out else pltpu.VMEM)
            for number in range(len(outs))
        ],
        input_output_aliases=aliases or {},
        scratch_shapes=list(scratch),
        compiler_params=pltpu.CompilerParams(vmem_limit_bytes=megabytes << 20),
        cost_estimate=pl.CostEstimate(flops=flops, bytes_accessed=moved, transcendentals=0),
        name=name,
    )(*args)


def like(shape, dtype=F32):
    return jax.ShapeDtypeStruct(shape, dtype)


def shift(value, axis, route):
    count = lax.axis_size(axis)
    pairs = [(i, route(i)) for i in range(count)]
    return lax.ppermute(value, axis, [(i, j) for i, j in pairs if 0 <= j < count])


def between_chips(value, routes):
    return shift(value, "seq", lambda i: 2 * routes[i // 2] + i % 2 if i // 2 in routes else -1)


def entering_states(own_states, got, reverse, beside):
    chips = lax.axis_size("seq") // 2
    message = like(got[0].shape, BF16)
    entry = like((got[0].shape[0] - DEC_ROWS, LANES), BF16)
    chip, decays, mine = [], [], []
    for stream, other in enumerate(got):
        mine.append(own_states(stream, chip))
        whole, decay = call(
            functools.partial(meet_kernel, reverse),
            [message, like((DEC_ROWS, LANES))],
            [mine[-1], other],
            name="meet",
        )
        chip.append(whole)
        decays.append(decay)
    if 1 < chips <= 4:
        order = list(range(chips))[::-1] if reverse else list(range(chips))
        arrived = [[] for _ in chip]
        moving = chip
        for hop in range(chips - 1):
            route = {order[hop]: order[hop + 1]}
            landed = [between_chips(part, route) for part in moving]
            if hop < len(beside):
                landed = beside[hop](moving, landed)
            for stream, part in zip(arrived, landed):
                stream.append(part)
            if hop < chips - 2:
                moving = [
                    call(pass_kernel, [entry], list(parts), name="pass")[0] for parts in zip(landed, chip, decays)
                ]
    else:
        sign = -1 if reverse else 1
        before = [shift(part, "seq", lambda i: i + 2 * sign) for part in chip]
        before = beside[1](chip, beside[0](chip, before))
        window = 1
        while window < chips - 1:
            distance = window + 1
            longer = [call(join_kernel, [message], pair, name="join")[0] for pair in zip(before, chip)]
            far = [shift(part, "seq", lambda i: i + 2 * distance * sign) for part in longer]
            before = [call(join_kernel, [message], pair, name="join")[0] for pair in zip(far, before)]
            window = 2 * window + 1
        arrived = [[part] for part in before]
    owns, others = [], []
    for parts, a, b in zip(arrived, mine, got):
        own, send = call(functools.partial(enter_kernel, reverse), [entry, entry], parts + [a, b], name="enter")
        owns.append(own)
        others.append(shift(send, "seq", lambda i: i ^ 1))
    return owns, others


def after(value, *signals):
    return lax.optimization_barrier((value, *signals))[0]


def shards(
    conv_input, gate_input, dt_raw, grad_output, conv_weight, conv_bias, dt_bias, a_log, skip, norm_gain
):
    gate, grad = gate_input[0], grad_output[0]
    dt = dt_raw[0].T
    length, channels = conv_input.shape[1:]
    features = gate.shape[1]
    heads = dt.shape[0]
    half = heads // 4
    taps, width = conv_weight.shape
    gain_width = norm_gain.shape[0]
    heads_here = dt_bias.shape[0]
    parts = lax.axis_size("fsdp")
    devices = lax.axis_size("seq")
    sizes = (width, gain_width, heads_here)
    piece_width = -(-width // LANES) * LANES
    full_width = placement(parts - 1, width)[0] + piece_width + LANES
    piece_like = like((SMALL, piece_width))
    shares = [
        conv_weight,
        conv_bias.reshape(1, -1),
        dt_bias.reshape(1, -1),
        a_log.reshape(1, -1),
        skip.reshape(1, -1),
        norm_gain,
    ]

    x = conv_input[0]
    halo, piece, own = call(
        open_kernel,
        [like((HALO, channels), BF16), piece_like, like((2 * SMALL, piece_width))],
        [x, dt] + shares,
        [pltpu.VMEM((2 * HALO, channels), BF16), pltpu.VMEM(dt.shape, F32)]
        + [pltpu.VMEM(share.shape, F32) for share in shares]
        + [pltpu.SemaphoreType.DMA((len(shares) + 2,))],
        fetched=range(len(shares) + 2),
        megabytes=60,
        name="open",
    )
    pieces = [shift(piece, "fsdp", lambda i: peer(i, distance, parts)) for distance in range(1, parts)]
    halo = shift(halo, "seq", lambda i: i + 1)
    lifted = jnp.pad(after(x, piece).astype(F32), ((HALO, 0), (0, 0)))

    group = half // STREAMS
    message = like((group * N + DEC_ROWS, LANES), BF16)
    entry = pltpu.VMEM((2 * STREAMS, group * N, LANES), BF16)
    wide = like((length, features))
    square = like((length, LANES))
    full, gain, small, cols, rows, decs = call(
        functools.partial(gather_kernel, taps, sizes, parts, length),
        [
            like((SMALL, full_width)),
            like((1, features)),
            like((8, LANES)),
            like((2, length, LANES)),
            like((3, LANES, length)),
            like((2 * STREAMS, DEC_ROWS, LANES), BF16),
        ],
        [own] + pieces,
        [pltpu.VMEM((LANES, LANES), F32), pltpu.VMEM((parts, SMALL, piece_width), F32)],
        name="gather",
    )
    conv_like = like((length, channels), BF16)
    padded, conv, write_t, other = call(
        functools.partial(front_kernel, taps),
        [like(lifted.shape), conv_like, like((N, length)), message],
        [lifted, halo, full, rows, decs],
        name="front",
        aliases={0: 0},
    )
    got = [shift(other, "seq", lambda i: i ^ 1)]
    for stream in range(1, STREAMS):
        conv, other = call(
            functools.partial(front_next_kernel, taps, False, (stream,)),
            [conv_like, message],
            [conv, padded, full, rows, decs, write_t],
            name="front",
            aliases={0: 0},
        )
        got.append(shift(other, "seq", lambda i: i ^ 1))
    held = [conv]

    def own_first(stream, signals):
        held[0], mine = call(
            functools.partial(front_next_kernel, taps, True, (stream,)),
            [conv_like, message],
            [after(held[0], *signals), padded, full, rows, decs, write_t],
            name="own",
            aliases={0: 0},
        )
        return mine

    work = {}

    def intra(signal, value):
        work["local"], work["slope"] = call(
            functools.partial(intra_kernel, taps),
            [wide, like((length, channels))],
            [padded, full, after(held[0], *signal), cols, rows, small],
            flops=2 * length * length * features,
            name="intra",
        )
        return [after(part, work["local"]) for part in value]

    def factors(signal, value):
        *work["factors"], work["picks"], work["shifted"] = call(
            factor_kernel,
            [wide] * 3 + [like((half * LANES, LANES), BF16), like((taps - 1, length, channels))],
            [after(cols, *signal), gate, grad, gain, padded],
            flops=length * features * 16,
            name="factors",
        )
        return [after(part, work["factors"][0]) for part in value]

    sums_like = like((2, length, LANES))

    entry_own, entry_got = entering_states(own_first, got, False, (intra, factors))
    conv = held[0]
    silus, grown, decays = work["factors"]
    given = [work["local"], conv, silus, grown, decays]
    mixed, gated, sums = call(mix_kernel, [wide, wide, sums_like], given + entry_own, name="mix")
    mixed, gated, stats, other = call(
        norm_kernel,
        [wide, wide, square, message],
        [mixed, gated] + given + [sums, decs] + entry_got,
        name="norm",
        aliases={0: 0, 1: 1},
    )
    got = [shift(other, "seq", lambda i: i ^ 1)]
    given = [conv, silus, grown, decays, gated, decs]

    def norm_next(own, stream, signals):
        return call(
            functools.partial(norm_next_kernel, own, (stream,)),
            [message],
            [after(stats, *signals)] + given,
            name="norm_next",
        )[0]

    for stream in range(1, STREAMS):
        got.append(shift(norm_next(False, stream, []), "seq", lambda i: i ^ 1))

    def gates(signal, value):
        work["gates"] = call(
            gate_kernel,
            [
                like((length, features), BF16),
                like((length, features)),
                like((length, LANES)),
                like((1, features)),
                like((8, LANES)),
                like((length, LANES)),
            ],
            [mixed, after(conv, *signal), cols, small, gate, grad, gain, stats] + entry_own + entry_got,
            [entry],
                flops=2 * length * length * features,
            name="gates",
        )
        return [after(part, work["gates"][0]) for part in value]

    def back(signal, value):
        grad_mixed, grad_read = work["gates"][1], work["gates"][5]
        work["back"] = call(
            back_kernel,
            [like((length, features)), like((length, LANES)), like((length, LANES))],
            [after(grad_mixed, *signal), conv, cols, rows, small, grad_read],
            flops=4 * length * length * features,
            name="back",
        )
        return [after(part, work["back"][0]) for part in value]

    shapes = [like((2 * HALO + length, channels)), like((SMALL, full_width)), square, like((8, LANES)), square]
    fixed = [padded, work["shifted"], conv, work["slope"], cols, work["picks"]]
    side = half * LANES
    scratch = [pltpu.VMEM((length, side), BF16)] * 2 + [pltpu.VMEM((N, side), BF16), pltpu.VMEM((8, side), F32)]

    leave_own, leave_got = entering_states(functools.partial(norm_next, True), got, True, (gates, back))
    grad_gate, _, out_sums, grad_gain, grad_small, _ = work["gates"]
    grad_values, in_sums, grad_vecs = work["back"]
    slopes, whole, *sums = call(
        functools.partial(close_own_kernel, taps),
        shapes,
        fixed + [grad_values] + entry_own + leave_own,
        scratch,
        name="close_own",
    )
    slopes, whole, grad_raw, *shares = call(
        functools.partial(close_kernel, taps, sizes),
        shapes[:2] + [square] + [piece_like] * parts,
        [slopes, whole] + fixed + [small, grad_values, grad_vecs, out_sums, in_sums, grad_gain, grad_small]
        + sums + entry_got + leave_got,
        [pltpu.VMEM((parts, SMALL, piece_width), F32)] + scratch,
        name="close",
        aliases={0: 0, 1: 1},
    )
    terms = [shares[0]]
    for distance in range(1, parts):
        terms.append(shift(shares[distance], "fsdp", lambda i: (i + distance) % parts))
    earlier = call(
        functools.partial(before_kernel, taps), [like((BACK_ROWS, piece_width))], [full, slopes], name="before"
    )[0]
    bundle = like((SMALL + BACK_ROWS, piece_width))
    total = call(add_kernel, [bundle], terms + [earlier], name="add")[0]
    partner = shift(total, "seq", lambda i: i ^ 1)
    total, alone = call(add_pair_kernel, [bundle, piece_like], [total, partner], name="add")
    chips = devices // 2
    behind = between_chips(total, {i: (i - 1) % chips for i in range(chips)})
    if chips <= 4:
        terms = [alone] + [
            between_chips(alone, {i: (i + distance) % chips for i in range(chips)})
            for distance in range(1, chips - 1)
        ]
        terms += [behind] if chips > 1 else []
    else:
        terms = [lax.psum(alone, "seq") * 0.5]
    grad_x, ending, grad_dt = call(
        functools.partial(input_kernel, taps),
        [like((length, channels), BF16), like((2 * HALO, channels)), like((heads, length))],
        [full, after(slopes, alone), grad_raw],
        flops=length * channels * 16,
        name="inputs",
    )
    grad_x = call(
        functools.partial(patch_kernel, chips, taps),
        [like((length, channels), BF16)],
        [grad_x, ending, partner, behind],
        [pltpu.VMEM((2 * HALO, channels), BF16), pltpu.SemaphoreType.DMA],
        fetched=(0,),
        aliases={0: 0},
        flops=length * channels * 8,
        name="patch",
    )[0]
    cw, cb, dtb, al, sk, gn = call(
        functools.partial(unpack_kernel, len(terms), taps),
        [
            like((taps, width)),
            like((width,)),
            like((1, heads_here)),
            like((1, heads_here)),
            like((1, heads_here)),
            like((gain_width,)),
        ],
        terms,
        name="unpack",
    )
    return (
        grad_x[None],
        grad_gate[None],
        grad_dt.T[None],
        cw,
        cb,
        dtb.reshape(-1),
        al.reshape(-1),
        sk.reshape(-1),
        gn,
    )


def solution(mesh):
    tokens = P("fsdp", "seq", None)
    in_specs = (tokens,) * 4 + (P(None, "fsdp"),) + (P("fsdp"),) * 5
    out_specs = (tokens,) * 3 + (P(None, "fsdp"),) + (P("fsdp"),) * 5
    return jax.shard_map(shards, mesh=mesh, in_specs=in_specs, out_specs=out_specs, check_vma=False)
```

```python
import functools

import jax
import jax.numpy as jnp
from jax import lax
from jax.experimental import pallas as pl
from jax.experimental.pallas import tpu as pltpu
from jax.sharding import PartitionSpec as P

P_SIZE = 64
N = 64
EPS = 1e-05
LANES = 2 * P_SIZE
HALO = 8
SMALL = 8
STREAMS = 2
FOLDS = 4
BACK_ROWS = 16
DEC_ROWS = 16
F32, BF16 = jnp.float32, jnp.bfloat16


def dot(a, b, over=(1, 0)):
    return lax.dot_general(
        a, b, (((over[0],), (over[1],)), ((), ())), preferred_element_type=F32
    )


def here_at():
    index = lax.axis_index("seq")
    return lax.rem(index, 2), lax.div(index, 2), lax.axis_index("fsdp")


def iota(shape, axis):
    return lax.broadcasted_iota(jnp.int32, shape, axis)


def sigmoid(x):
    return 0.5 * jnp.tanh(0.5 * x) + 0.5


def split(x):
    high = x.astype(BF16)
    return high, (x - high.astype(F32)).astype(BF16)


def dot_parts(ones, value, parts):
    pieces = []
    for _ in range(parts):
        piece = value.astype(BF16)
        pieces.append(piece)
        value = value - piece.astype(F32)
    ones = ones.astype(BF16)
    return dot(jnp.concatenate([ones] * parts, axis=1), jnp.concatenate(pieces, axis=0))


def block(position):
    return slice(position * LANES, (position + 1) * LANES)


def by_head(columns, pair, shape):
    first = jnp.broadcast_to(columns[:, 2 * pair : 2 * pair + 1], shape)
    second = jnp.broadcast_to(columns[:, 2 * pair + 1 : 2 * pair + 2], shape)
    return jnp.where(iota(shape, 1) < P_SIZE, first, second)


def apart(pair_block):
    first = iota(pair_block.shape, 1) < P_SIZE
    zero = jnp.zeros_like(pair_block)
    return jnp.concatenate(
        [jnp.where(first, pair_block, zero), jnp.where(first, zero, pair_block)], axis=0
    )


def head_sums(product, pair, parts=2):
    shape = (LANES, LANES)
    pick = (iota(shape, 1) == 2 * pair + (iota(shape, 0) >= P_SIZE).astype(jnp.int32)).astype(BF16)
    if parts == 1:
        return dot(product.astype(BF16), pick)
    high, low = split(product)
    return dot(jnp.concatenate([high, low], axis=1), jnp.concatenate([pick, pick], axis=0))


def before_silu(rows, full, cols, taps, length):
    start = HALO - (taps - 1)
    total = full[taps : taps + 1, cols] + full[0:1, cols] * rows[start : start + length, cols]
    for tap in range(1, taps):
        total = total + full[tap : tap + 1, cols] * rows[start + tap : start + tap + length, cols]
    return total


def open_kernel(x, dt, cw, cb, dtb, al, sk, gain, halo, out, own, late, raw, *rest):
    held, sems = rest[:-1], rest[-1]
    ending = x.at[pl.ds(x.shape[0] - late.shape[0], late.shape[0])]
    copies = [
        pltpu.make_async_copy(source, target, sems.at[number])
        for number, (source, target) in enumerate(
            zip((cw, cb, dtb, al, sk, gain, dt, ending), held + (raw, late))
        )
    ]
    for copy in copies:
        copy.start()
    out[...] = jnp.zeros_like(out)
    for copy in copies:
        copy.wait()
    halo[...] = late[...].astype(F32)[HALO:].astype(BF16)
    cw, cb, dtb, al, sk, gain = held
    taps, width = cw.shape
    out[0:taps, 0:width] = cw[...]
    out[taps : taps + 1, 0:width] = cb[...]
    out[taps + 1 : taps + 2, 0 : gain.shape[0]] = gain[...].reshape(1, -1)
    for number, ref in enumerate((dtb, al, sk)):
        out[taps + 2 : taps + 3, number * LANES : number * LANES + ref.shape[1]] = ref[...]
    own[0:SMALL, :] = out[...]
    own[SMALL:, :] = jnp.zeros((SMALL, own.shape[1]), F32)
    for group in range(raw.shape[0] // SMALL):
        own[SMALL:, block(group)] = raw[group * SMALL : (group + 1) * SMALL, :]


def peer(position, distance, parts):
    if parts & (parts - 1) == 0:
        return position ^ distance
    return (position + distance) % parts


def peer_back(position, distance, parts):
    if parts & (parts - 1) == 0:
        return position ^ distance
    return lax.rem(position + parts - distance, parts)


def placement(position, width):
    start = position * width
    base = start // LANES * LANES
    return base, start - base


def put_state(states, pair, value):
    states[pair * N : (pair + 1) * N, :] = value


def get_state(states, pair):
    return states[pair * N : (pair + 1) * N, :]


def pack_decays(decays):
    high, low = split(decays)
    group = iota(decays.shape, 1) // (P_SIZE // 2)
    return jnp.where(lax.rem(group, 2) == 0, high.astype(F32), low.astype(F32)).astype(BF16)


def unpack_decays(packed):
    value = packed.astype(F32)
    group = iota(value.shape, 1) // (P_SIZE // 2)
    ahead = pltpu.roll(value, LANES - P_SIZE // 2, 1)
    behind = pltpu.roll(value, P_SIZE // 2, 1)
    return value + jnp.where(lax.rem(group, 2) == 0, ahead, behind)


def gather_kernel(taps, sizes, parts, length, own, *refs):
    given, refs = refs[: parts - 1], refs[parts - 1 :]
    full, gain, small, cols, rows_out, decs, wide, pieces = refs
    mine_at = here_at()[2]
    piece_width = pieces.shape[2]
    pieces[mine_at] = own[0:SMALL, :]
    for distance in range(1, parts):
        pieces[peer_back(mine_at, distance, parts)] = given[distance - 1][...]
    width, gain_width, heads_here = sizes
    heads = heads_here * parts
    half = heads // 4
    full[...] = jnp.zeros_like(full)
    small[...] = jnp.zeros_like(small)
    wide[...] = jnp.zeros_like(wide)
    for group in range(heads // SMALL):
        wide[group * SMALL : (group + 1) * SMALL, :] = own[SMALL:, block(group)]
    for part in range(parts):
        base, shift = placement(part, width)
        piece = jnp.concatenate([pieces[part], jnp.zeros((SMALL, LANES), F32)], axis=1)
        if shift:
            piece = pltpu.roll(piece, shift, 1)
        full[:, base : base + piece_width + LANES] += piece
        gain[:, part * gain_width : (part + 1) * gain_width] = pieces[
            part, taps + 1 : taps + 2, 0:gain_width
        ]
        for number in range(3):
            row = pieces[part, taps + 2 : taps + 3, block(number)]
            if part:
                row = pltpu.roll(row, part * heads_here, 1)
            small[number : number + 1, :] += row
    raw = wide[...].T + small[0:1, :]
    step = jnp.maximum(raw, 0.0) + jnp.log1p(jnp.exp(-jnp.abs(raw)))
    logs = -jnp.exp(small[1:2, :]) * step
    square = (length, length)
    lower = iota(square, 0) >= iota(square, 1)
    running = dot_parts(lower, logs, 3)
    running_t = running.T
    step_t = step.T
    last = jnp.broadcast_to(running_t[:, length - 1 : length], running_t.shape)
    cols[0] = step
    cols[1] = running
    rows_out[0] = step_t
    rows_out[1] = running_t
    rows_out[2] = jnp.exp(last - running_t) * step_t
    wide[...] = jnp.exp(last)[:, 0:LANES]
    group = half // STREAMS
    first = iota((group, LANES), 1) < P_SIZE
    for number in range(2 * STREAMS):
        even = wide[pl.ds(2 * group * number, group, stride=2), :]
        odd = wide[pl.ds(2 * group * number + 1, group, stride=2), :]
        decays = jnp.where(first, even, odd)
        decs[number] = pack_decays(
            jnp.concatenate([decays, jnp.zeros((DEC_ROWS - group, LANES), F32)], axis=0)
        )


def side_block(pair):
    return pl.ds(pl.multiple_of(pair * LANES, LANES), LANES)


def front_group(taps, number, rows, full, tails, decs, write_t, conv, out):
    length = conv.shape[0]
    group = (out.shape[0] - DEC_ROWS) // N
    scale = tails[2, pl.ds(number * 2 * group, 2 * group), :]
    for pair in range(group):
        here = side_block(number * group + pair)
        pre = before_silu(rows, full, here, taps, length)
        value = (pre * sigmoid(pre)).astype(BF16)
        conv[:, here] = value
        scaled = jnp.concatenate(
            [
                (write_t * scale[2 * pair + which : 2 * pair + which + 1, :]).astype(BF16)
                for which in range(2)
            ],
            axis=1,
        )
        put_state(out, pair, dot(scaled, apart(value)).astype(BF16))
    out[group * N :, :] = decs[number]


def front_kernel(taps, lifted, halo, full, tails, decs, rows, conv, write_out, out):
    length, channels = conv.shape
    rows[0:HALO, :] = halo[...].astype(F32)
    here = block(channels // LANES - 1)
    pre = before_silu(rows, full, here, taps, length)
    vectors = (pre * sigmoid(pre)).astype(BF16)
    conv[:, here] = vectors
    write_t = vectors.astype(F32).T[0:N, :]
    write_out[...] = write_t
    front_group(taps, group_at(False, 0), rows, full, tails, decs, write_t, conv, out)


def group_at(own, stream):
    core = here_at()[0]
    return (core if own else 1 - core) * STREAMS + stream


def front_next_kernel(taps, own, streams, conv_in, rows, full, tails, decs, write_t, conv, *outs):
    for stream, out in zip(streams, outs):
        front_group(taps, group_at(own, stream), rows, full, tails, decs, write_t[...], conv, out)


def head_weights(cols, rows_ref, head, causal, scores):
    gap = cols[1, :, head : head + 1] - rows_ref[1, head : head + 1, :]
    scaled = jnp.exp(jnp.where(causal, gap, -1e30)) * rows_ref[0, head : head + 1, :]
    return scaled, (scaled * scores).astype(BF16)


def factor_kernel(cols, gate, grad, gain, rows, silus, grown, decays, picks, shifted):
    length, features = gate.shape
    taps = shifted.shape[0] + 1
    for tap in range(taps - 1):
        start = HALO - taps + 1 + tap
        shifted[tap] = rows[start : start + length, :]
    decay = jnp.exp(cols[1])
    picks[...] = (iota(picks.shape, 1) == iota(picks.shape, 0) // P_SIZE).astype(BF16)
    for pair in range(features // LANES):
        here = block(pair)
        z = gate[:, here].astype(F32)
        silus[:, here] = z * sigmoid(z)
        grown[:, here] = grad[:, here].astype(F32) * gain[:, here]
        decays[:, here] = by_head(decay, pair, (length, LANES))


def intra_kernel(taps, rows, full, conv, cols, rows_ref, small, local, slope):
    length, channels = conv.shape
    features = local.shape[1]
    pairs = features // LANES
    write = conv[:, features : features + N]
    read = conv[:, features + N : features + 2 * N]
    scores = dot(read, write, (1, 1))
    square = (length, length)
    causal = iota(square, 0) >= iota(square, 1)
    for pair in range(pairs):
        weights = jnp.concatenate(
            [head_weights(cols, rows_ref, 2 * pair + which, causal, scores)[1] for which in range(2)],
            axis=1,
        )
        values = conv[:, block(pair)]
        skip = by_head(small[2:3, :], pair, (1, LANES))
        here = block(pair)
        local[:, here] = dot(weights, apart(values)) + skip * values.astype(F32)
    for position in range(channels // LANES):
        here = block(position)
        pre = before_silu(rows, full, here, taps, length)
        gate = sigmoid(pre)
        slope[:, here] = gate * (1.0 + pre * (1.0 - gate))


def mix_groups(groups, local, conv, silus, grown, decays, entries, mixed, gated):
    length, features = local.shape
    shape = (length, LANES)
    read = conv[:, features + N : features + 2 * N]
    square_sum = jnp.zeros(shape, F32)
    cross_sum = jnp.zeros(shape, F32)
    for (own, stream), entry in zip(groups, entries):
        number = group_at(own, stream)
        group = entry.shape[0] // N
        for pair in range(group):
            here = side_block(number * group + pair)
            carried = dot(read, get_state(entry, pair))
            mix = local[:, here] + decays[:, here] * carried
            mixed[:, here] = mix
            product = mix * silus[:, here]
            gated[:, here] = product
            square_sum += product * product
            cross_sum += product * grown[:, here]
    return square_sum, cross_sum


def mix_kernel(groups, local, conv, silus, grown, decays, *refs):
    entries, (mixed, gated, sums) = refs[:-3], refs[-3:]
    square, cross = mix_groups(groups, local, conv, silus, grown, decays, entries, mixed, gated)
    sums[0] = square
    sums[1] = cross


def back_state(number, stats, conv, silus, grown, decays, gated, decs, out):
    length, features = gated.shape
    group = (out.shape[0] - DEC_ROWS) // N
    shape = (length, LANES)
    read = conv[:, features + N : features + 2 * N]
    scale = jnp.broadcast_to(stats[:, 0:1], shape)
    factor = jnp.broadcast_to(stats[:, 1:2], shape)
    for pair in range(group):
        here = side_block(number * group + pair)
        grad_gated = scale * grown[:, here] - factor * gated[:, here]
        weighted = decays[:, here] * (grad_gated * silus[:, here])
        put_state(out, pair, dot(read, weighted.astype(BF16), (0, 0)).astype(BF16))
    out[group * N :, :] = decs[number]


def norm_kernel(mixed_in, gated_in, local, conv, silus, grown, decays, sums, decs, *refs):
    entry, mixed, gated, stats, out = refs
    length, features = local.shape
    groups = [(False, STREAMS - 1)]
    square, cross = mix_groups(groups, local, conv, silus, grown, decays, [entry], mixed, gated)
    square = jnp.sum(square + sums[0], axis=1, keepdims=True)
    cross = jnp.sum(cross + sums[1], axis=1, keepdims=True)
    scale = lax.rsqrt(square * (1.0 / features) + EPS)
    factor = scale * scale * scale * cross * (1.0 / features)
    lane = iota((length, LANES), 1)
    values = jnp.where(lane == 0, scale, jnp.where(lane == 1, factor, 0.0))
    stats[...] = values
    back_state(group_at(False, 0), values, conv, silus, grown, decays, gated, decs, out)


def norm_next_kernel(own, streams, stats, conv, silus, grown, decays, gated, decs, *outs):
    for stream, out in zip(streams, outs):
        back_state(group_at(own, stream), stats[...], conv, silus, grown, decays, gated, decs, out)


def gate_kernel(
    mixed, conv, cols, small, gate, grad, gain, stats, *refs
):
    given, refs = refs[: 2 * STREAMS], refs[2 * STREAMS :]
    grad_gate, grad_mixed, sums, grad_gain, grad_small, grad_read, entry = refs
    length, features = mixed.shape
    pairs = features // LANES
    group = pairs // (2 * STREAMS)
    shape = (length, LANES)
    for number, ref in enumerate(given):
        entry[group_at(number < STREAMS, number % STREAMS)] = ref[...]
    scale = jnp.broadcast_to(stats[:, 0:1], shape)
    factor = jnp.broadcast_to(stats[:, 1:2], shape)
    decay = jnp.exp(cols[1])
    read_grad = jnp.zeros((length, N), F32)
    out_sums = jnp.zeros(shape, F32)
    skip_sums = jnp.zeros(shape, F32)
    for pair in range(pairs):
        here = block(pair)
        z = gate[:, here].astype(F32)
        sig = sigmoid(z)
        silu = z * sig
        mix = mixed[:, here]
        product = mix * silu
        grads = grad[:, here].astype(F32)
        grad_gain[:, here] = jnp.sum(grads * (product * scale), axis=0, keepdims=True)
        grad_gated = scale * (grads * gain[:, here]) - factor * product
        grad_mix = grad_gated * silu
        grad_mixed[:, here] = grad_mix
        grad_gate[:, here] = (grad_gated * mix * (sig * (1.0 + z * (1.0 - sig)))).astype(BF16)
        values = conv[:, here].astype(F32)
        skip = by_head(small[2:3, :], pair, (1, LANES))
        rounded = grad_mix.astype(BF16).astype(F32)
        out_sums += head_sums(rounded * (mix - skip * values), pair)
        skip_sums += head_sums(grad_mix * values, pair)
        weighted = (by_head(decay, pair, shape) * grad_mix).astype(BF16)
        read_grad += dot(weighted, get_state(entry.at[pair // group], pair % group), (1, 1))
    sums[...] = out_sums
    grad_read[...] = jnp.concatenate([jnp.zeros_like(read_grad), read_grad], axis=1)
    grad_small[...] = jnp.zeros_like(grad_small)
    grad_small[2:3, :] = jnp.sum(skip_sums, axis=0, keepdims=True)


def back_kernel(grad_mixed, conv, cols, rows_ref, small, grad_read, grad_values, sums, grad_vecs):
    length, features = grad_mixed.shape
    pairs = features // LANES
    shape = (length, LANES)
    write = conv[:, features : features + N]
    read = conv[:, features + N : features + 2 * N]
    scores = dot(read, write, (1, 1))
    square = (length, length)
    causal = iota(square, 0) >= iota(square, 1)
    score_grad = jnp.zeros(square, F32)
    in_sums = jnp.zeros(shape, F32)
    first = iota(shape, 1) < P_SIZE
    for pair in range(pairs):
        here = block(pair)
        grad_mix = grad_mixed[:, here]
        values = conv[:, here]
        rounded = grad_mix.astype(BF16)
        scaled = [head_weights(cols, rows_ref, 2 * pair + which, causal, scores) for which in range(2)]
        weight_grad = dot(rounded, apart(values), (1, 1))
        score_grad += weight_grad[:, 0:length] * scaled[0][0] + weight_grad[:, length:] * scaled[1][0]
        both = dot(jnp.concatenate([scaled[0][1], scaled[1][1]], axis=1), rounded, (0, 0))
        value_grad = jnp.where(first, both[0:length], both[length:])
        in_sums += head_sums(values.astype(F32) * value_grad, pair)
        skip = by_head(small[2:3, :], pair, (1, LANES))
        grad_values[:, here] = value_grad + skip * grad_mix
    sums[...] = in_sums
    high, low = split(score_grad)
    read_grad = dot(high, write) + dot(low, write)
    write_grad = dot(high, read, (0, 0)) + dot(low, read, (0, 0))
    grad_vecs[...] = grad_read[...] + jnp.concatenate([write_grad, read_grad], axis=1)


def through_taps(taps, full, slopes, cols, start, count):
    total = full[0:1, cols] * slopes[start + taps - 1 : start + taps - 1 + count, cols]
    for tap in range(1, taps):
        ahead = start + taps - 1 - tap
        total = total + full[tap : tap + 1, cols] * slopes[ahead : ahead + count, cols]
    return total


def through_conv(taps, here, grad_out, rows, shifted, slope, slopes, whole):
    length = grad_out.shape[0]
    grad_pre = grad_out.astype(BF16).astype(F32) * slope[:, here]
    slopes[HALO : HALO + length, here] = grad_pre
    for tap in range(taps):
        given = shifted[tap, :, here] if tap < taps - 1 else rows[HALO : HALO + length, here]
        whole[tap : tap + 1, here] = jnp.sum(grad_pre * given, axis=0, keepdims=True)
    whole[taps : taps + 1, here] = jnp.sum(grad_pre, axis=0, keepdims=True)


def close_side(taps, own, rows, shifted, conv, slope, cols, picks, entries, leaves, grad_values, slopes, whole, scratch):
    products, holds, leavings, overlaps = scratch
    length, features = grad_values.shape
    half = features // LANES // 2
    group = half // STREAMS
    shape = (length, LANES)
    side = here_at()[0] if own else 1 - here_at()[0]
    write = conv[:, features : features + N]
    running = cols[1]
    tail = jnp.exp(running[length - 1 : length, :] - running) * cols[0]
    tail = pltpu.roll(tail, lax.rem(LANES - 2 * half * side, LANES), 1)
    for pair in range(half):
        here = side_block(side * half + pair)
        local = block(pair)
        leaving = get_state(leaves[pair // group], pair % group)
        values = conv[:, here].astype(F32)
        tail_wide = by_head(tail, pair, shape)
        state_grad = tail_wide * dot(write, leaving)
        products[:, local] = (values * state_grad).astype(BF16)
        holds[:, local] = (tail_wide * values).astype(BF16)
        leavings[:, local] = leaving
        entering = get_state(entries[pair // group], pair % group).astype(F32)
        overlap = jnp.sum(leaving.astype(F32) * entering, axis=0, keepdims=True)
        overlaps[:, local] = jnp.broadcast_to(overlap, (8, LANES))
        through_conv(taps, here, grad_values[:, here] + state_grad, rows, shifted, slope, slopes, whole)
    back = 2 * half * side
    choose = picks[...]
    state_sums = dot(products[...], choose)
    high, low = split(overlaps[...])
    end_sums = dot(high, choose) + dot(low, choose)
    write_grad = dot(holds[...], leavings[...], (1, 1))
    write_grad = jnp.concatenate([write_grad, jnp.zeros_like(write_grad)], axis=1)
    return pltpu.roll(state_sums, back, 1), pltpu.roll(end_sums, back, 1), write_grad


def close_own_kernel(taps, rows, shifted, conv, slope, cols, picks, grad_values, *refs):
    given, (slopes, whole, state_out, end_out, write_out, *scratch) = refs[: 2 * STREAMS], refs[2 * STREAMS :]
    length, channels = conv.shape
    slopes[0:HALO, :] = jnp.zeros((HALO, channels), F32)
    slopes[HALO + length :, :] = jnp.zeros((HALO, channels), F32)
    whole[...] = jnp.zeros_like(whole)
    state_out[...], end_out[...], write_out[...] = close_side(
        taps, True, rows, shifted, conv, slope, cols, picks, given[:STREAMS], given[STREAMS:], grad_values, slopes, whole, scratch
    )


def close_kernel(
    taps, sizes, slopes_in, whole_in, rows, shifted, conv, slope, cols, picks, small, grad_values, grad_vecs, out_sums, in_sums,
    grad_gain, grad_small, state_in, end_in, write_in, *rest
):
    given, rest, scratch = rest[: 2 * STREAMS], rest[2 * STREAMS : -4], rest[-4:]
    slopes, whole, grad_raw, *outs, cut = rest
    parts = len(outs)
    position_here = here_at()[2]
    length, channels = conv.shape
    width, gain_width, heads_here = sizes
    step = cols[0]
    last = cols[1, length - 1 : length, :]
    state_sums, end_sums, write_grad = close_side(
        taps, False, rows, shifted, conv, slope, cols, picks, given[:STREAMS], given[STREAMS:], grad_values, slopes, whole, scratch
    )
    state_sums = state_sums + state_in[...]
    end_sums = end_sums + end_in[...]
    vecs = grad_vecs[...] + (write_in[...] + write_grad)
    through_conv(taps, block(channels // LANES - 1), vecs, rows, shifted, slope, slopes, whole)

    into = in_sums[...] + state_sums
    change = out_sums[...] - into
    end_grad = jnp.sum(state_sums, axis=0, keepdims=True) + jnp.exp(last) * end_sums[0:1, :]
    square = (length, length)
    upper = iota(square, 0) <= iota(square, 1)
    log_grad = dot_parts(upper, change, 2) + end_grad
    rate = jnp.exp(small[1:2, :])
    raw_grad = (into / step - rate * log_grad) * (1.0 - jnp.exp(-step))
    grad_raw[...] = raw_grad
    vectors = (
        jnp.sum(raw_grad, axis=0, keepdims=True),
        jnp.sum(-rate * step * log_grad, axis=0, keepdims=True),
        grad_small[2:3, :],
    )
    piece_width = cut.shape[2]
    for part in range(parts):
        base, shift = placement(part, width)
        piece = whole[:, base : base + piece_width + LANES]
        if shift:
            piece = pltpu.roll(piece, piece_width + LANES - shift, 1)
        cut[part] = piece[:, 0:piece_width]
        cut[part, taps + 1 : taps + 2, 0:gain_width] = grad_gain[:, part * gain_width : (part + 1) * gain_width]
        for number, vector in enumerate(vectors):
            row = pltpu.roll(vector, LANES - part * heads_here, 1) if part else vector
            cut[part, taps + 2 : taps + 3, block(number)] = row
    for distance in range(parts):
        outs[distance][...] = cut[lax.rem(position_here + distance, parts)]


def input_kernel(taps, full, slopes, grad_raw, grad_x, ending, grad_dt):
    grad_dt[...] = grad_raw[...].T[0 : grad_dt.shape[0], :]
    length, channels = grad_x.shape
    for position in range(channels // LANES):
        here = block(position)
        total = through_taps(taps, full, slopes, here, HALO, length)
        grad_x[:, here] = total.astype(BF16)
        ending[:, here] = total[length - 2 * HALO :]


def before_kernel(taps, full, slopes, back):
    channels = slopes.shape[1]
    folded = back.shape[1] // LANES
    back[...] = jnp.zeros_like(back)
    for position in range(channels // LANES):
        here = block(position)
        ahead = through_taps(taps, full, slopes, here, 0, HALO)
        for tap in range(taps - 1):
            at = tap * FOLDS + position // folded
            back[at : at + 1, block(position % folded)] = ahead[HALO - taps + 1 + tap : HALO - taps + 2 + tap]


def patch_kernel(chips, taps, grad_in, ending, from_core, from_chip, grad_x, late, sem):
    core, chip, _ = here_at()
    rows = late.shape[0]
    channels = ending.shape[1]
    folded = from_core.shape[1] // LANES
    inside = core == 0
    later = jnp.where(inside, from_core[SMALL:, :], from_chip[SMALL:, :])
    later = jnp.where(jnp.logical_or(inside, chip < chips - 1), later, 0.0)
    padding = jnp.zeros((rows - taps + 1, LANES), F32)
    for position in range(channels // LANES):
        here = block(position)
        lines = [
            later[tap * FOLDS + position // folded : tap * FOLDS + position // folded + 1, block(position % folded)]
            for tap in range(taps - 1)
        ]
        late[:, here] = (ending[:, here] + jnp.concatenate([padding] + lines, axis=0)).astype(BF16)
    copy = pltpu.make_async_copy(late, grad_x.at[pl.ds(grad_x.shape[0] - rows, rows)], sem)
    copy.start()
    copy.wait()


def unpack_kernel(terms, taps, *refs):
    given, (cw, cb, dtb, al, sk, gain) = refs[:terms], refs[terms:]
    total = given[0][0:SMALL, :]
    for ref in given[1:]:
        total = total + ref[0:SMALL, :]
    width = cw.shape[1]
    cw[...] = total[0:taps, 0:width]
    cb[...] = total[taps, 0:width]
    gain[...] = total[taps + 1, 0 : gain.shape[0]]
    for number, ref in enumerate((dtb, al, sk)):
        ref[...] = total[taps + 2 : taps + 3, number * LANES : number * LANES + ref.shape[1]]


def add_kernel(*refs):
    *terms, back, out = refs
    total = terms[0][...]
    for ref in terms[1:]:
        total = total + ref[...]
    out[0:SMALL, :] = total
    out[SMALL:, :] = back[...]


def add_pair_kernel(own, other, out, alone):
    total = own[0:SMALL, :] + other[0:SMALL, :]
    out[0:SMALL, :] = total
    out[SMALL:, :] = other[SMALL:, :]
    alone[...] = total


def parts_of(message):
    end = message.shape[0] - DEC_ROWS
    return message[0:end, :].astype(F32), unpack_decays(message[end:, :])


def decayed(state, decay):
    group = state.shape[0] // N
    split_rows = state.reshape(group, N, LANES)
    return (split_rows * decay[0:group].reshape(group, 1, LANES)).reshape(state.shape)


def joined(first, second):
    state, decay = second
    return decayed(first[0], decay) + state, decay * first[1]


def store(out, value):
    state, decay = value
    end = state.shape[0]
    out[0:end, :] = state.astype(BF16)
    out[end:, :] = pack_decays(decay)


def ordered(later, a, b):
    return jnp.where(later, b, a), jnp.where(later, a, b)


def meet_kernel(reverse, mine, got, out, decay):
    later = here_at()[0] == (0 if reverse else 1)
    first, second = ordered(later, mine[...], got[...])
    whole = joined(parts_of(first), parts_of(second))
    store(out, whole)
    decay[...] = whole[1]


def join_kernel(first, second, out):
    store(out, joined(parts_of(first[...]), parts_of(second[...])))


def pass_kernel(before, own, decay, out):
    end = out.shape[0]
    state = decayed(before[0:end, :].astype(F32), decay[...])
    out[...] = (state + own[0:end, :].astype(F32)).astype(BF16)


def enter_kernel(reverse, *refs):
    given, (mine, got, own, send) = refs[:-4], refs[-4:]
    later = here_at()[0] == (0 if reverse else 1)
    end = own.shape[0]
    start = given[0][0:end, :].astype(F32)
    for ref in given[1:]:
        start = start + ref[0:end, :].astype(F32)
    state, decay = parts_of(ordered(later, mine[...], got[...])[0])
    after = decayed(start, decay) + state
    own[...] = jnp.where(later, after, start).astype(BF16)
    send[...] = jnp.where(later, start, after).astype(BF16)


def call(kernel, outs, args, scratch=(), megabytes=8, flops=0, name=None, fetched=(), aliases=None):
    specs = [
        pl.BlockSpec(
            memory_space=pltpu.HBM if number in fetched else pltpu.VMEM
        )
        for number in range(len(args))
    ]
    fetched_out = [out for given, out in (aliases or {}).items() if given in fetched]
    moved = sum(a.size * a.dtype.itemsize for a in args)
    moved += sum(o.size * o.dtype.itemsize for o in outs)
    return pl.pallas_call(
        kernel,
        out_shape=outs,
        in_specs=specs,
        out_specs=[
            pl.BlockSpec(memory_space=pltpu.HBM if number in fetched_out else pltpu.VMEM)
            for number in range(len(outs))
        ],
        input_output_aliases=aliases or {},
        scratch_shapes=list(scratch),
        compiler_params=pltpu.CompilerParams(vmem_limit_bytes=megabytes << 20),
        cost_estimate=pl.CostEstimate(flops=flops, bytes_accessed=moved, transcendentals=0),
        name=name,
    )(*args)


def like(shape, dtype=F32):
    return jax.ShapeDtypeStruct(shape, dtype)


def shift(value, axis, route):
    count = lax.axis_size(axis)
    pairs = [(i, route(i)) for i in range(count)]
    return lax.ppermute(value, axis, [(i, j) for i, j in pairs if 0 <= j < count])


def between_chips(value, routes):
    return shift(value, "seq", lambda i: 2 * routes[i // 2] + i % 2 if i // 2 in routes else -1)


def entering_states(own_states, got, reverse, beside):
    chips = lax.axis_size("seq") // 2
    message = like(got[0].shape, BF16)
    entry = like((got[0].shape[0] - DEC_ROWS, LANES), BF16)
    chip, decays, mine = [], [], []
    for stream, other in enumerate(got):
        mine.append(own_states(stream, chip))
        whole, decay = call(
            functools.partial(meet_kernel, reverse),
            [message, like((DEC_ROWS, LANES))],
            [mine[-1], other],
            name="meet",
        )
        chip.append(whole)
        decays.append(decay)
    if 1 < chips <= 4:
        order = list(range(chips))[::-1] if reverse else list(range(chips))
        arrived = [[] for _ in chip]
        moving = chip
        for hop in range(chips - 1):
            route = {order[hop]: order[hop + 1]}
            landed = [between_chips(part, route) for part in moving]
            if hop < len(beside):
                landed = beside[hop](moving, landed)
            for stream, part in zip(arrived, landed):
                stream.append(part)
            if hop < chips - 2:
                moving = [
                    call(pass_kernel, [entry], list(parts), name="pass")[0] for parts in zip(landed, chip, decays)
                ]
    else:
        sign = -1 if reverse else 1
        before = [shift(part, "seq", lambda i: i + 2 * sign) for part in chip]
        before = beside[1](chip, beside[0](chip, before))
        window = 1
        while window < chips - 1:
            distance = window + 1
            longer = [call(join_kernel, [message], pair, name="join")[0] for pair in zip(before, chip)]
            far = [shift(part, "seq", lambda i: i + 2 * distance * sign) for part in longer]
            before = [call(join_kernel, [message], pair, name="join")[0] for pair in zip(far, before)]
            window = 2 * window + 1
        arrived = [[part] for part in before]
    owns, others = [], []
    for parts, a, b in zip(arrived, mine, got):
        own, send = call(functools.partial(enter_kernel, reverse), [entry, entry], parts + [a, b], name="enter")
        owns.append(own)
        others.append(shift(send, "seq", lambda i: i ^ 1))
    return owns, others


def after(value, *signals):
    return lax.optimization_barrier((value, *signals))[0]


def shards(
    conv_input, gate_input, dt_raw, grad_output, conv_weight, conv_bias, dt_bias, a_log, skip, norm_gain
):
    gate, grad = gate_input[0], grad_output[0]
    dt = dt_raw[0].T
    length, channels = conv_input.shape[1:]
    features = gate.shape[1]
    heads = dt.shape[0]
    half = heads // 4
    taps, width = conv_weight.shape
    gain_width = norm_gain.shape[0]
    heads_here = dt_bias.shape[0]
    parts = lax.axis_size("fsdp")
    devices = lax.axis_size("seq")
    sizes = (width, gain_width, heads_here)
    piece_width = -(-width // LANES) * LANES
    full_width = placement(parts - 1, width)[0] + piece_width + LANES
    piece_like = like((SMALL, piece_width))
    shares = [
        conv_weight,
        conv_bias.reshape(1, -1),
        dt_bias.reshape(1, -1),
        a_log.reshape(1, -1),
        skip.reshape(1, -1),
        norm_gain,
    ]

    x = conv_input[0]
    halo, piece, own = call(
        open_kernel,
        [like((HALO, channels), BF16), piece_like, like((2 * SMALL, piece_width))],
        [x, dt] + shares,
        [pltpu.VMEM((2 * HALO, channels), BF16), pltpu.VMEM(dt.shape, F32)]
        + [pltpu.VMEM(share.shape, F32) for share in shares]
        + [pltpu.SemaphoreType.DMA((len(shares) + 2,))],
        fetched=range(len(shares) + 2),
        megabytes=60,
        name="open",
    )
    pieces = [shift(piece, "fsdp", lambda i: peer(i, distance, parts)) for distance in range(1, parts)]
    halo = shift(halo, "seq", lambda i: i + 1)
    lifted = jnp.pad(after(x, piece).astype(F32), ((HALO, 0), (0, 0)))

    group = half // STREAMS
    message = like((group * N + DEC_ROWS, LANES), BF16)
    entry = pltpu.VMEM((2 * STREAMS, group * N, LANES), BF16)
    wide = like((length, features))
    square = like((length, LANES))
    full, gain, small, cols, rows, decs = call(
        functools.partial(gather_kernel, taps, sizes, parts, length),
        [
            like((SMALL, full_width)),
            like((1, features)),
            like((8, LANES)),
            like((2, length, LANES)),
            like((3, LANES, length)),
            like((2 * STREAMS, DEC_ROWS, LANES), BF16),
        ],
        [own] + pieces,
        [pltpu.VMEM((LANES, LANES), F32), pltpu.VMEM((parts, SMALL, piece_width), F32)],
        name="gather",
    )
    conv_like = like((length, channels), BF16)
    padded, conv, write_t, other = call(
        functools.partial(front_kernel, taps),
        [like(lifted.shape), conv_like, like((N, length)), message],
        [lifted, halo, full, rows, decs],
        name="front",
        aliases={0: 0},
    )
    got = [shift(other, "seq", lambda i: i ^ 1)]
    for stream in range(1, STREAMS):
        conv, other = call(
            functools.partial(front_next_kernel, taps, False, (stream,)),
            [conv_like, message],
            [conv, padded, full, rows, decs, write_t],
            name="front",
            aliases={0: 0},
        )
        got.append(shift(other, "seq", lambda i: i ^ 1))
    held = [conv]

    def own_first(stream, signals):
        held[0], mine = call(
            functools.partial(front_next_kernel, taps, True, (stream,)),
            [conv_like, message],
            [after(held[0], *signals), padded, full, rows, decs, write_t],
            name="own",
            aliases={0: 0},
        )
        return mine

    work = {}

    def intra(signal, value):
        work["local"], work["slope"] = call(
            functools.partial(intra_kernel, taps),
            [wide, like((length, channels))],
            [padded, full, after(held[0], *signal), cols, rows, small],
            flops=2 * length * length * features,
            name="intra",
        )
        return [after(part, work["local"]) for part in value]

    def factors(signal, value):
        *work["factors"], work["picks"], work["shifted"] = call(
            factor_kernel,
            [wide] * 3 + [like((half * LANES, LANES), BF16), like((taps - 1, length, channels))],
            [after(cols, *signal), gate, grad, gain, padded],
            flops=length * features * 16,
            name="factors",
        )
        return [after(part, work["factors"][0]) for part in value]

    sums_like = like((2, length, LANES))

    entry_own, entry_got = entering_states(own_first, got, False, (intra, factors))
    conv = held[0]
    silus, grown, decays = work["factors"]
    given = [work["local"], conv, silus, grown, decays]
    groups = [(True, stream) for stream in range(STREAMS)] + [(False, stream) for stream in range(STREAMS - 1)]
    mixed, gated, sums = call(
        functools.partial(mix_kernel, groups),
        [wide, wide, sums_like],
        given + entry_own + entry_got[:-1],
        name="mix",
    )
    mixed, gated, stats, other = call(
        norm_kernel,
        [wide, wide, square, message],
        [mixed, gated] + given + [sums, decs, entry_got[-1]],
        name="norm",
        aliases={0: 0, 1: 1},
    )
    got = [shift(other, "seq", lambda i: i ^ 1)]
    given = [conv, silus, grown, decays, gated, decs]

    def norm_next(own, stream, signals):
        return call(
            functools.partial(norm_next_kernel, own, (stream,)),
            [message],
            [after(stats, *signals)] + given,
            name="norm_next",
        )[0]

    for stream in range(1, STREAMS):
        got.append(shift(norm_next(False, stream, []), "seq", lambda i: i ^ 1))

    def gates(signal, value):
        work["gates"] = call(
            gate_kernel,
            [
                like((length, features), BF16),
                like((length, features)),
                like((length, LANES)),
                like((1, features)),
                like((8, LANES)),
                like((length, LANES)),
            ],
            [mixed, after(conv, *signal), cols, small, gate, grad, gain, stats] + entry_own + entry_got,
            [entry],
                flops=2 * length * length * features,
            name="gates",
        )
        return [after(part, work["gates"][0]) for part in value]

    def back(signal, value):
        grad_mixed, grad_read = work["gates"][1], work["gates"][5]
        work["back"] = call(
            back_kernel,
            [like((length, features)), like((length, LANES)), like((length, LANES))],
            [after(grad_mixed, *signal), conv, cols, rows, small, grad_read],
            flops=4 * length * length * features,
            name="back",
        )
        return [after(part, work["back"][0]) for part in value]

    shapes = [like((2 * HALO + length, channels)), like((SMALL, full_width)), square, like((8, LANES)), square]
    fixed = [padded, work["shifted"], conv, work["slope"], cols, work["picks"]]
    side = half * LANES
    scratch = [pltpu.VMEM((length, side), BF16)] * 2 + [pltpu.VMEM((N, side), BF16), pltpu.VMEM((8, side), F32)]

    leave_own, leave_got = entering_states(functools.partial(norm_next, True), got, True, (gates, back))
    grad_gate, _, out_sums, grad_gain, grad_small, _ = work["gates"]
    grad_values, in_sums, grad_vecs = work["back"]
    slopes, whole, *sums = call(
        functools.partial(close_own_kernel, taps),
        shapes,
        fixed + [grad_values] + entry_own + leave_own,
        scratch,
        name="close_own",
    )
    slopes, whole, grad_raw, *shares = call(
        functools.partial(close_kernel, taps, sizes),
        shapes[:2] + [square] + [piece_like] * parts,
        [slopes, whole] + fixed + [small, grad_values, grad_vecs, out_sums, in_sums, grad_gain, grad_small]
        + sums + entry_got + leave_got,
        [pltpu.VMEM((parts, SMALL, piece_width), F32)] + scratch,
        name="close",
        aliases={0: 0, 1: 1},
    )
    terms = [shares[0]]
    for distance in range(1, parts):
        terms.append(shift(shares[distance], "fsdp", lambda i: (i + distance) % parts))
    earlier = call(
        functools.partial(before_kernel, taps), [like((BACK_ROWS, piece_width))], [full, slopes], name="before"
    )[0]
    bundle = like((SMALL + BACK_ROWS, piece_width))
    total = call(add_kernel, [bundle], terms + [earlier], name="add")[0]
    partner = shift(total, "seq", lambda i: i ^ 1)
    total, alone = call(add_pair_kernel, [bundle, piece_like], [total, partner], name="add")
    chips = devices // 2
    behind = between_chips(total, {i: (i - 1) % chips for i in range(chips)})
    if chips <= 4:
        terms = [alone] + [
            between_chips(alone, {i: (i + distance) % chips for i in range(chips)})
            for distance in range(1, chips - 1)
        ]
        terms += [behind] if chips > 1 else []
    else:
        terms = [lax.psum(alone, "seq") * 0.5]
    grad_x, ending, grad_dt = call(
        functools.partial(input_kernel, taps),
        [like((length, channels), BF16), like((2 * HALO, channels)), like((heads, length))],
        [full, after(slopes, alone), grad_raw],
        flops=length * channels * 16,
        name="inputs",
    )
    grad_x = call(
        functools.partial(patch_kernel, chips, taps),
        [like((length, channels), BF16)],
        [grad_x, ending, partner, behind],
        [pltpu.VMEM((2 * HALO, channels), BF16), pltpu.SemaphoreType.DMA],
        fetched=(0,),
        aliases={0: 0},
        flops=length * channels * 8,
        name="patch",
    )[0]
    cw, cb, dtb, al, sk, gn = call(
        functools.partial(unpack_kernel, len(terms), taps),
        [
            like((taps, width)),
            like((width,)),
            like((1, heads_here)),
            like((1, heads_here)),
            like((1, heads_here)),
            like((gain_width,)),
        ],
        terms,
        name="unpack",
    )
    return (
        grad_x[None],
        grad_gate[None],
        grad_dt.T[None],
        cw,
        cb,
        dtb.reshape(-1),
        al.reshape(-1),
        sk.reshape(-1),
        gn,
    )


def solution(mesh):
    tokens = P("fsdp", "seq", None)
    in_specs = (tokens,) * 4 + (P(None, "fsdp"),) + (P("fsdp"),) * 5
    out_specs = (tokens,) * 3 + (P(None, "fsdp"),) + (P("fsdp"),) * 5
    return jax.shard_map(shards, mesh=mesh, in_specs=in_specs, out_specs=out_specs, check_vma=False)
```

```python
import functools

import jax
import jax.numpy as jnp
from jax import lax
from jax.experimental import pallas as pl
from jax.experimental.pallas import tpu as pltpu
from jax.sharding import PartitionSpec as P

P_SIZE = 64
N = 64
EPS = 1e-05
LANES = 2 * P_SIZE
HALO = 8
SMALL = 8
STREAMS = 2
FOLDS = 4
BACK_ROWS = 16
DEC_ROWS = 16
F32, BF16 = jnp.float32, jnp.bfloat16


def dot(a, b, over=(1, 0)):
    return lax.dot_general(
        a, b, (((over[0],), (over[1],)), ((), ())), preferred_element_type=F32
    )


def here_at():
    index = lax.axis_index("seq")
    return lax.rem(index, 2), lax.div(index, 2), lax.axis_index("fsdp")


def iota(shape, axis):
    return lax.broadcasted_iota(jnp.int32, shape, axis)


def sigmoid(x):
    return 0.5 * jnp.tanh(0.5 * x) + 0.5


def split(x):
    high = x.astype(BF16)
    return high, (x - high.astype(F32)).astype(BF16)


def dot_parts(ones, value, parts):
    pieces = []
    for _ in range(parts):
        piece = value.astype(BF16)
        pieces.append(piece)
        value = value - piece.astype(F32)
    ones = ones.astype(BF16)
    return dot(jnp.concatenate([ones] * parts, axis=1), jnp.concatenate(pieces, axis=0))


def block(position):
    return slice(position * LANES, (position + 1) * LANES)


def by_head(columns, pair, shape):
    first = jnp.broadcast_to(columns[:, 2 * pair : 2 * pair + 1], shape)
    second = jnp.broadcast_to(columns[:, 2 * pair + 1 : 2 * pair + 2], shape)
    return jnp.where(iota(shape, 1) < P_SIZE, first, second)


def apart(pair_block):
    first = iota(pair_block.shape, 1) < P_SIZE
    zero = jnp.zeros_like(pair_block)
    return jnp.concatenate(
        [jnp.where(first, pair_block, zero), jnp.where(first, zero, pair_block)], axis=0
    )


def head_sums(product, pair, parts=2):
    shape = (LANES, LANES)
    pick = (iota(shape, 1) == 2 * pair + (iota(shape, 0) >= P_SIZE).astype(jnp.int32)).astype(BF16)
    if parts == 1:
        return dot(product.astype(BF16), pick)
    high, low = split(product)
    return dot(jnp.concatenate([high, low], axis=1), jnp.concatenate([pick, pick], axis=0))


def before_silu(rows, full, cols, taps, length):
    start = HALO - (taps - 1)
    total = full[taps : taps + 1, cols] + full[0:1, cols] * rows[start : start + length, cols]
    for tap in range(1, taps):
        total = total + full[tap : tap + 1, cols] * rows[start + tap : start + tap + length, cols]
    return total


def open_kernel(x, dt, cw, cb, dtb, al, sk, gain, halo, out, own, late, raw, *rest):
    held, sems = rest[:-1], rest[-1]
    ending = x.at[pl.ds(x.shape[0] - late.shape[0], late.shape[0])]
    copies = [
        pltpu.make_async_copy(source, target, sems.at[number])
        for number, (source, target) in enumerate(
            zip((cw, cb, dtb, al, sk, gain, dt, ending), held + (raw, late))
        )
    ]
    for copy in copies:
        copy.start()
    out[...] = jnp.zeros_like(out)
    for copy in copies:
        copy.wait()
    halo[...] = late[...].astype(F32)[HALO:].astype(BF16)
    cw, cb, dtb, al, sk, gain = held
    taps, width = cw.shape
    out[0:taps, 0:width] = cw[...]
    out[taps : taps + 1, 0:width] = cb[...]
    out[taps + 1 : taps + 2, 0 : gain.shape[0]] = gain[...].reshape(1, -1)
    for number, ref in enumerate((dtb, al, sk)):
        out[taps + 2 : taps + 3, number * LANES : number * LANES + ref.shape[1]] = ref[...]
    own[0:SMALL, :] = out[...]
    own[SMALL:, :] = jnp.zeros((SMALL, own.shape[1]), F32)
    for group in range(raw.shape[0] // SMALL):
        own[SMALL:, block(group)] = raw[group * SMALL : (group + 1) * SMALL, :]


def peer(position, distance, parts):
    if parts & (parts - 1) == 0:
        return position ^ distance
    return (position + distance) % parts


def peer_back(position, distance, parts):
    if parts & (parts - 1) == 0:
        return position ^ distance
    return lax.rem(position + parts - distance, parts)


def placement(position, width):
    start = position * width
    base = start // LANES * LANES
    return base, start - base


def put_state(states, pair, value):
    states[pair * N : (pair + 1) * N, :] = value


def get_state(states, pair):
    return states[pair * N : (pair + 1) * N, :]


def pack_decays(decays):
    high, low = split(decays)
    group = iota(decays.shape, 1) // (P_SIZE // 2)
    return jnp.where(lax.rem(group, 2) == 0, high.astype(F32), low.astype(F32)).astype(BF16)


def unpack_decays(packed):
    value = packed.astype(F32)
    group = iota(value.shape, 1) // (P_SIZE // 2)
    ahead = pltpu.roll(value, LANES - P_SIZE // 2, 1)
    behind = pltpu.roll(value, P_SIZE // 2, 1)
    return value + jnp.where(lax.rem(group, 2) == 0, ahead, behind)


def gather_kernel(taps, sizes, parts, length, own, *refs):
    given, refs = refs[: parts - 1], refs[parts - 1 :]
    full, gain, small, cols, rows_out, decs, wide, pieces = refs
    mine_at = here_at()[2]
    piece_width = pieces.shape[2]
    pieces[mine_at] = own[0:SMALL, :]
    for distance in range(1, parts):
        pieces[peer_back(mine_at, distance, parts)] = given[distance - 1][...]
    width, gain_width, heads_here = sizes
    heads = heads_here * parts
    half = heads // 4
    full[...] = jnp.zeros_like(full)
    small[...] = jnp.zeros_like(small)
    wide[...] = jnp.zeros_like(wide)
    for group in range(heads // SMALL):
        wide[group * SMALL : (group + 1) * SMALL, :] = own[SMALL:, block(group)]
    for part in range(parts):
        base, shift = placement(part, width)
        piece = jnp.concatenate([pieces[part], jnp.zeros((SMALL, LANES), F32)], axis=1)
        if shift:
            piece = pltpu.roll(piece, shift, 1)
        full[:, base : base + piece_width + LANES] += piece
        gain[:, part * gain_width : (part + 1) * gain_width] = pieces[
            part, taps + 1 : taps + 2, 0:gain_width
        ]
        for number in range(3):
            row = pieces[part, taps + 2 : taps + 3, block(number)]
            if part:
                row = pltpu.roll(row, part * heads_here, 1)
            small[number : number + 1, :] += row
    raw = wide[...].T + small[0:1, :]
    step = jnp.maximum(raw, 0.0) + jnp.log1p(jnp.exp(-jnp.abs(raw)))
    logs = -jnp.exp(small[1:2, :]) * step
    square = (length, length)
    lower = iota(square, 0) >= iota(square, 1)
    running = dot_parts(lower, logs, 3)
    running_t = running.T
    step_t = step.T
    last = jnp.broadcast_to(running_t[:, length - 1 : length], running_t.shape)
    cols[0] = step
    cols[1] = running
    rows_out[0] = step_t
    rows_out[1] = running_t
    rows_out[2] = jnp.exp(last - running_t) * step_t
    wide[...] = jnp.exp(last)[:, 0:LANES]
    group = half // STREAMS
    first = iota((group, LANES), 1) < P_SIZE
    for number in range(2 * STREAMS):
        even = wide[pl.ds(2 * group * number, group, stride=2), :]
        odd = wide[pl.ds(2 * group * number + 1, group, stride=2), :]
        decays = jnp.where(first, even, odd)
        decs[number] = pack_decays(
            jnp.concatenate([decays, jnp.zeros((DEC_ROWS - group, LANES), F32)], axis=0)
        )


def side_block(pair):
    return pl.ds(pl.multiple_of(pair * LANES, LANES), LANES)


def front_group(taps, number, rows, full, tails, decs, write_t, conv, out):
    length = conv.shape[0]
    group = (out.shape[0] - DEC_ROWS) // N
    scale = tails[2, pl.ds(number * 2 * group, 2 * group), :]
    for pair in range(group):
        here = side_block(number * group + pair)
        pre = before_silu(rows, full, here, taps, length)
        value = (pre * sigmoid(pre)).astype(BF16)
        conv[:, here] = value
        scaled = jnp.concatenate(
            [
                (write_t * scale[2 * pair + which : 2 * pair + which + 1, :]).astype(BF16)
                for which in range(2)
            ],
            axis=1,
        )
        put_state(out, pair, dot(scaled, apart(value)).astype(BF16))
    out[group * N :, :] = decs[number]


def front_kernel(taps, lifted, halo, full, tails, decs, rows, conv, write_out, out):
    length, channels = conv.shape
    rows[0:HALO, :] = halo[...].astype(F32)
    here = block(channels // LANES - 1)
    pre = before_silu(rows, full, here, taps, length)
    vectors = (pre * sigmoid(pre)).astype(BF16)
    conv[:, here] = vectors
    write_t = vectors.astype(F32).T[0:N, :]
    write_out[...] = write_t
    front_group(taps, group_at(False, 0), rows, full, tails, decs, write_t, conv, out)


def group_at(own, stream):
    core = here_at()[0]
    return (core if own else 1 - core) * STREAMS + stream


def front_next_kernel(taps, own, streams, conv_in, rows, full, tails, decs, write_t, conv, *outs):
    for stream, out in zip(streams, outs):
        front_group(taps, group_at(own, stream), rows, full, tails, decs, write_t[...], conv, out)


def head_weights(cols, rows_ref, head, causal, scores):
    gap = cols[1, :, head : head + 1] - rows_ref[1, head : head + 1, :]
    scaled = jnp.exp(jnp.where(causal, gap, -1e30)) * rows_ref[0, head : head + 1, :]
    return scaled, (scaled * scores).astype(BF16)


def factor_kernel(cols, gate, grad, gain, rows, silus, grown, decays, picks, shifted):
    length, features = gate.shape
    taps = shifted.shape[0] + 1
    for tap in range(taps - 1):
        start = HALO - taps + 1 + tap
        shifted[tap] = rows[start : start + length, :]
    decay = jnp.exp(cols[1])
    picks[...] = (iota(picks.shape, 1) == iota(picks.shape, 0) // P_SIZE).astype(BF16)
    for pair in range(features // LANES):
        here = block(pair)
        z = gate[:, here].astype(F32)
        silus[:, here] = z * sigmoid(z)
        grown[:, here] = grad[:, here].astype(F32) * gain[:, here]
        decays[:, here] = by_head(decay, pair, (length, LANES))


def intra_kernel(taps, rows, full, conv, cols, rows_ref, small, local, slope):
    length, channels = conv.shape
    features = local.shape[1]
    pairs = features // LANES
    write = conv[:, features : features + N]
    read = conv[:, features + N : features + 2 * N]
    scores = dot(read, write, (1, 1))
    square = (length, length)
    causal = iota(square, 0) >= iota(square, 1)
    for pair in range(pairs):
        weights = jnp.concatenate(
            [head_weights(cols, rows_ref, 2 * pair + which, causal, scores)[1] for which in range(2)],
            axis=1,
        )
        values = conv[:, block(pair)]
        skip = by_head(small[2:3, :], pair, (1, LANES))
        here = block(pair)
        local[:, here] = dot(weights, apart(values)) + skip * values.astype(F32)
    for position in range(channels // LANES):
        here = block(position)
        pre = before_silu(rows, full, here, taps, length)
        gate = sigmoid(pre)
        slope[:, here] = gate * (1.0 + pre * (1.0 - gate))


def mix_groups(groups, local, conv, silus, grown, decays, entries, mixed, gated):
    length, features = local.shape
    shape = (length, LANES)
    read = conv[:, features + N : features + 2 * N]
    square_sum = jnp.zeros(shape, F32)
    cross_sum = jnp.zeros(shape, F32)
    for (own, stream), entry in zip(groups, entries):
        number = group_at(own, stream)
        group = entry.shape[0] // N
        for pair in range(group):
            here = side_block(number * group + pair)
            carried = dot(read, get_state(entry, pair))
            mix = local[:, here] + decays[:, here] * carried
            mixed[:, here] = mix
            product = mix * silus[:, here]
            gated[:, here] = product
            square_sum += product * product
            cross_sum += product * grown[:, here]
    return square_sum, cross_sum


def mix_kernel(groups, local, conv, silus, grown, decays, *refs):
    entries, (mixed, gated, sums) = refs[:-3], refs[-3:]
    square, cross = mix_groups(groups, local, conv, silus, grown, decays, entries, mixed, gated)
    sums[0] = square
    sums[1] = cross


def back_state(number, stats, conv, silus, grown, decays, gated, decs, out):
    length, features = gated.shape
    group = (out.shape[0] - DEC_ROWS) // N
    shape = (length, LANES)
    read = conv[:, features + N : features + 2 * N]
    scale = jnp.broadcast_to(stats[:, 0:1], shape)
    factor = jnp.broadcast_to(stats[:, 1:2], shape)
    for pair in range(group):
        here = side_block(number * group + pair)
        grad_gated = scale * grown[:, here] - factor * gated[:, here]
        weighted = decays[:, here] * (grad_gated * silus[:, here])
        put_state(out, pair, dot(read, weighted.astype(BF16), (0, 0)).astype(BF16))
    out[group * N :, :] = decs[number]


def norm_kernel(mixed_in, gated_in, local, conv, silus, grown, decays, sums, decs, *refs):
    entry, mixed, gated, stats, out = refs
    length, features = local.shape
    groups = [(False, STREAMS - 1)]
    square, cross = mix_groups(groups, local, conv, silus, grown, decays, [entry], mixed, gated)
    square = jnp.sum(square + sums[0], axis=1, keepdims=True)
    cross = jnp.sum(cross + sums[1], axis=1, keepdims=True)
    scale = lax.rsqrt(square * (1.0 / features) + EPS)
    factor = scale * scale * scale * cross * (1.0 / features)
    lane = iota((length, LANES), 1)
    values = jnp.where(lane == 0, scale, jnp.where(lane == 1, factor, 0.0))
    stats[...] = values
    back_state(group_at(False, 0), values, conv, silus, grown, decays, gated, decs, out)


def norm_next_kernel(own, streams, stats, conv, silus, grown, decays, gated, decs, *outs):
    for stream, out in zip(streams, outs):
        back_state(group_at(own, stream), stats[...], conv, silus, grown, decays, gated, decs, out)


def gate_kernel(
    mixed, conv, cols, small, gate, grad, gain, stats, *refs
):
    given, refs = refs[: 2 * STREAMS], refs[2 * STREAMS :]
    grad_gate, grad_mixed, sums, grad_gain, grad_small, grad_read, entry = refs
    length, features = mixed.shape
    pairs = features // LANES
    group = pairs // (2 * STREAMS)
    shape = (length, LANES)
    for number, ref in enumerate(given):
        entry[group_at(number < STREAMS, number % STREAMS)] = ref[...]
    scale = jnp.broadcast_to(stats[:, 0:1], shape)
    factor = jnp.broadcast_to(stats[:, 1:2], shape)
    decay = jnp.exp(cols[1])
    read_grad = jnp.zeros((length, N), F32)
    out_sums = jnp.zeros(shape, F32)
    skip_sums = jnp.zeros(shape, F32)
    for pair in range(pairs):
        here = block(pair)
        z = gate[:, here].astype(F32)
        sig = sigmoid(z)
        silu = z * sig
        mix = mixed[:, here]
        product = mix * silu
        grads = grad[:, here].astype(F32)
        grad_gain[:, here] = jnp.sum(grads * (product * scale), axis=0, keepdims=True)
        grad_gated = scale * (grads * gain[:, here]) - factor * product
        grad_mix = grad_gated * silu
        grad_mixed[:, here] = grad_mix
        grad_gate[:, here] = (grad_gated * mix * (sig * (1.0 + z * (1.0 - sig)))).astype(BF16)
        values = conv[:, here].astype(F32)
        skip = by_head(small[2:3, :], pair, (1, LANES))
        rounded = grad_mix.astype(BF16).astype(F32)
        out_sums += head_sums(rounded * (mix - skip * values), pair)
        skip_sums += head_sums(grad_mix * values, pair)
        weighted = (by_head(decay, pair, shape) * grad_mix).astype(BF16)
        read_grad += dot(weighted, get_state(entry.at[pair // group], pair % group), (1, 1))
    sums[...] = out_sums
    grad_read[...] = jnp.concatenate([jnp.zeros_like(read_grad), read_grad], axis=1)
    grad_small[...] = jnp.zeros_like(grad_small)
    grad_small[2:3, :] = jnp.sum(skip_sums, axis=0, keepdims=True)


def back_kernel(grad_mixed, conv, cols, rows_ref, small, grad_read, grad_values, sums, grad_vecs):
    length, features = grad_mixed.shape
    pairs = features // LANES
    shape = (length, LANES)
    write = conv[:, features : features + N]
    read = conv[:, features + N : features + 2 * N]
    scores = dot(read, write, (1, 1))
    square = (length, length)
    causal = iota(square, 0) >= iota(square, 1)
    score_grad = jnp.zeros(square, F32)
    in_sums = jnp.zeros(shape, F32)
    first = iota(shape, 1) < P_SIZE
    for pair in range(pairs):
        here = block(pair)
        grad_mix = grad_mixed[:, here]
        values = conv[:, here]
        rounded = grad_mix.astype(BF16)
        scaled = [head_weights(cols, rows_ref, 2 * pair + which, causal, scores) for which in range(2)]
        weight_grad = dot(rounded, apart(values), (1, 1))
        score_grad += weight_grad[:, 0:length] * scaled[0][0] + weight_grad[:, length:] * scaled[1][0]
        both = dot(jnp.concatenate([scaled[0][1], scaled[1][1]], axis=1), rounded, (0, 0))
        value_grad = jnp.where(first, both[0:length], both[length:])
        in_sums += head_sums(values.astype(F32) * value_grad, pair)
        skip = by_head(small[2:3, :], pair, (1, LANES))
        grad_values[:, here] = value_grad + skip * grad_mix
    sums[...] = in_sums
    high, low = split(score_grad)
    read_grad = dot(high, write) + dot(low, write)
    write_grad = dot(high, read, (0, 0)) + dot(low, read, (0, 0))
    grad_vecs[...] = grad_read[...] + jnp.concatenate([write_grad, read_grad], axis=1)


def through_taps(taps, full, slopes, cols, start, count):
    total = full[0:1, cols] * slopes[start + taps - 1 : start + taps - 1 + count, cols]
    for tap in range(1, taps):
        ahead = start + taps - 1 - tap
        total = total + full[tap : tap + 1, cols] * slopes[ahead : ahead + count, cols]
    return total


def through_conv(taps, here, grad_out, rows, shifted, slope, slopes, whole):
    length = grad_out.shape[0]
    grad_pre = grad_out.astype(BF16).astype(F32) * slope[:, here]
    slopes[HALO : HALO + length, here] = grad_pre
    for tap in range(taps):
        given = shifted[tap, :, here] if tap < taps - 1 else rows[HALO : HALO + length, here]
        whole[tap : tap + 1, here] = jnp.sum(grad_pre * given, axis=0, keepdims=True)
    whole[taps : taps + 1, here] = jnp.sum(grad_pre, axis=0, keepdims=True)


def close_side(taps, own, rows, shifted, conv, slope, cols, picks, entries, leaves, grad_values, slopes, whole, scratch):
    products, holds, leavings, overlaps = scratch
    length, features = grad_values.shape
    half = features // LANES // 2
    group = half // STREAMS
    shape = (length, LANES)
    side = here_at()[0] if own else 1 - here_at()[0]
    write = conv[:, features : features + N]
    running = cols[1]
    tail = jnp.exp(running[length - 1 : length, :] - running) * cols[0]
    tail = pltpu.roll(tail, lax.rem(LANES - 2 * half * side, LANES), 1)
    for pair in range(half):
        here = side_block(side * half + pair)
        local = block(pair)
        leaving = get_state(leaves[pair // group], pair % group)
        values = conv[:, here].astype(F32)
        tail_wide = by_head(tail, pair, shape)
        state_grad = tail_wide * dot(write, leaving)
        products[:, local] = (values * state_grad).astype(BF16)
        holds[:, local] = (tail_wide * values).astype(BF16)
        leavings[:, local] = leaving
        entering = get_state(entries[pair // group], pair % group).astype(F32)
        overlap = jnp.sum(leaving.astype(F32) * entering, axis=0, keepdims=True)
        overlaps[:, local] = jnp.broadcast_to(overlap, (8, LANES))
        through_conv(taps, here, grad_values[:, here] + state_grad, rows, shifted, slope, slopes, whole)
    back = 2 * half * side
    choose = picks[...]
    state_sums = dot(products[...], choose)
    high, low = split(overlaps[...])
    end_sums = dot(high, choose) + dot(low, choose)
    write_grad = dot(holds[...], leavings[...], (1, 1))
    write_grad = jnp.concatenate([write_grad, jnp.zeros_like(write_grad)], axis=1)
    return pltpu.roll(state_sums, back, 1), pltpu.roll(end_sums, back, 1), write_grad


def close_own_kernel(taps, rows, shifted, conv, slope, cols, picks, grad_values, *refs):
    given, (slopes, whole, state_out, end_out, write_out, *scratch) = refs[: 2 * STREAMS], refs[2 * STREAMS :]
    length, channels = conv.shape
    slopes[0:HALO, :] = jnp.zeros((HALO, channels), F32)
    slopes[HALO + length :, :] = jnp.zeros((HALO, channels), F32)
    whole[...] = jnp.zeros_like(whole)
    state_out[...], end_out[...], write_out[...] = close_side(
        taps, True, rows, shifted, conv, slope, cols, picks, given[:STREAMS], given[STREAMS:], grad_values, slopes, whole, scratch
    )


def close_kernel(
    taps, sizes, slopes_in, whole_in, rows, shifted, conv, slope, cols, picks, small, grad_values, grad_vecs, out_sums, in_sums,
    grad_gain, grad_small, state_in, end_in, write_in, *rest
):
    given, rest, scratch = rest[: 2 * STREAMS], rest[2 * STREAMS : -4], rest[-4:]
    slopes, whole, grad_raw, *outs, cut = rest
    parts = len(outs)
    position_here = here_at()[2]
    length, channels = conv.shape
    width, gain_width, heads_here = sizes
    step = cols[0]
    last = cols[1, length - 1 : length, :]
    state_sums, end_sums, write_grad = close_side(
        taps, False, rows, shifted, conv, slope, cols, picks, given[:STREAMS], given[STREAMS:], grad_values, slopes, whole, scratch
    )
    state_sums = state_sums + state_in[...]
    end_sums = end_sums + end_in[...]
    vecs = grad_vecs[...] + (write_in[...] + write_grad)
    through_conv(taps, block(channels // LANES - 1), vecs, rows, shifted, slope, slopes, whole)

    into = in_sums[...] + state_sums
    change = out_sums[...] - into
    end_grad = jnp.sum(state_sums, axis=0, keepdims=True) + jnp.exp(last) * end_sums[0:1, :]
    square = (length, length)
    upper = iota(square, 0) <= iota(square, 1)
    log_grad = dot_parts(upper, change, 2) + end_grad
    rate = jnp.exp(small[1:2, :])
    raw_grad = (into / step - rate * log_grad) * (1.0 - jnp.exp(-step))
    grad_raw[...] = raw_grad
    vectors = (
        jnp.sum(raw_grad, axis=0, keepdims=True),
        jnp.sum(-rate * step * log_grad, axis=0, keepdims=True),
        grad_small[2:3, :],
    )
    piece_width = cut.shape[2]
    for part in range(parts):
        base, shift = placement(part, width)
        piece = whole[:, base : base + piece_width + LANES]
        if shift:
            piece = pltpu.roll(piece, piece_width + LANES - shift, 1)
        cut[part] = piece[:, 0:piece_width]
        cut[part, taps + 1 : taps + 2, 0:gain_width] = grad_gain[:, part * gain_width : (part + 1) * gain_width]
        for number, vector in enumerate(vectors):
            row = pltpu.roll(vector, LANES - part * heads_here, 1) if part else vector
            cut[part, taps + 2 : taps + 3, block(number)] = row
    for distance in range(parts):
        outs[distance][...] = cut[lax.rem(position_here + distance, parts)]


def input_kernel(taps, full, slopes, grad_raw, grad_x, ending, grad_dt):
    grad_dt[...] = grad_raw[...].T[0 : grad_dt.shape[0], :]
    length, channels = grad_x.shape
    for position in range(channels // LANES):
        here = block(position)
        total = through_taps(taps, full, slopes, here, HALO, length)
        grad_x[:, here] = total.astype(BF16)
        ending[:, here] = total[length - 2 * HALO :]


def before_kernel(taps, full, slopes, back):
    channels = slopes.shape[1]
    folded = back.shape[1] // LANES
    back[...] = jnp.zeros_like(back)
    for position in range(channels // LANES):
        here = block(position)
        ahead = through_taps(taps, full, slopes, here, 0, HALO)
        for tap in range(taps - 1):
            at = tap * FOLDS + position // folded
            back[at : at + 1, block(position % folded)] = ahead[HALO - taps + 1 + tap : HALO - taps + 2 + tap]


def patch_kernel(chips, taps, grad_in, ending, from_core, from_chip, grad_x, late, sem):
    core, chip, _ = here_at()
    rows = late.shape[0]
    channels = ending.shape[1]
    folded = from_core.shape[1] // LANES
    inside = core == 0
    later = jnp.where(inside, from_core[SMALL:, :], from_chip[SMALL:, :])
    later = jnp.where(jnp.logical_or(inside, chip < chips - 1), later, 0.0)
    padding = jnp.zeros((rows - taps + 1, LANES), F32)
    for position in range(channels // LANES):
        here = block(position)
        lines = [
            later[tap * FOLDS + position // folded : tap * FOLDS + position // folded + 1, block(position % folded)]
            for tap in range(taps - 1)
        ]
        late[:, here] = (ending[:, here] + jnp.concatenate([padding] + lines, axis=0)).astype(BF16)
    copy = pltpu.make_async_copy(late, grad_x.at[pl.ds(grad_x.shape[0] - rows, rows)], sem)
    copy.start()
    copy.wait()


def unpack_kernel(terms, taps, *refs):
    given, (cw, cb, dtb, al, sk, gain) = refs[:terms], refs[terms:]
    total = given[0][0:SMALL, :]
    for ref in given[1:]:
        total = total + ref[0:SMALL, :]
    width = cw.shape[1]
    cw[...] = total[0:taps, 0:width]
    cb[...] = total[taps, 0:width]
    gain[...] = total[taps + 1, 0 : gain.shape[0]]
    for number, ref in enumerate((dtb, al, sk)):
        ref[...] = total[taps + 2 : taps + 3, number * LANES : number * LANES + ref.shape[1]]


def add_kernel(*refs):
    *terms, back, out = refs
    total = terms[0][...]
    for ref in terms[1:]:
        total = total + ref[...]
    out[0:SMALL, :] = total
    out[SMALL:, :] = back[...]


def add_pair_kernel(own, other, out, alone):
    total = own[0:SMALL, :] + other[0:SMALL, :]
    out[0:SMALL, :] = total
    out[SMALL:, :] = other[SMALL:, :]
    alone[...] = total


def parts_of(message):
    end = message.shape[0] - DEC_ROWS
    return message[0:end, :].astype(F32), unpack_decays(message[end:, :])


def decayed(state, decay):
    group = state.shape[0] // N
    split_rows = state.reshape(group, N, LANES)
    return (split_rows * decay[0:group].reshape(group, 1, LANES)).reshape(state.shape)


def joined(first, second):
    state, decay = second
    return decayed(first[0], decay) + state, decay * first[1]


def store(out, value):
    state, decay = value
    end = state.shape[0]
    out[0:end, :] = state.astype(BF16)
    out[end:, :] = pack_decays(decay)


def ordered(later, a, b):
    return jnp.where(later, b, a), jnp.where(later, a, b)


def meet_kernel(reverse, mine, got, out, decay):
    later = here_at()[0] == (0 if reverse else 1)
    first, second = ordered(later, mine[...], got[...])
    whole = joined(parts_of(first), parts_of(second))
    store(out, whole)
    decay[...] = whole[1]


def join_kernel(first, second, out):
    store(out, joined(parts_of(first[...]), parts_of(second[...])))


def pass_kernel(before, own, decay, out):
    end = out.shape[0]
    state = decayed(before[0:end, :].astype(F32), decay[...])
    out[...] = (state + own[0:end, :].astype(F32)).astype(BF16)


def enter_kernel(reverse, *refs):
    given, (mine, got, own, send) = refs[:-4], refs[-4:]
    later = here_at()[0] == (0 if reverse else 1)
    end = own.shape[0]
    start = given[0][0:end, :].astype(F32)
    for ref in given[1:]:
        start = start + ref[0:end, :].astype(F32)
    state, decay = parts_of(ordered(later, mine[...], got[...])[0])
    after = decayed(start, decay) + state
    own[...] = jnp.where(later, after, start).astype(BF16)
    send[...] = jnp.where(later, start, after).astype(BF16)


def call(kernel, outs, args, scratch=(), megabytes=8, flops=0, name=None, fetched=(), aliases=None):
    specs = [
        pl.BlockSpec(
            memory_space=pltpu.HBM if number in fetched else pltpu.VMEM
        )
        for number in range(len(args))
    ]
    fetched_out = [out for given, out in (aliases or {}).items() if given in fetched]
    moved = sum(a.size * a.dtype.itemsize for a in args)
    moved += sum(o.size * o.dtype.itemsize for o in outs)
    return pl.pallas_call(
        kernel,
        out_shape=outs,
        in_specs=specs,
        out_specs=[
            pl.BlockSpec(memory_space=pltpu.HBM if number in fetched_out else pltpu.VMEM)
            for number in range(len(outs))
        ],
        input_output_aliases=aliases or {},
        scratch_shapes=list(scratch),
        compiler_params=pltpu.CompilerParams(vmem_limit_bytes=megabytes << 20),
        cost_estimate=pl.CostEstimate(flops=flops, bytes_accessed=moved, transcendentals=0),
        name=name,
    )(*args)


def like(shape, dtype=F32):
    return jax.ShapeDtypeStruct(shape, dtype)


def shift(value, axis, route):
    count = lax.axis_size(axis)
    pairs = [(i, route(i)) for i in range(count)]
    return lax.ppermute(value, axis, [(i, j) for i, j in pairs if 0 <= j < count])


def between_chips(value, routes):
    return shift(value, "seq", lambda i: 2 * routes[i // 2] + i % 2 if i // 2 in routes else -1)


def entering_states(own_states, got, reverse, beside):
    chips = lax.axis_size("seq") // 2
    message = like(got[0].shape, BF16)
    entry = like((got[0].shape[0] - DEC_ROWS, LANES), BF16)
    chip, decays, mine = [], [], []
    for stream, other in enumerate(got):
        mine.append(own_states(stream, chip))
        whole, decay = call(
            functools.partial(meet_kernel, reverse),
            [message, like((DEC_ROWS, LANES))],
            [mine[-1], other],
            name="meet",
        )
        chip.append(whole)
        decays.append(decay)
    if 1 < chips <= 4:
        order = list(range(chips))[::-1] if reverse else list(range(chips))
        arrived = [[] for _ in chip]
        moving = chip
        for hop in range(chips - 1):
            route = {order[hop]: order[hop + 1]}
            landed = [between_chips(part, route) for part in moving]
            if hop < len(beside):
                landed = beside[hop](moving, landed)
            for stream, part in zip(arrived, landed):
                stream.append(part)
            if hop < chips - 2:
                moving = [
                    call(pass_kernel, [entry], list(parts), name="pass")[0] for parts in zip(landed, chip, decays)
                ]
    else:
        sign = -1 if reverse else 1
        before = [shift(part, "seq", lambda i: i + 2 * sign) for part in chip]
        before = beside[1](chip, beside[0](chip, before))
        window = 1
        while window < chips - 1:
            distance = window + 1
            longer = [call(join_kernel, [message], pair, name="join")[0] for pair in zip(before, chip)]
            far = [shift(part, "seq", lambda i: i + 2 * distance * sign) for part in longer]
            before = [call(join_kernel, [message], pair, name="join")[0] for pair in zip(far, before)]
            window = 2 * window + 1
        arrived = [[part] for part in before]
    owns, others = [], []
    for parts, a, b in zip(arrived, mine, got):
        own, send = call(functools.partial(enter_kernel, reverse), [entry, entry], parts + [a, b], name="enter")
        owns.append(own)
        others.append(shift(send, "seq", lambda i: i ^ 1))
    return owns, others


def after(value, *signals):
    return lax.optimization_barrier((value, *signals))[0]


def shards(
    conv_input, gate_input, dt_raw, grad_output, conv_weight, conv_bias, dt_bias, a_log, skip, norm_gain
):
    gate, grad = gate_input[0], grad_output[0]
    dt = dt_raw[0].T
    length, channels = conv_input.shape[1:]
    features = gate.shape[1]
    heads = dt.shape[0]
    half = heads // 4
    taps, width = conv_weight.shape
    gain_width = norm_gain.shape[0]
    heads_here = dt_bias.shape[0]
    parts = lax.axis_size("fsdp")
    devices = lax.axis_size("seq")
    sizes = (width, gain_width, heads_here)
    piece_width = -(-width // LANES) * LANES
    full_width = placement(parts - 1, width)[0] + piece_width + LANES
    piece_like = like((SMALL, piece_width))
    shares = [
        conv_weight,
        conv_bias.reshape(1, -1),
        dt_bias.reshape(1, -1),
        a_log.reshape(1, -1),
        skip.reshape(1, -1),
        norm_gain,
    ]

    x = conv_input[0]
    halo, piece, own = call(
        open_kernel,
        [like((HALO, channels), BF16), piece_like, like((2 * SMALL, piece_width))],
        [x, dt] + shares,
        [pltpu.VMEM((2 * HALO, channels), BF16), pltpu.VMEM(dt.shape, F32)]
        + [pltpu.VMEM(share.shape, F32) for share in shares]
        + [pltpu.SemaphoreType.DMA((len(shares) + 2,))],
        fetched=range(len(shares) + 2),
        megabytes=60,
        name="open",
    )
    pieces = [shift(piece, "fsdp", lambda i: peer(i, distance, parts)) for distance in range(1, parts)]
    halo = shift(halo, "seq", lambda i: i + 1)
    lifted = jnp.pad(after(x, piece).astype(F32), ((HALO, 0), (0, 0)))

    group = half // STREAMS
    message = like((group * N + DEC_ROWS, LANES), BF16)
    entry = pltpu.VMEM((2 * STREAMS, group * N, LANES), BF16)
    wide = like((length, features))
    square = like((length, LANES))
    full, gain, small, cols, rows, decs = call(
        functools.partial(gather_kernel, taps, sizes, parts, length),
        [
            like((SMALL, full_width)),
            like((1, features)),
            like((8, LANES)),
            like((2, length, LANES)),
            like((3, LANES, length)),
            like((2 * STREAMS, DEC_ROWS, LANES), BF16),
        ],
        [own] + pieces,
        [pltpu.VMEM((LANES, LANES), F32), pltpu.VMEM((parts, SMALL, piece_width), F32)],
        name="gather",
    )
    conv_like = like((length, channels), BF16)
    padded, conv, write_t, other = call(
        functools.partial(front_kernel, taps),
        [like(lifted.shape), conv_like, like((N, length)), message],
        [lifted, halo, full, rows, decs],
        name="front",
        aliases={0: 0},
    )
    got = [shift(other, "seq", lambda i: i ^ 1)]
    for stream in range(1, STREAMS):
        conv, other = call(
            functools.partial(front_next_kernel, taps, False, (stream,)),
            [conv_like, message],
            [conv, padded, full, rows, decs, write_t],
            name="front",
            aliases={0: 0},
        )
        got.append(shift(other, "seq", lambda i: i ^ 1))
    held = [conv]

    def own_first(stream, signals):
        held[0], mine = call(
            functools.partial(front_next_kernel, taps, True, (stream,)),
            [conv_like, message],
            [after(held[0], *signals), padded, full, rows, decs, write_t],
            name="own",
            aliases={0: 0},
        )
        return mine

    work = {}

    def intra(signal, value):
        work["local"], work["slope"] = call(
            functools.partial(intra_kernel, taps),
            [wide, like((length, channels))],
            [padded, full, after(held[0], *signal), cols, rows, small],
            flops=2 * length * length * features,
            name="intra",
        )
        return [after(part, work["local"]) for part in value]

    def factors(signal, value):
        *work["factors"], work["picks"], work["shifted"] = call(
            factor_kernel,
            [wide] * 3 + [like((half * LANES, LANES), BF16), like((taps - 1, length, channels))],
            [after(cols, *signal), gate, grad, gain, padded],
            flops=length * features * 16,
            name="factors",
        )
        return [after(part, work["factors"][0]) for part in value]

    sums_like = like((2, length, LANES))

    entry_own, entry_got = entering_states(own_first, got, False, (intra, factors))
    conv = held[0]
    silus, grown, decays = work["factors"]
    given = [work["local"], conv, silus, grown, decays]
    groups = [(True, stream) for stream in range(STREAMS)] + [(False, stream) for stream in range(STREAMS - 1)]
    mixed, gated, sums = call(
        functools.partial(mix_kernel, groups),
        [wide, wide, sums_like],
        given + entry_own + entry_got[:-1],
        name="mix",
    )
    mixed, gated, stats, other = call(
        norm_kernel,
        [wide, wide, square, message],
        [mixed, gated] + given + [sums, decs, entry_got[-1]],
        name="norm",
        aliases={0: 0, 1: 1},
    )
    got = [shift(other, "seq", lambda i: i ^ 1)]
    given = [conv, silus, grown, decays, gated, decs]

    def norm_next(own, streams):
        return call(
            functools.partial(norm_next_kernel, own, streams),
            [message] * len(streams),
            [stats] + given,
            name="norm_next",
        )

    for stream in range(1, STREAMS):
        got.append(shift(norm_next(False, (stream,))[0], "seq", lambda i: i ^ 1))
    mine = norm_next(True, tuple(range(STREAMS)))

    def gates(signal, value):
        work["gates"] = call(
            gate_kernel,
            [
                like((length, features), BF16),
                like((length, features)),
                like((length, LANES)),
                like((1, features)),
                like((8, LANES)),
                like((length, LANES)),
            ],
            [mixed, after(conv, *signal), cols, small, gate, grad, gain, stats] + entry_own + entry_got,
            [entry],
                flops=2 * length * length * features,
            name="gates",
        )
        return [after(part, work["gates"][0]) for part in value]

    def back(signal, value):
        grad_mixed, grad_read = work["gates"][1], work["gates"][5]
        work["back"] = call(
            back_kernel,
            [like((length, features)), like((length, LANES)), like((length, LANES))],
            [after(grad_mixed, *signal), conv, cols, rows, small, grad_read],
            flops=4 * length * length * features,
            name="back",
        )
        return [after(part, work["back"][0]) for part in value]

    shapes = [like((2 * HALO + length, channels)), like((SMALL, full_width)), square, like((8, LANES)), square]
    fixed = [padded, work["shifted"], conv, work["slope"], cols, work["picks"]]
    side = half * LANES
    scratch = [pltpu.VMEM((length, side), BF16)] * 2 + [pltpu.VMEM((N, side), BF16), pltpu.VMEM((8, side), F32)]

    leave_own, leave_got = entering_states(lambda stream, signals: mine[stream], got, True, (gates, back))
    grad_gate, _, out_sums, grad_gain, grad_small, _ = work["gates"]
    grad_values, in_sums, grad_vecs = work["back"]
    slopes, whole, *sums = call(
        functools.partial(close_own_kernel, taps),
        shapes,
        fixed + [grad_values] + entry_own + leave_own,
        scratch,
        name="close_own",
    )
    slopes, whole, grad_raw, *shares = call(
        functools.partial(close_kernel, taps, sizes),
        shapes[:2] + [square] + [piece_like] * parts,
        [slopes, whole] + fixed + [small, grad_values, grad_vecs, out_sums, in_sums, grad_gain, grad_small]
        + sums + entry_got + leave_got,
        [pltpu.VMEM((parts, SMALL, piece_width), F32)] + scratch,
        name="close",
        aliases={0: 0, 1: 1},
    )
    terms = [shares[0]]
    for distance in range(1, parts):
        terms.append(shift(shares[distance], "fsdp", lambda i: (i + distance) % parts))
    earlier = call(
        functools.partial(before_kernel, taps), [like((BACK_ROWS, piece_width))], [full, slopes], name="before"
    )[0]
    bundle = like((SMALL + BACK_ROWS, piece_width))
    total = call(add_kernel, [bundle], terms + [earlier], name="add")[0]
    partner = shift(total, "seq", lambda i: i ^ 1)
    total, alone = call(add_pair_kernel, [bundle, piece_like], [total, partner], name="add")
    chips = devices // 2
    behind = between_chips(total, {i: (i - 1) % chips for i in range(chips)})
    if chips <= 4:
        terms = [alone] + [
            between_chips(alone, {i: (i + distance) % chips for i in range(chips)})
            for distance in range(1, chips - 1)
        ]
        terms += [behind] if chips > 1 else []
    else:
        terms = [lax.psum(alone, "seq") * 0.5]
    grad_x, ending, grad_dt = call(
        functools.partial(input_kernel, taps),
        [like((length, channels), BF16), like((2 * HALO, channels)), like((heads, length))],
        [full, after(slopes, alone), grad_raw],
        flops=length * channels * 16,
        name="inputs",
    )
    grad_x = call(
        functools.partial(patch_kernel, chips, taps),
        [like((length, channels), BF16)],
        [grad_x, ending, partner, behind],
        [pltpu.VMEM((2 * HALO, channels), BF16), pltpu.SemaphoreType.DMA],
        fetched=(0,),
        aliases={0: 0},
        flops=length * channels * 8,
        name="patch",
    )[0]
    cw, cb, dtb, al, sk, gn = call(
        functools.partial(unpack_kernel, len(terms), taps),
        [
            like((taps, width)),
            like((width,)),
            like((1, heads_here)),
            like((1, heads_here)),
            like((1, heads_here)),
            like((gain_width,)),
        ],
        terms,
        name="unpack",
    )
    return (
        grad_x[None],
        grad_gate[None],
        grad_dt.T[None],
        cw,
        cb,
        dtb.reshape(-1),
        al.reshape(-1),
        sk.reshape(-1),
        gn,
    )


def solution(mesh):
    tokens = P("fsdp", "seq", None)
    in_specs = (tokens,) * 4 + (P(None, "fsdp"),) + (P("fsdp"),) * 5
    out_specs = (tokens,) * 3 + (P(None, "fsdp"),) + (P("fsdp"),) * 5
    return jax.shard_map(shards, mesh=mesh, in_specs=in_specs, out_specs=out_specs, check_vma=False)
```
